32 devices in a mesh: ea: 4 (over z), gx: 2 (over core), gy: 4 (over y, x).
Axes of the slice: x: 2, y: 2, z: 4, core: 2. Of those that a mesh axis runs over, the one named last changes fastest.
Arguments:
- tokens: bfloat16 [12608, 768], P(('ea', 'gx', 'gy')), may hold values from -6 to 6
- routes: int32 [12608, 2], P(('ea', 'gx', 'gy')), may hold values from 0 to 3, all different within a row; in each aligned block of 394 rows (0 to 393, 394 to 787, ...) at most 263 rows name the same one
- cotangent: bfloat16 [12608, 768], P(('ea', 'gx', 'gy')), may hold values from -6 to 6
- norm1_gain: float32 [768], replicated, may hold values from 0.5 to 1.5
- norm1_shift: float32 [768], replicated, may hold values from -3 to 3
- w_qkv: bfloat16 [768, 3, 768], replicated, may hold values from -0.21875 to 0.21875
- qv_bias: float32 [2, 768], replicated, may hold values from -3 to 3
- w_proj: bfloat16 [768, 768], replicated, may hold values from -0.875 to 0.875
- proj_bias: float32 [768], replicated, may hold values from -3 to 3
- norm2_gain: float32 [768], replicated, may hold values from 0.5 to 1.5
- norm2_shift: float32 [768], replicated, may hold values from -3 to 3
- router_w: bfloat16 [768, 4], replicated, may hold values from -0.4375 to 0.4375
- expert_in: bfloat16 [4, 768, 3072], P('ea', 'gx', 'gy'), may hold values from -0.21875 to 0.21875
- expert_in_bias: float32 [4, 3072], P('ea'), may hold values from -3 to 3
- expert_out: bfloat16 [4, 3072, 768], P('ea', 'gy', 'gx'), may hold values from -0.21875 to 0.21875
- expert_out_bias: float32 [4, 768], P('ea'), may hold values from -3 to 3
Outputs:
- output: bfloat16 [12608, 768], P(('ea', 'gx', 'gy'))
- grad_tokens: float32 [12608, 768], P(('ea', 'gx', 'gy'))
- grad_norm1_gain: float32 [768], replicated
- grad_norm1_shift: float32 [768], replicated
- grad_w_qkv: float32 [768, 3, 768], replicated
- grad_qv_bias: float32 [2, 768], replicated
- grad_w_proj: float32 [768, 768], replicated
- grad_proj_bias: float32 [768], replicated
- grad_norm2_gain: float32 [768], replicated
- grad_norm2_shift: float32 [768], replicated
- grad_router_w: float32 [768, 4], replicated
- grad_expert_in: float32 [4, 768, 3072], P('ea', 'gx', 'gy')
- grad_expert_in_bias: float32 [4, 3072], P('ea')
- grad_expert_out: float32 [4, 3072, 768], P('ea', 'gy', 'gx')
- grad_expert_out_bias: float32 [4, 768], P('ea')
The draws below stay inside these ranges and needn't reach their ends.
Inputs may be any that keep to these rules, and one draw needn't show every extreme that they name: `routes`: each row names two different experts. In the rows of one device (aligned blocks of 394 rows) no expert is named more than 263 times, and in some blocks one is named exactly 263 times.
All inputs are finite; a program needn't handle non-finite values.
Results may differ from the reference program's by a relative error of at most 0.03.
Values may be sent and summed in bfloat16 or wider, within the bound.
No kernel may reach another device: no remote copies, remote signals or barrier semaphores. Data moves between devices by JAX's collectives and lax.ppermute only.
A program may use at most 192 MiB of HBM per device.

```python
import math
import jax
import jax.numpy as jnp
import numpy as np
from jax import lax

D = 768
HEADS = 12
HD = 64
H = 3072
SEQ = 197
IMG_DEV = 2
EXPERTS = 4
T_DEV = 394
TOKENS = 12608
CAP = 263
N_EA = 4
N_GX = 2
N_GY = 4


def steps_of(rng, shape, cuts, low, high):
    level = 1.0
    for dim, shards_of in cuts:
        steps = jax.random.uniform(jax.random.fold_in(jax.random.fold_in(rng, 6), dim), (shards_of,), jnp.float32, low / len(cuts), high / len(cuts))
        level = level * jnp.repeat(jnp.exp(steps), shape[dim] // shards_of).reshape((-1,) + (1,) * (len(shape) - 1 - dim))
    return level


def deal_out(key, own, number, rows, number_of, top, limit, slope):
    sequence = jax.random.permutation(key, number_of)
    crowded, common = portions_of(number_of, rows * top, limit, slope, True), portions_of(number_of, rows * top, limit, slope, False)
    places = jnp.arange(number_of)

    def named(sizes, turn):
        used = int((sizes > 0).sum())
        fixed = max(1, used // 4)
        moved = fixed + (places - fixed + turn * (used - fixed)) % max(1, number_of - fixed)
        return jnp.zeros((number_of,), jnp.int32).at[sequence[jnp.where(places < fixed, places, moved)]].set(jnp.asarray(sizes, jnp.int32))

    sizes = jnp.where(number % 4 == 0, named(crowded, number // 4), named(common, number - number // 4 - 1))
    mixed = jax.random.permutation(jax.random.fold_in(own, 3), number_of)
    giver, sink = mixed[0:number_of // 2 * 2:2], mixed[1:number_of // 2 * 2:2]
    margin = jnp.minimum(sizes[giver] - 1, limit - sizes[sink]) // 2
    margin = jnp.where((giver == sequence[0]) | (sink == sequence[0]) | (sizes[sink] == 0), 0, jnp.maximum(margin, 0))
    moved = jax.random.randint(jax.random.fold_in(own, 4), (number_of // 2,), 0, 1 << 20) % (margin + 1)
    sizes = sizes.at[giver].add(-moved).at[sink].add(moved)
    items = jnp.searchsorted(jnp.cumsum(sizes), jnp.arange(rows * top), side="right").astype(jnp.int32)
    listing = items.reshape(top, rows).T
    listing = listing[jax.random.permutation(jax.random.fold_in(own, 1), rows)]
    turn = jax.random.randint(jax.random.fold_in(own, 2), (rows, 1), 0, top)
    return jnp.take_along_axis(listing, (jnp.arange(top)[None, :] + turn) % top, axis=1)


def portions_of(amount, total, reach, skew, full):
    weights = [(1 << 20) // math.isqrt(standing ** skew) + 1 for standing in range(1, amount + 1)]
    largest = reach if full else min(reach, max(-(-total // amount), total * weights[0] // sum(weights)))
    least = 1 if total - largest >= amount - 1 else 0
    given, rest = [largest] + [least] * (amount - 1), total - largest - least * (amount - 1)
    while rest > 0:
        movable = [i for i in range(1, amount) if given[i] < largest] or [i for i in range(1, amount) if given[i] < reach]
        pool, budget = sum([weights[i] for i in movable]), rest
        for i in movable:
            addition = min(reach - given[i], max(1, budget * weights[i] // pool), rest)
            given[i] = given[i] + addition
            rest = rest - addition
    return np.array(given)


def scatter_about(key, shape, width, limit, cuts=(), kind=jnp.bfloat16):
    loudness = steps_of(key, shape, cuts, -0.22, 0.18) if cuts else 1.0
    drawn = jax.random.normal(key, shape, jnp.float32) * width * loudness
    return jnp.minimum(jnp.maximum(drawn, -limit), limit).astype(kind)


def setup_inputs(seed: int = 0) -> dict:
    key_list = jax.random.split(jax.random.key(seed), 17)
    tokens = scatter_about(key_list[0], (TOKENS, D), 1.0, 6.0, ((0, 32),))
    routes_keys = jax.random.split(jax.random.fold_in(key_list[1], 1), TOKENS // T_DEV)
    routes_turns = jax.random.permutation(jax.random.fold_in(key_list[1], 3), TOKENS // T_DEV)
    routes = jax.vmap(lambda own, number: deal_out(jax.random.fold_in(key_list[1], 2), own, number, T_DEV, EXPERTS, 2, CAP, 1))(routes_keys, routes_turns).reshape((TOKENS, 2))
    cotangent = scatter_about(key_list[2], (TOKENS, D), 1.0, 6.0, ((0, 32),))
    norm1_gain = jnp.clip(1.0 + 0.1 * jax.random.normal(key_list[3], (D,), jnp.float32), 0.5, 1.5)
    norm1_shift = scatter_about(key_list[4], (D,), 0.5, 3.0, (), jnp.float32)
    w_qkv = scatter_about(key_list[5], (D, 3, D), D ** -0.5, 0.21875)
    qv_bias = scatter_about(key_list[6], (2, D), 0.5, 3.0, (), jnp.float32)
    w_proj = scatter_about(key_list[7], (D, D), (D // 16) ** -0.5, 0.875)
    proj_bias = scatter_about(key_list[8], (D,), 0.5, 3.0, (), jnp.float32)
    norm2_gain = jnp.clip(1.0 + 0.1 * jax.random.normal(key_list[9], (D,), jnp.float32), 0.5, 1.5)
    norm2_shift = scatter_about(key_list[10], (D,), 0.5, 3.0, (), jnp.float32)
    router_w = scatter_about(key_list[11], (D, EXPERTS), (D // 4) ** -0.5, 0.4375)
    expert_in = scatter_about(key_list[12], (EXPERTS, D, H), D ** -0.5, 0.21875, ((0, 4), (1, 2), (2, 4)))
    expert_in_bias = scatter_about(key_list[13], (EXPERTS, H), 0.5, 3.0, ((0, 4),), jnp.float32)
    expert_out = scatter_about(key_list[14], (EXPERTS, H, D), (max(1, H * 4 // (EXPERTS * EXPERTS))) ** -0.5, 0.21875, ((0, 4), (1, 4), (2, 2)))
    expert_out_bias = scatter_about(key_list[15], (EXPERTS, D), 0.5, 3.0, ((0, 4),), jnp.float32)
    return {"tokens": tokens, "routes": routes, "cotangent": cotangent, "norm1_gain": norm1_gain, "norm1_shift": norm1_shift, "w_qkv": w_qkv, "qv_bias": qv_bias, "w_proj": w_proj, "proj_bias": proj_bias, "norm2_gain": norm2_gain, "norm2_shift": norm2_shift, "router_w": router_w, "expert_in": expert_in, "expert_in_bias": expert_in_bias, "expert_out": expert_out, "expert_out_bias": expert_out_bias}


@jax.custom_vjp
def low(v):
    return lax.optimization_barrier(v.astype(jnp.bfloat16)).astype(jnp.float32)

@jax.custom_vjp
def low_back(v):
    return v

def low_keep(v):
    return (low(v), None)

def low_pass(kept, grad):
    return (grad,)

def back_keep(v):
    return (v, None)

def back_low(kept, grad):
    return (low(grad),)
low.defvjp(low_keep, low_pass)
low_back.defvjp(back_keep, back_low)
norm_eps = 1e-06
highest_mode = lax.Precision.HIGHEST

def both_round(value):
    return low(low_back(value))

def layer_norm(values, norm_gain, norm_shift):
    centered = values - lax.optimization_barrier(jnp.mean(values, axis=-1, keepdims=True))
    variance = lax.optimization_barrier(jnp.mean(centered * centered, axis=-1, keepdims=True))
    return centered * lax.rsqrt(variance + norm_eps) * norm_gain + norm_shift

def softmax_last(logit_rows):
    row_max = lax.optimization_barrier(jnp.max(logit_rows, axis=-1, keepdims=True))
    powered = jnp.exp(logit_rows - row_max)
    return powered / lax.optimization_barrier(jnp.sum(powered, axis=-1, keepdims=True))

def attend_block(block_rows, qkv_weight, qv_shift, proj_weight):
    row_count = block_rows.shape[0]
    model_width = block_rows.shape[1]
    images = row_count // SEQ
    projected = jnp.dot(block_rows, qkv_weight.reshape(model_width, 3 * model_width), precision=highest_mode).reshape(row_count, 3, model_width)
    queries = both_round(projected[:, 0] + qv_shift[0]).reshape(images, SEQ, HEADS, HD)
    key_rows = both_round(projected[:, 1]).reshape(images, SEQ, HEADS, HD)
    value_rows = both_round(projected[:, 2] + qv_shift[1]).reshape(images, SEQ, HEADS, HD)
    scores = low_back(jnp.einsum('bqhd,bkhd->bhqk', queries, key_rows, precision=highest_mode) * HD ** (-0.5))
    attn_probs = softmax_last(scores)
    context = jnp.einsum('bhqk,bkhd->bqhd', low(attn_probs), value_rows, precision=highest_mode)
    context = both_round(context.reshape(row_count, model_width))
    return low_back(jnp.dot(context, proj_weight, precision=highest_mode))

def expert_apply(rows_block, in_weight, in_shift, out_weight, out_shift):
    pre_act = low_back(jnp.dot(rows_block, in_weight, precision=highest_mode) + in_shift)
    hidden_low = low(jax.nn.gelu(pre_act, approximate=True))
    return both_round(jnp.dot(hidden_low, out_weight, precision=highest_mode) + out_shift)

def reference(tokens, routes, cotangent, norm1_gain, norm1_shift, w_qkv, qv_bias, w_proj, proj_bias, norm2_gain, norm2_shift, router_w, expert_in, expert_in_bias, expert_out, expert_out_bias):
    device_count = N_EA * N_GX * N_GY
    token_total = tokens.shape[0]
    model_width = tokens.shape[1]
    route_blocks = routes.reshape(device_count, 2 * T_DEV)
    expert_iota = jnp.arange(EXPERTS, dtype=jnp.int32)
    one_hot = (route_blocks[:, :, None] == expert_iota[None, None, :]).astype(jnp.int32)
    earlier = jnp.cumsum(one_hot, axis=1) - one_hot
    slot_ids = lax.optimization_barrier(jnp.sum(earlier * one_hot, axis=2))
    device_ids = jnp.arange(device_count, dtype=jnp.int32)[:, None]
    targets = ((route_blocks * device_count + device_ids) * CAP + slot_ids).reshape(-1).astype(jnp.int32)
    block_rows = IMG_DEV * N_GY * SEQ
    block_count = token_total // block_rows

    def forward(inputs, gain_one, shift_one, qkv_weight, qv_shift, proj_weight, proj_shift, gain_two, shift_two, router_weight, in_weight, in_shift, out_weight, out_shift):
        attn_in = low(layer_norm(inputs, gain_one, shift_one))

        def attend(block):
            return attend_block(block, qkv_weight, qv_shift, proj_weight)
        mixed = lax.map(jax.checkpoint(attend), attn_in.reshape(block_count, block_rows, model_width))
        residual = inputs + mixed.reshape(token_total, model_width) + proj_shift
        moe_in = low(layer_norm(residual, gain_two, shift_two))
        logits = low_back(jnp.dot(moe_in, router_weight, precision=highest_mode))
        router_probs = softmax_last(logits)
        gates = jnp.take_along_axis(router_probs, routes, axis=1)
        slot_rows = jnp.zeros((EXPERTS * device_count * CAP, model_width), jnp.float32)
        slot_rows = slot_rows.at[targets].set(jnp.repeat(moe_in, 2, axis=0))
        slot_rows = low_back(slot_rows).reshape(EXPERTS, device_count * CAP, model_width)

        def expert_step(pieces):
            return expert_apply(pieces[0], pieces[1], pieces[2], pieces[3], pieces[4])
        results = lax.map(jax.checkpoint(expert_step), (slot_rows, in_weight, in_shift, out_weight, out_shift))
        picked = results.reshape(EXPERTS * device_count * CAP, model_width)[targets].reshape(token_total, 2, model_width)
        return residual + lax.optimization_barrier(jnp.sum(gates[:, :, None] * picked, axis=1))
    output, pull_back = jax.vjp(forward, tokens.astype(jnp.float32), norm1_gain, norm1_shift, w_qkv.astype(jnp.float32), qv_bias, w_proj.astype(jnp.float32), proj_bias, norm2_gain, norm2_shift, router_w.astype(jnp.float32), expert_in.astype(jnp.float32), expert_in_bias, expert_out.astype(jnp.float32), expert_out_bias)
    grads = pull_back(cotangent.astype(jnp.float32))
    return (output.astype(jnp.bfloat16), grads[0], grads[1], grads[2], grads[3], grads[4], grads[5], grads[6], grads[7], grads[8], grads[9], grads[10], grads[11], grads[12], grads[13])
```

```python
import functools
import math

import jax
import jax.numpy as jnp
from jax import lax
from jax.experimental import pallas as pl
from jax.experimental.pallas import tpu as pltpu
from jax.sharding import PartitionSpec as P

HEADS = 12
HD = 64
SEQ = 197
SEQ_PAD = 208
PAIR = 2 * HD
norm_eps = 1e-06

f32 = jnp.float32
bf16 = jnp.bfloat16
LAST = (((1,), (1,)), ((), ()))
FIRST = (((0,), (0,)), ((), ()))
K0 = math.sqrt(2.0 / math.pi)
C3 = 0.044715


def dot(a, b, dims=None):
    if dims is None:
        return jnp.dot(a, b, preferred_element_type=f32)
    return lax.dot_general(a, b, dims, preferred_element_type=f32)


def spec():
    return pl.BlockSpec(memory_space=pltpu.VMEM)


def call(name, kernel, out_shape, args, flops=0, bytes_accessed=0, scratch=(), smem=0):
    return pl.pallas_call(
        kernel,
        name=name,
        out_shape=out_shape,
        in_specs=[pl.BlockSpec(memory_space=pltpu.SMEM)] * smem
        + [spec()] * (len(args) - smem),
        out_specs=jax.tree.map(lambda _: spec(), out_shape),
        scratch_shapes=list(scratch),
        compiler_params=pltpu.CompilerParams(vmem_limit_bytes=60 * 1024 * 1024),
        cost_estimate=pl.CostEstimate(
            flops=flops, bytes_accessed=bytes_accessed, transcendentals=0
        ),
    )(*args)


def shape(dims, dtype):
    return jax.ShapeDtypeStruct(tuple(dims), dtype)


def norm_rows(values):
    centered = values - jnp.mean(values, axis=1, keepdims=True)
    inverse = lax.rsqrt(jnp.mean(centered * centered, axis=1, keepdims=True) + norm_eps)
    return centered * inverse, inverse


def norm_back(grad, normed, inverse, gain):
    scaled = grad * gain
    return inverse * (
        scaled
        - jnp.mean(scaled, axis=1, keepdims=True)
        - normed * jnp.mean(scaled * normed, axis=1, keepdims=True)
    )


def spread_images(dst, src, images):
    width = src.shape[1]
    for i in range(images):
        dst[i * SEQ_PAD : i * SEQ_PAD + SEQ, :] = src[i * SEQ : (i + 1) * SEQ, :]
        dst[i * SEQ_PAD + SEQ : (i + 1) * SEQ_PAD, :] = jnp.zeros((SEQ_PAD - SEQ, width), dst.dtype)


def pick_rows(slot_rows, d, cap):
    slots = lax.broadcasted_iota(jnp.int32, (cap, slot_rows.shape[1]), 0).astype(f32)
    return jnp.where(slots == slot_rows[d : d + 1, :], 1.0, 0.0).astype(bf16)


def pick_cols(slot_cols, d, cap):
    slots = lax.broadcasted_iota(jnp.int32, (slot_cols.shape[0], cap), 1).astype(f32)
    return jnp.where(slots == slot_cols[:, d : d + 1], 1.0, 0.0).astype(bf16)


def prep_kernel(n_exp, cap, rel_r, rel_c, g_ref, slot_r, slot_c, g_pad, *rest):
    sent, wide = rest[:n_exp], rest[n_exp]
    tp = rel_r.shape[1]
    lanes = slot_r.shape[0]
    ids = lax.broadcasted_iota(jnp.int32, (lanes, tp), 0)
    sel_r = (rel_r[0:1, :] == ids) | (rel_r[1:2, :] == ids)
    ti = lax.broadcasted_iota(jnp.int32, (tp, tp), 0)
    tj = lax.broadcasted_iota(jnp.int32, (tp, tp), 1)
    before = jnp.where(ti < tj, 1.0, 0.0).astype(bf16)
    count_r = dot(jnp.where(sel_r, 1.0, 0.0).astype(bf16), before)
    slot_r[...] = jnp.where(sel_r, count_r, -1.0)
    ids = lax.broadcasted_iota(jnp.int32, (tp, 128), 1)
    sel_c = (rel_c[:, 0:1] == ids) | (rel_c[:, 1:2] == ids)
    after = jnp.where(tj < ti, 1.0, 0.0).astype(bf16)
    count_c = dot(after, jnp.where(sel_c, 1.0, 0.0).astype(bf16))
    slot_c[...] = jnp.where(sel_c, count_c, -1.0)
    spread_images(wide, g_ref[...].astype(f32), tp // SEQ_PAD)
    g_pad[...] = wide[...].astype(bf16)
    rows = slot_r[...]
    for d in range(n_exp):
        sent[d][...] = dot(pick_rows(rows, d, cap), g_pad[...]).astype(bf16)


def head_masks(rows):
    lane = lax.broadcasted_iota(jnp.int32, (rows, PAIR), 1)
    return lane < HD


def attn_probs(q_head, k_pair):
    scores = dot(q_head, k_pair, LAST)
    keys = lax.broadcasted_iota(jnp.int32, scores.shape, 1)
    scores = jnp.where(keys < SEQ, scores, -1e30)
    powered = jnp.exp(scores - jnp.max(scores, axis=1, keepdims=True))
    return powered * (1.0 / jnp.sum(powered, axis=1, keepdims=True))


def fwd_kernel(
    n_exp, cap, x_ref, gain1, shift1, w3, qvb, wp, pb, gain2, shift2, slot_r,
    res, qkv, ctx, attn_in, moe_in, *rest,
):
    sent, wide = rest[:n_exp], rest[n_exp]
    tp = res.shape[0]
    width = res.shape[1]
    images = tp // SEQ_PAD
    spread_images(wide, x_ref[...].astype(f32), images)
    normed, _ = norm_rows(wide[...])
    attn_in[...] = (normed * gain1[...] + shift1[...]).astype(bf16)
    a = attn_in[...]
    qkv[0] = ((dot(a, w3[0]) + qvb[0:1, :]).astype(bf16).astype(f32) * (HD**-0.5)).astype(bf16)
    qkv[1] = dot(a, w3[1]).astype(bf16)
    qkv[2] = (dot(a, w3[2]) + qvb[1:2, :]).astype(bf16)
    low = head_masks(SEQ_PAD)
    pairs = width // PAIR

    def pair_step(step, carry):
        img, pair = step // pairs, lax.rem(step, pairs)
        rows = pl.ds(pl.multiple_of(img * SEQ_PAD, 16), SEQ_PAD)
        cols = pl.ds(pl.multiple_of(pair * PAIR, PAIR), PAIR)
        q, k, v = qkv[0, rows, cols], qkv[1, rows, cols], qkv[2, rows, cols]
        zero = jnp.zeros_like(q)
        p0 = attn_probs(jnp.where(low, q, zero), k).astype(bf16)
        p1 = attn_probs(jnp.where(low, zero, q), k).astype(bf16)
        ctx[rows, cols] = jnp.where(low, dot(p0, v), dot(p1, v)).astype(bf16)
        return carry

    lax.fori_loop(0, images * pairs, pair_step, 0, unroll=2)
    res[...] = wide[...] + dot(ctx[...], wp[...]) + pb[...]
    normed, _ = norm_rows(res[...])
    moe_in[...] = (normed * gain2[...] + shift2[...]).astype(bf16)
    rows = slot_r[...]
    for d in range(n_exp):
        sent[d][...] = dot(pick_rows(rows, d, cap), moe_in[...]).astype(bf16)


def moe_kernel(
    nb, cap, n_exp, hc, sc, *refs,
):
    rows_in, g_in = refs[:nb], refs[nb : 2 * nb]
    mine_in, other_in, mine_out, other_out = (refs[2 * nb + 4 * i : 2 * nb + 4 * i + 4] for i in range(4))
    r = 2 * nb + 16
    in_bias, out_bias, router = refs[r : r + 3]
    r += 3
    y_out, gm_out = refs[r : r + nb], refs[r + nb : r + 2 * nb]
    r += 2 * nb
    hid, gp_out, gr, in_b, out_b, router_g = refs[r : r + 6]
    r += 6
    x, gf, wi, wo, acc_y, acc_g, probs_s, sems = refs[r:]
    c = pl.program_id(0)
    width = x.shape[1]
    half = width // 2
    part = wi.shape[2]

    def copies(i):
        gx = sc[1]
        near = pl.ds(pl.multiple_of(gx * half, half), half)
        far = pl.ds(pl.multiple_of((1 - gx) * half, half), half)
        return (
            pltpu.make_async_copy(mine_in[i], wi.at[i, near, :], sems.at[4 * i]),
            pltpu.make_async_copy(other_in[i], wi.at[i, far, :], sems.at[4 * i + 1]),
            pltpu.make_async_copy(mine_out[i], wo.at[i, :, near], sems.at[4 * i + 2]),
            pltpu.make_async_copy(other_out[i], wo.at[i, :, far], sems.at[4 * i + 3]),
        )

    @pl.when(c == 0)
    def _():
        for i in range(4):
            for one in copies(i):
                one.start()
        for b in range(nb):
            x[b * cap : (b + 1) * cap, :] = rows_in[b][...]
            gf[b * cap : (b + 1) * cap, :] = g_in[b][...]
        logits = dot(x[...], router[...], LAST)
        lane = lax.broadcasted_iota(jnp.int32, logits.shape, 1)
        logits = jnp.where(lane < n_exp, logits, -1e30)
        powered = jnp.exp(logits - jnp.max(logits, axis=1, keepdims=True))
        probs = powered / jnp.sum(powered, axis=1, keepdims=True)
        probs_s[...] = probs
        gate = jnp.sum(jnp.where(lane == sc[0], probs, 0.0), axis=1, keepdims=True)
        rows_g = (gate * gf[...].astype(f32)).astype(bf16)
        gr[...] = rows_g
        out_b[...] = jnp.sum(rows_g.astype(f32), axis=0, keepdims=True)
        acc_y[...] = jnp.zeros_like(acc_y)
        acc_g[...] = jnp.zeros_like(acc_g)

    for i in range(4):

        @pl.when(c == i)
        def _():
            for one in copies(i):
                one.wait()

    def step(s, carry):
        cols = pl.ds(pl.multiple_of(s * hc, hc), hc)
        w_in = wi[c, :, cols]
        w_out = wo[c, cols, :]
        pre = dot(x[...], w_in) + in_bias[:, cols]
        gh = dot(gr[...], w_out, LAST)
        sq = pre * pre
        h = 0.5 + 0.5 * jnp.tanh(pre * (K0 + (K0 * C3) * sq))
        low_hidden = (pre * h).astype(bf16)
        hid[:, cols] = low_hidden
        acc_y[...] += dot(low_hidden, w_out)
        slope = h + (h - h * h) * (pre * (2.0 * K0 + (6.0 * C3 * K0) * sq))
        gp = gh * slope
        in_b[:, cols] = jnp.sum(gp, axis=0, keepdims=True)
        gp = gp.astype(bf16)
        gp_out[:, cols] = gp
        acc_g[...] += dot(gp, w_in, LAST)
        return carry

    lax.fori_loop(0, part // hc, step, 0)

    @pl.when(c == 3)
    def _():
        y = (acc_y[...] + out_bias[...]).astype(bf16)
        grad_gate = jnp.sum(gf[...].astype(f32) * y.astype(f32), axis=1, keepdims=True)
        probs = probs_s[...]
        lane = lax.broadcasted_iota(jnp.int32, probs.shape, 1)
        own = jnp.where(lane == sc[0], 1.0, 0.0)
        gate = jnp.sum(own * probs, axis=1, keepdims=True)
        grad_logits = ((grad_gate * gate) * (own - probs)).astype(bf16)
        gm = (acc_g[...] + dot(grad_logits, router[...])).astype(bf16)
        router_g[...] = dot(grad_logits, x[...], FIRST)[: router_g.shape[0], :]
        for b in range(nb):
            y_out[b][...] = y[b * cap : (b + 1) * cap, :]
            gm_out[b][...] = gm[b * cap : (b + 1) * cap, :]


def moe_rows(sc, rows, grads, weights, in_bias, out_bias, router, cap, n_exp):
    nb = len(rows)
    nr = nb * cap
    width = rows[0].shape[1]
    part = weights[0][0].shape[1]
    hidden = 4 * part
    lanes = -(-n_exp // 8) * 8
    hc = 256
    whole = lambda dims: pl.BlockSpec(dims, lambda c, sc: (0,) * len(dims))
    grid_spec = pltpu.PrefetchScalarGridSpec(
        num_scalar_prefetch=1,
        grid=(4,),
        in_specs=[whole((cap, width))] * (2 * nb)
        + [pl.BlockSpec(memory_space=pl.ANY)] * 16
        + [
            pl.BlockSpec((1, part), lambda c, sc: (0, sc[2 + c])),
            whole((1, width)),
            whole((128, width)),
        ],
        out_specs=[whole((cap, width))] * (2 * nb)
        + [
            pl.BlockSpec((nr, part), lambda c, sc: (0, c)),
            pl.BlockSpec((nr, part), lambda c, sc: (0, c)),
            whole((nr, width)),
            pl.BlockSpec((1, part), lambda c, sc: (0, sc[2 + c])),
            whole((1, width)),
            whole((lanes, width)),
        ],
        scratch_shapes=[
            pltpu.VMEM((nr, width), bf16),
            pltpu.VMEM((nr, width), bf16),
            pltpu.VMEM((4, width, part), bf16),
            pltpu.VMEM((4, part, width), bf16),
            pltpu.VMEM((nr, width), f32),
            pltpu.VMEM((nr, width), f32),
            pltpu.VMEM((nr, 128), f32),
            pltpu.SemaphoreType.DMA((16,)),
        ],
    )
    out = pl.pallas_call(
        functools.partial(moe_kernel, nb, cap, n_exp, hc),
        name="expert_rows",
        grid_spec=grid_spec,
        out_shape=[shape((cap, width), bf16)] * (2 * nb)
        + [
            shape((nr, hidden), bf16),
            shape((nr, hidden), bf16),
            shape((nr, width), bf16),
            shape((1, hidden), f32),
            shape((1, width), f32),
            shape((lanes, width), f32),
        ],
        compiler_params=pltpu.CompilerParams(vmem_limit_bytes=60 * 1024 * 1024),
        cost_estimate=pl.CostEstimate(
            flops=8 * nr * width * hidden,
            bytes_accessed=4 * width * hidden + 4 * nr * hidden,
            transcendentals=nr * hidden,
        ),
    )(sc, *rows, *grads, *[w for kind in weights for w in kind], in_bias, out_bias, router)
    return out[:nb], out[nb : 2 * nb], out[2 * nb :]


def weight_kernel(nb, cap, counts, sc, *refs):
    rows, gr, hid, gp = (
        refs[:nb],
        refs[nb : nb + len(counts)],
        refs[nb + len(counts) : nb + 2 * len(counts)],
        refs[nb + 2 * len(counts) : nb + 3 * len(counts)],
    )
    keep, send, xt, gt, cat = refs[nb + 3 * len(counts) :]
    c = pl.program_id(0)
    width = xt.shape[0]
    half = width // 2

    def gather(parts):
        at = 0
        for one in parts:
            cat[at : at + one.shape[0], :] = one[...]
            at += one.shape[0]

    @pl.when(c == 0)
    def _():
        gather(rows)
        xt[...] = cat[...].T
        gather(gr)
        gt[...] = cat[...].T

    near = pl.ds(pl.multiple_of(sc[1] * half, half), half)
    far = pl.ds(pl.multiple_of((1 - sc[1]) * half, half), half)
    gather(gp)
    keep[0, 0] = dot(xt[near, :], cat[...]).astype(bf16)
    send[0, 0] = dot(xt[far, :], cat[...]).astype(bf16)
    gather(hid)
    keep[0, 1] = dot(gt[near, :], cat[...]).astype(bf16)
    send[0, 1] = dot(gt[far, :], cat[...]).astype(bf16)


def weight_grads(sc, rows, groups, cap):
    nb = len(rows)
    width = rows[0].shape[1]
    hidden = groups[0][1].shape[1]
    part = hidden // 4
    counts = [g[0].shape[0] for g in groups]
    total = nb * cap
    whole = lambda dims: pl.BlockSpec(dims, lambda c, sc: (0,) * len(dims))
    block = (1, 2, width // 2, part)
    grid_spec = pltpu.PrefetchScalarGridSpec(
        num_scalar_prefetch=1,
        grid=(4,),
        in_specs=[whole((cap, width))] * nb
        + [whole((n, width)) for n in counts]
        + [pl.BlockSpec((n, part), lambda c, sc: (0, c)) for n in counts] * 2,
        out_specs=[
            pl.BlockSpec(block, lambda c, sc: (c, 0, 0, 0)),
            pl.BlockSpec(
                block,
                lambda c, sc: (jnp.where(c == 1, 2, jnp.where(c == 2, 1, c)), 0, 0, 0),
            ),
        ],
        scratch_shapes=[
            pltpu.VMEM((width, total), bf16),
            pltpu.VMEM((width, total), bf16),
            pltpu.VMEM((total, width), bf16),
        ],
    )
    return pl.pallas_call(
        functools.partial(weight_kernel, nb, cap, counts),
        name="expert_weights",
        grid_spec=grid_spec,
        out_shape=[shape((4, 2, width // 2, part), bf16)] * 2,
        compiler_params=pltpu.CompilerParams(vmem_limit_bytes=60 * 1024 * 1024),
        cost_estimate=pl.CostEstimate(
            flops=4 * total * width * hidden,
            bytes_accessed=4 * total * hidden + 4 * width * hidden,
            transcendentals=0,
        ),
    )(sc, *rows, *[g[0] for g in groups], *[g[1] for g in groups], *[g[2] for g in groups])


def attn_back(qkv, dctx, dqkv, pair_range, low, images):
    lo, hi = pair_range
    pairs = hi - lo

    def pair_step(step, carry):
        img, pair = step // pairs, lax.rem(step, pairs)
        rows = pl.ds(pl.multiple_of(img * SEQ_PAD, 16), SEQ_PAD)
        cols = pl.ds(pl.multiple_of((pair + lo) * PAIR, PAIR), PAIR)
        local = pl.ds(pl.multiple_of(pair * PAIR, PAIR), PAIR)
        q, k, v, gc = qkv[0, rows, cols], qkv[1, rows, cols], qkv[2, rows, cols], dctx[rows, cols]
        zero = jnp.zeros_like(q)
        outs = []
        for first in (True, False):
            mine = lambda t: jnp.where(low, t, zero) if first else jnp.where(low, zero, t)
            probs = attn_probs(mine(q), k)
            grad_p = dot(mine(gc), v, LAST)
            mean = jnp.sum(grad_p * probs, axis=1, keepdims=True)
            ds = (probs * (grad_p - mean)).astype(bf16)
            outs.append((dot(ds, k), dot(ds, q, FIRST), dot(probs.astype(bf16), gc, FIRST)))
        join = [jnp.where(low, a, b) for a, b in zip(*outs, strict=True)]
        dqkv[0, rows, local] = (join[0] * (HD**-0.5)).astype(bf16)
        dqkv[1, rows, local] = join[1].astype(bf16)
        dqkv[2, rows, local] = join[2].astype(bf16)
        return carry

    lax.fori_loop(0, images * pairs, pair_step, 0, unroll=2)


def store_slabs(sc, full, keep, send, zs):
    n = keep.shape[2]
    for i in range(4):
        for d in range(zs):
            z = lax.rem(sc[0] + d, zs) if zs > 1 else 0
            base = sc[2 + i] * (n * zs) + z * n
            near = pl.multiple_of(sc[1] * (n * zs * 4) + base, 8)
            keep[i, d] = full[pl.ds(near, n), :].astype(bf16)
            base = sc[6 + i] * (n * zs) + z * n
            far = pl.multiple_of((1 - sc[1]) * (n * zs * 4) + base, 8)
            send[i, d] = full[pl.ds(far, n), :].astype(bf16)


def back_one_kernel(
    n_exp, cap, zs, sc, slot_c, res, gain2, g_pad, ctx, wp, qkv, attn_in, *refs
):
    gm_in = refs[:n_exp]
    keep, send, grad_res, dctx, dqkv, small, full = refs[n_exp:]
    tp, width = res.shape
    images = tp // SEQ_PAD
    cols = slot_c[...]
    grad_moe = dot(pick_cols(cols, 0, cap), gm_in[0][...])
    for d in range(1, n_exp):
        grad_moe += dot(pick_cols(cols, d, cap), gm_in[d][...])
    normed, inverse = norm_rows(res[...])
    grad_res[...] = g_pad[...].astype(f32) + norm_back(grad_moe, normed, inverse, gain2[...])
    small[0:1, :] = jnp.sum(grad_moe * normed, axis=0, keepdims=True)
    small[1:2, :] = jnp.sum(grad_moe, axis=0, keepdims=True)
    small[2:3, :] = jnp.sum(grad_res[...], axis=0, keepdims=True)
    mix = grad_res[...].astype(bf16)
    part = dqkv.shape[2]
    full[:, 3 * part :] = dot(ctx[...], mix, FIRST)
    dctx[...] = dot(mix, wp[...], LAST).astype(bf16)
    attn_back(qkv, dctx, dqkv, (0, part // PAIR), head_masks(SEQ_PAD), images)
    a = attn_in[...]
    for i in range(3):
        full[:, i * part : (i + 1) * part] = dot(a, dqkv[i], FIRST)
    store_slabs(sc, full, keep, send, zs)
    small[3:4, :part] = jnp.sum(dqkv[0].astype(f32), axis=0, keepdims=True)
    small[4:5, :part] = jnp.sum(dqkv[2].astype(f32), axis=0, keepdims=True)


def back_two_kernel(
    zs, sc, qkv, attn_in, dctx, done, grad_res, w3, x_ref, gain1,
    keep, send, grad_tokens, small, full, dqkv, wide,
):
    tp, width = grad_res.shape
    images = tp // SEQ_PAD
    part = done.shape[2]
    rest = width - part
    attn_back(qkv, dctx, dqkv, (part // PAIR, width // PAIR), head_masks(SEQ_PAD), images)
    a = attn_in[...]
    for i in range(3):
        full[:, i * rest : (i + 1) * rest] = dot(a, dqkv[i], FIRST)
    store_slabs(sc, full, keep, send, zs)
    small[2:3, :rest] = jnp.sum(dqkv[0].astype(f32), axis=0, keepdims=True)
    small[3:4, :rest] = jnp.sum(dqkv[2].astype(f32), axis=0, keepdims=True)
    grad_in = dot(done[0], w3[0, :, :part], LAST) + dot(dqkv[0], w3[0, :, part:], LAST)
    for i in (1, 2):
        grad_in += dot(done[i], w3[i, :, :part], LAST) + dot(dqkv[i], w3[i, :, part:], LAST)
    spread_images(wide, x_ref[...].astype(f32), images)
    normed, inverse = norm_rows(wide[...])
    small[0:1, :] = jnp.sum(grad_in * normed, axis=0, keepdims=True)
    small[1:2, :] = jnp.sum(grad_in, axis=0, keepdims=True)
    wide[...] = grad_res[...] + norm_back(grad_in, normed, inverse, gain1[...])
    for i in range(images):
        grad_tokens[i * SEQ : (i + 1) * SEQ, :] = wide[i * SEQ_PAD : i * SEQ_PAD + SEQ, :]


def out_kernel(n_exp, cap, slot_c, moe_in, router, res, *refs):
    y_in = refs[:n_exp]
    out, wide, tight = refs[n_exp:]
    cols = slot_c[...]
    logits = dot(moe_in[...], router[...], LAST)
    lane = lax.broadcasted_iota(jnp.int32, logits.shape, 1)
    logits = jnp.where(lane < n_exp, logits, -1e30)
    powered = jnp.exp(logits - jnp.max(logits, axis=1, keepdims=True))
    probs = powered / jnp.sum(powered, axis=1, keepdims=True)
    total = res[...]
    for d in range(n_exp):
        total += probs[:, d : d + 1] * dot(pick_cols(cols, d, cap), y_in[d][...])
    wide[...] = total
    for i in range(res.shape[0] // SEQ_PAD):
        tight[i * SEQ : (i + 1) * SEQ, :] = wide[i * SEQ_PAD : i * SEQ_PAD + SEQ, :]
    out[...] = tight[...].astype(bf16)


def unpack_kernel(zs, pieces, sc, *refs):
    ins, (w_qkv, w_proj) = refs[:-2], refs[-2:]
    width = w_proj.shape[0]
    at = 0
    for which, lanes in enumerate(pieces):
        for q in range(2):
            for i in range(4):
                ref = ins[at]
                at += 1
                n = ref.shape[1]
                for d in range(zs):
                    z = lax.rem(sc[0] - d + zs, zs) if zs > 1 else 0
                    gx = sc[1] if q == 0 else 1 - sc[1]
                    row = pl.multiple_of(((gx * 4 + sc[2 + i]) * zs + z) * n, 8)
                    rows = pl.ds(row, n)
                    start = 0 if which == 0 else width - lanes
                    for p in range(3):
                        w_qkv[p, rows, start : start + lanes] = ref[d, :, p * lanes : (p + 1) * lanes].astype(f32)
                    if which == 0:
                        w_proj[rows, :] = ref[d, :, 3 * lanes :].astype(f32)


def per_device(
    tokens, routes, cotangent, norm1_gain, norm1_shift, w_qkv, qv_bias, w_proj, proj_bias,
    norm2_gain, norm2_shift, router_w, expert_in, expert_in_bias, expert_out, expert_out_bias,
):
    n_ea, n_gx, n_gy = (lax.axis_size(a) for a in ("ea", "gx", "gy"))
    n_exp = expert_in.shape[0] * n_ea
    assert expert_in.shape[0] == 1 and n_gx == 2 and n_gy == 4
    t, width = tokens.shape
    images = t // SEQ
    tp = images * SEQ_PAD
    capacity = max(2, 8 * t // (3 * n_exp) + 1)
    cap = -(-capacity // 16) * 16
    half = width // 2
    part = expert_in.shape[2]
    zs = n_ea if (width // 8) % (8 * n_ea) == 0 else 1
    first = (HEADS // 4) * PAIR

    ea, gx, gy = (lax.axis_index(a) for a in ("ea", "gx", "gy"))
    near, far = 1 + gx, 2 - gx
    sc = jnp.stack([
        ea, gx, gy, gy ^ near, gy ^ far, gy ^ 3, gy, gy ^ far, gy ^ near, gy ^ 3,
    ]).astype(jnp.int32)
    swap = (0, 2, 1, 3)
    cross = [(0, 1), (1, 0)]
    perm_a = [(g * 4 + y, g * 4 + (y ^ (1 + g))) for g in range(2) for y in range(4)]
    perm_b = [(g * 4 + y, g * 4 + (y ^ (2 - g))) for g in range(2) for y in range(4)]

    def over_gx(v):
        return lax.ppermute(v, "gx", cross)

    def over_a(v):
        return lax.ppermute(v, ("gx", "gy"), perm_a)

    def over_b(v):
        return lax.ppermute(v, ("gx", "gy"), perm_b)

    def shift(v, d):
        return lax.ppermute(v, "ea", [(i, (i + d) % n_ea) for i in range(n_ea)])

    order = [1, 3, 2] if n_ea == 4 else list(range(1, n_ea))

    def dispatch(blocks):
        got = [blocks[0]] + [None] * (n_ea - 1)
        for d in order:
            got[d] = shift(blocks[d], d)
        return got

    def give_back(blocks):
        got = [blocks[0]] + [None] * (n_ea - 1)
        for d in order:
            got[d] = shift(blocks[d], n_ea - d)
        return got

    w_in, w_out = expert_in[0], expert_out[0]
    mine_in, mine_out = [w_in], [w_out]
    mine_in.append(over_a(w_in))
    mine_out.append(over_a(w_out))
    for i in range(2):
        mine_in.append(over_b(mine_in[i]))
        mine_out.append(over_b(mine_out[i]))
    other_in = [over_gx(v) for v in mine_in]
    other_out = [over_gx(v) for v in mine_out]
    weights = (mine_in, [other_in[i] for i in swap], mine_out, [other_out[i] for i in swap])

    rel = jnp.where(routes >= ea, routes - ea, routes - ea + n_exp)
    rel_c = jnp.pad(
        rel.reshape(images, SEQ, 2), ((0, 0), (0, SEQ_PAD - SEQ), (0, 0)), constant_values=-1
    ).reshape(tp, 2)
    rel_r = rel_c.T
    lanes = -(-n_exp // 8) * 8
    block = shape((cap, width), bf16)
    slot_r, slot_c, g_pad, *g_sent = call(
        "route",
        functools.partial(prep_kernel, n_exp, cap),
        [shape((lanes, tp), f32), shape((tp, 128), f32), shape((tp, width), bf16)] + [block] * n_exp,
        (rel_r, rel_c, cotangent),
        flops=2 * n_exp * cap * tp * width,
        bytes_accessed=2 * t * width * 4,
        scratch=[pltpu.VMEM((tp, width), f32)],
    )
    g_rows = dispatch(g_sent)

    w3 = w_qkv.transpose(1, 0, 2)
    row = lambda v: v.reshape(1, width)
    res, qkv, ctx, attn_in, moe_in, *m_sent = call(
        "attn_fwd",
        functools.partial(fwd_kernel, n_exp, cap),
        [
            shape((tp, width), f32), shape((3, tp, width), bf16), shape((tp, width), bf16),
            shape((tp, width), bf16), shape((tp, width), bf16),
        ] + [block] * n_exp,
        (
            tokens, row(norm1_gain), row(norm1_shift), w3, qv_bias, w_proj, row(proj_bias),
            row(norm2_gain), row(norm2_shift), slot_r,
        ),
        flops=20 * tp * width * width,
        bytes_accessed=8 * width * width + 20 * tp * width,
        scratch=[pltpu.VMEM((tp, width), f32)],
    )
    m_rows = dispatch(m_sent)

    router = jnp.pad(router_w.T, ((0, 128 - n_exp), (0, 0)))
    groups = [[0, 1], [3], [2]] if n_ea == 4 else [list(range(n_ea))]
    y_back, gm_back = [None] * n_ea, [None] * n_ea
    kept, in_bias_g, out_bias_g, router_g = [], 0.0, 0.0, 0.0
    for group in groups:
        ys, gms, (hid, gp, gr, ib, ob, rg) = moe_rows(
            sc, [m_rows[d] for d in group], [g_rows[d] for d in group], weights,
            expert_in_bias, expert_out_bias, router, cap, n_exp,
        )
        kept.append((gr, hid, gp))
        in_bias_g, out_bias_g, router_g = in_bias_g + ib, out_bias_g + ob, router_g + rg
        for d, y, gm in zip(group, ys, gms, strict=True):
            gm_back[d] = shift(gm, n_ea - d) if d else gm
            y_back[d] = y
    keep, send = weight_grads(sc, [m_rows[d] for group in groups for d in group], kept, cap)

    def add(*parts):
        return functools.reduce(lambda a, b: a + b, [p.astype(f32) for p in parts]).astype(bf16)

    got = over_gx(send)
    got_b = over_b(add(keep[2:], got[2:]))
    to_a = over_a(add(keep[1], got[1], got_b[1]))
    expert_grads = (
        keep[0].astype(f32) + got[0].astype(f32) + got_b[0].astype(f32) + to_a.astype(f32)
    )
    in_w_grad = expert_grads[0][None]
    out_w_grad = expert_grads[1].T[None]

    def reduce_slabs(keep, send):
        got = over_gx(send)
        got_b = over_b(add(keep[2:], got[2:]))
        got_a = over_a(add(keep[1], got[1], got_b[1]))
        slabs = add(keep[0], got[0], got_b[0], got_a)
        if zs > 1:
            own = [slabs[0]] + [shift(slabs[d], d) for d in range(1, zs)]
            own = add(*own)
            b0 = jnp.stack([own] + [shift(own, d) for d in range(1, zs)])
        else:
            b0 = lax.psum(slabs, "ea")
        b1 = over_a(b0)
        b2, b3 = over_b(b0), over_b(b1)
        mine = [b0, b1, b2, b3]
        other = [over_gx(v) for v in mine]
        return mine + [other[i] for i in swap]

    gm_rows = gm_back
    n = width // (8 * zs)
    slabs = lambda l: [shape((4, zs, n, l), bf16)] * 2
    keep_one, send_one, grad_res, dctx, dqkv, small_one = call(
        "back_one",
        functools.partial(back_one_kernel, n_exp, cap, zs),
        slabs(3 * first + width) + [
            shape((tp, width), f32), shape((tp, width), bf16), shape((3, tp, first), bf16),
            shape((8, width), f32),
        ],
        (
            sc, slot_c, res, row(norm2_gain), g_pad, ctx, w_proj, qkv, attn_in, *gm_rows,
        ),
        flops=12 * tp * width * width,
        bytes_accessed=16 * tp * width + 10 * width * width,
        scratch=[pltpu.VMEM((width, 3 * first + width), f32)],
        smem=1,
    )
    one = reduce_slabs(keep_one, send_one)
    rest = width - first
    keep_two, send_two, grad_tokens, small_two = call(
        "back_two",
        functools.partial(back_two_kernel, zs),
        slabs(3 * rest) + [shape((t, width), f32), shape((8, width), f32)],
        (sc, qkv, attn_in, dctx, dqkv, grad_res, w3, tokens, row(norm1_gain)),
        flops=14 * tp * width * width,
        bytes_accessed=16 * tp * width + 10 * width * width,
        scratch=[
            pltpu.VMEM((width, 3 * rest), f32),
            pltpu.VMEM((3, tp, rest), bf16),
            pltpu.VMEM((tp, width), f32),
        ],
        smem=1,
    )
    two = reduce_slabs(keep_two, send_two)

    y_rows = [shift(y_back[d], n_ea - d) if d else y_back[d] for d in range(n_ea)]
    rolled = jnp.pad(
        lax.dynamic_slice_in_dim(jnp.concatenate([router_w.T, router_w.T]), ea, n_exp, 0),
        ((0, 128 - n_exp), (0, 0)),
    )
    output = call(
        "combine",
        functools.partial(out_kernel, n_exp, cap),
        shape((t, width), bf16),
        (slot_c, moe_in, rolled, res, *y_rows),
        flops=2 * n_exp * cap * tp * width,
        bytes_accessed=8 * tp * width,
        scratch=[pltpu.VMEM((tp, width), f32), pltpu.VMEM((t, width), f32)],
    )

    qv_g = jnp.stack([
        jnp.concatenate([small_one[3, :first], small_two[2, :rest]]),
        jnp.concatenate([small_one[4, :first], small_two[3, :rest]]),
    ])
    small = jnp.concatenate([
        small_two[0:2], small_one[0:3], qv_g, in_bias_g.reshape(4, part), out_bias_g, router_g[:n_exp],
    ])
    small = small + over_gx(small)
    whole_gy = [lax.ppermute(small, "gy", [(y, y ^ k) for y in range(4)]) for k in (1, 2, 3)]
    small = small + whole_gy[0] + (whole_gy[1] + whole_gy[2])
    if n_ea <= 4:
        over_ea = sum([shift(small, d) for d in range(1, n_ea)], small)
    else:
        over_ea = lax.psum(small, "ea")

    w_qkv_g, w_proj_g = call(
        "unpack",
        functools.partial(unpack_kernel, zs, (first, rest)),
        [shape((3, width, width), f32), shape((width, width), f32)],
        (sc, *one, *two),
        bytes_accessed=24 * width * width,
        smem=1,
    )
    return (
        output,
        grad_tokens,
        over_ea[0],
        over_ea[1],
        w_qkv_g.transpose(1, 0, 2),
        over_ea[5:7],
        w_proj_g,
        over_ea[4],
        over_ea[2],
        over_ea[3],
        over_ea[12:].T,
        in_w_grad,
        small[7:11].reshape(1, 4 * part),
        out_w_grad,
        small[11:12],
    )


def solution(mesh):
    tok = P(("ea", "gx", "gy"), None)
    in_specs = (
        tok, tok, tok, P(), P(), P(), P(), P(), P(), P(), P(), P(),
        P("ea", "gx", "gy"), P("ea", None), P("ea", "gy", "gx"), P("ea", None),
    )
    out_specs = (
        tok, tok, P(), P(), P(), P(), P(), P(), P(), P(), P(),
        P("ea", "gx", "gy"), P("ea", None), P("ea", "gy", "gx"), P("ea", None),
    )
    return jax.shard_map(per_device, mesh=mesh, in_specs=in_specs, out_specs=out_specs, check_vma=False)
```

```python
import functools
import math

import jax
import jax.numpy as jnp
from jax import lax
from jax.experimental import pallas as pl
from jax.experimental.pallas import tpu as pltpu
from jax.sharding import PartitionSpec as P

HEADS = 12
HD = 64
SEQ = 197
SEQ_PAD = 208
PAIR = 2 * HD
norm_eps = 1e-06

f32 = jnp.float32
bf16 = jnp.bfloat16
LAST = (((1,), (1,)), ((), ()))
FIRST = (((0,), (0,)), ((), ()))
K0 = math.sqrt(2.0 / math.pi)
C3 = 0.044715


def dot(a, b, dims=None):
    if dims is None:
        return jnp.dot(a, b, preferred_element_type=f32)
    return lax.dot_general(a, b, dims, preferred_element_type=f32)


def spec():
    return pl.BlockSpec(memory_space=pltpu.VMEM)


def call(name, kernel, out_shape, args, flops=1, scratch=(), smem=0):
    return pl.pallas_call(
        kernel,
        name=name,
        out_shape=out_shape,
        in_specs=[pl.BlockSpec(memory_space=pltpu.SMEM)] * smem
        + [spec()] * (len(args) - smem),
        out_specs=jax.tree.map(lambda _: spec(), out_shape),
        scratch_shapes=list(scratch),
        compiler_params=pltpu.CompilerParams(vmem_limit_bytes=60 * 1024 * 1024),
        cost_estimate=pl.CostEstimate(
            flops=flops, bytes_accessed=1, transcendentals=0
        ),
    )(*args)


def shape(dims, dtype):
    return jax.ShapeDtypeStruct(tuple(dims), dtype)


def norm_rows(values):
    centered = values - jnp.mean(values, axis=1, keepdims=True)
    inverse = lax.rsqrt(jnp.mean(centered * centered, axis=1, keepdims=True) + norm_eps)
    return centered * inverse, inverse


def norm_back(grad, normed, inverse, gain):
    scaled = grad * gain
    return inverse * (
        scaled
        - jnp.mean(scaled, axis=1, keepdims=True)
        - normed * jnp.mean(scaled * normed, axis=1, keepdims=True)
    )


def spread_images(dst, src, images):
    width = src.shape[1]
    for i in range(images):
        dst[i * SEQ_PAD : i * SEQ_PAD + SEQ, :] = src[i * SEQ : (i + 1) * SEQ, :]
        dst[i * SEQ_PAD + SEQ : (i + 1) * SEQ_PAD, :] = jnp.zeros((SEQ_PAD - SEQ, width), dst.dtype)


def pick_rows(slot_rows, d, cap):
    slots = lax.broadcasted_iota(jnp.int32, (cap, slot_rows.shape[1]), 0).astype(f32)
    return jnp.where(slots == slot_rows[d : d + 1, :], 1.0, 0.0).astype(bf16)


def pick_cols(slot_cols, d, cap):
    slots = lax.broadcasted_iota(jnp.int32, (slot_cols.shape[0], cap), 1).astype(f32)
    return jnp.where(slots == slot_cols[:, d : d + 1], 1.0, 0.0).astype(bf16)


def prep_kernel(
    n_exp, cap, sc, routes, g_ref, x_ref, gain1, shift1, w3, qvb,
    slot_r, slot_c, g_pad, wide, qkv, attn_in, *sent,
):
    t, tp = routes.shape[1], slot_r.shape[1]
    lanes = slot_r.shape[0]
    ids = lax.broadcasted_iota(jnp.int32, (lanes, t), 0) + sc[0]
    ids = jnp.where(ids >= n_exp, ids - n_exp, ids)
    real = lax.broadcasted_iota(jnp.int32, (lanes, t), 0) < n_exp
    chosen = ((routes[0:1, :] == ids) | (routes[1:2, :] == ids)) & real
    ti = lax.broadcasted_iota(jnp.int32, (t, tp), 0)
    tj = lax.broadcasted_iota(jnp.int32, (t, tp), 1)
    moved = jnp.where(ti + (ti // SEQ) * (SEQ_PAD - SEQ) == tj, 1.0, 0.0).astype(bf16)
    chosen = dot(jnp.where(chosen, 1.0, 0.0).astype(bf16), moved)
    ti = lax.broadcasted_iota(jnp.int32, (tp, tp), 0)
    tj = lax.broadcasted_iota(jnp.int32, (tp, tp), 1)
    before = jnp.where(ti < tj, 1.0, 0.0).astype(bf16)
    slots = jnp.where(chosen > 0.5, dot(chosen.astype(bf16), before), -1.0)
    slot_r[...] = slots
    slot_c[...] = jnp.full(slot_c.shape, -1.0, f32)
    slot_c[:, :lanes] = slots.T
    spread_images(wide, g_ref[...].astype(f32), tp // SEQ_PAD)
    g_pad[...] = wide[...].astype(bf16)
    rows = slot_r[...]
    for d in range(n_exp):
        sent[d][...] = dot(pick_rows(rows, d, cap), g_pad[...]).astype(bf16)
    spread_images(wide, x_ref[...].astype(f32), tp // SEQ_PAD)
    normed, _ = norm_rows(wide[...])
    attn_in[...] = (normed * gain1[...].reshape(1, -1) + shift1[...].reshape(1, -1)).astype(bf16)
    a = attn_in[...]
    qkv[0] = ((dot(a, w3[0]) + qvb[0:1, :]).astype(bf16).astype(f32) * (HD**-0.5)).astype(bf16)
    qkv[1] = dot(a, w3[1]).astype(bf16)
    qkv[2] = (dot(a, w3[2]) + qvb[1:2, :]).astype(bf16)


def head_masks(rows):
    lane = lax.broadcasted_iota(jnp.int32, (rows, PAIR), 1)
    return lane < HD


def attn_probs(q_head, k_pair):
    scores = dot(q_head, k_pair, LAST)
    keys = lax.broadcasted_iota(jnp.int32, scores.shape, 1)
    scores = jnp.where(keys < SEQ, scores, -1e30)
    powered = jnp.exp(scores - jnp.max(scores, axis=1, keepdims=True))
    return powered * (1.0 / jnp.sum(powered, axis=1, keepdims=True))


def fwd_kernel(n_exp, cap, qkv, wide, wp, pb, gain2, shift2, slot_r, res, ctx, moe_in, *sent):
    tp, width = res.shape
    images = tp // SEQ_PAD
    low = head_masks(SEQ_PAD)
    pairs = width // PAIR

    def pair_step(step, carry):
        img, pair = step // pairs, lax.rem(step, pairs)
        rows = pl.ds(pl.multiple_of(img * SEQ_PAD, 16), SEQ_PAD)
        cols = pl.ds(pl.multiple_of(pair * PAIR, PAIR), PAIR)
        q, k, v = qkv[0, rows, cols], qkv[1, rows, cols], qkv[2, rows, cols]
        zero = jnp.zeros_like(q)
        p0 = attn_probs(jnp.where(low, q, zero), k).astype(bf16)
        p1 = attn_probs(jnp.where(low, zero, q), k).astype(bf16)
        ctx[rows, cols] = jnp.where(low, dot(p0, v), dot(p1, v)).astype(bf16)
        return carry

    lax.fori_loop(0, images * pairs, pair_step, 0, unroll=2)
    res[...] = wide[...] + dot(ctx[...], wp[...]) + pb[...].reshape(1, -1)
    normed, _ = norm_rows(res[...])
    moe_in[...] = (normed * gain2[...].reshape(1, -1) + shift2[...].reshape(1, -1)).astype(bf16)
    rows = slot_r[...]
    for d in range(n_exp):
        sent[d][...] = dot(pick_rows(rows, d, cap), moe_in[...]).astype(bf16)


def moe_kernel(places, cap, n_exp, hc, fresh, sc, *refs):
    nb = len(places)
    rows_in, g_in = refs[:nb], refs[nb : 2 * nb]
    mine, other = refs[2 * nb : 2 * nb + 5], refs[2 * nb + 5 : 2 * nb + 10]
    r = 2 * nb + 10
    in_bias, out_bias, router = refs[r : r + 3]
    r += 3 if fresh else 4
    y_all, gm_out = refs[r], refs[r + 1 : r + 1 + nb]
    r += 1 + nb
    hid, gp_out, gr, in_b, out_b, router_g = refs[r : r + 6]
    r += 6
    x, gf, wi, wo, acc_y, acc_g, probs_s, y_s, sems, y_sems = refs[r:]
    c = pl.program_id(0)
    width = x.shape[1]
    half = width // 2
    part = wi.shape[2]

    def copies(i):
        gx = sc[1]
        near = pl.ds(pl.multiple_of(gx * half, half), half)
        far = pl.ds(pl.multiple_of((1 - gx) * half, half), half)
        found = []
        for k, (held, cols) in enumerate(((mine, near), (other, far))):
            first, second = (held[i].at[0], held[i].at[1]) if i < 3 else (held[3], held[4])
            found.append(pltpu.make_async_copy(first, wi.at[i, cols, :], sems.at[6 * i + 3 * k]))
            for u in range(2):
                found.append(
                    pltpu.make_async_copy(
                        second.at[:, u * half : (u + 1) * half],
                        wo.at[i, u * half : (u + 1) * half, cols],
                        sems.at[6 * i + 3 * k + 1 + u],
                    )
                )
        return found

    @pl.when(c == 0)
    def _():
        for i in range(4):
            for one in copies(i):
                one.start()
        for b in range(nb):
            x[b * cap : (b + 1) * cap, :] = rows_in[b][...]
            gf[b * cap : (b + 1) * cap, :] = g_in[b][...]
        logits = dot(x[...], router[...], LAST)
        lane = lax.broadcasted_iota(jnp.int32, logits.shape, 1)
        logits = jnp.where(lane < n_exp, logits, -1e30)
        powered = jnp.exp(logits - jnp.max(logits, axis=1, keepdims=True))
        probs = powered / jnp.sum(powered, axis=1, keepdims=True)
        probs_s[...] = probs
        gate = jnp.sum(jnp.where(lane == sc[0], probs, 0.0), axis=1, keepdims=True)
        rows_g = (gate * gf[...].astype(f32)).astype(bf16)
        gr[...] = rows_g
        out_b[...] = jnp.sum(rows_g.astype(f32), axis=0, keepdims=True)
        acc_y[...] = jnp.zeros_like(acc_y)
        acc_g[...] = jnp.zeros_like(acc_g)

    for i in range(4):

        @pl.when(c == i)
        def _():
            for one in copies(i):
                one.wait()

    def step(s, carry):
        cols = pl.ds(pl.multiple_of(s * hc, hc), hc)
        w_in = wi[c, :, cols]
        w_out = wo[c, cols, :]
        pre = dot(x[...], w_in) + in_bias[:, cols]
        gh = dot(gr[...], w_out, LAST)
        sq = pre * pre
        h = 0.5 + 0.5 * jnp.tanh(pre * (K0 + (K0 * C3) * sq))
        low_hidden = (pre * h).astype(bf16)
        hid[:, cols] = low_hidden
        acc_y[...] += dot(low_hidden, w_out)
        slope = h + (h - h * h) * (pre * (2.0 * K0 + (6.0 * C3 * K0) * sq))
        gp = gh * slope
        in_b[:, cols] = jnp.sum(gp, axis=0, keepdims=True)
        gp = gp.astype(bf16)
        gp_out[:, cols] = gp
        acc_g[...] += dot(gp, w_in, LAST)
        return carry

    lax.fori_loop(0, part // hc, step, 0)

    @pl.when(c == 3)
    def _():
        y = (acc_y[...] + out_bias[...]).astype(bf16)
        for b in range(nb):
            y_s[b] = y[b * cap : (b + 1) * cap, :]
        back = [
            pltpu.make_async_copy(
                y_s.at[b], y_all.at[lax.rem(sc[0] + n_exp - d, n_exp)], y_sems.at[b]
            )
            for b, d in enumerate(places)
        ]
        for one in back:
            one.start()
        grad_gate = jnp.sum(gf[...].astype(f32) * y.astype(f32), axis=1, keepdims=True)
        probs = probs_s[...]
        lane = lax.broadcasted_iota(jnp.int32, probs.shape, 1)
        own = jnp.where(lane == sc[0], 1.0, 0.0)
        gate = jnp.sum(own * probs, axis=1, keepdims=True)
        grad_logits = ((grad_gate * gate) * (own - probs)).astype(bf16)
        gm = (acc_g[...] + dot(grad_logits, router[...])).astype(bf16)
        router_g[...] = dot(grad_logits, x[...], FIRST)[: router_g.shape[0], :]
        for b in range(nb):
            gm_out[b][...] = gm[b * cap : (b + 1) * cap, :]
        for one in back:
            one.wait()


def moe_rows(sc, places, rows, grads, weights, in_bias, out_bias, router, y_all, cap, n_exp):
    nb = len(rows)
    fresh = y_all is None
    nr = nb * cap
    width = rows[0].shape[1]
    part = weights[0].shape[2]
    hidden = 4 * part
    lanes = -(-n_exp // 8) * 8
    hc = part
    whole = lambda dims: pl.BlockSpec(dims, lambda c, sc: (0,) * len(dims))
    grid_spec = pltpu.PrefetchScalarGridSpec(
        num_scalar_prefetch=1,
        grid=(4,),
        in_specs=[whole((cap, width))] * (2 * nb)
        + [pl.BlockSpec(memory_space=pl.ANY)] * 10
        + [
            pl.BlockSpec((1, part), lambda c, sc: (0, sc[10 + c])),
            whole((1, width)),
            whole((128, width)),
        ]
        + ([] if fresh else [pl.BlockSpec(memory_space=pl.ANY)]),
        out_specs=[pl.BlockSpec(memory_space=pl.ANY)]
        + [whole((cap, width))] * nb
        + [
            pl.BlockSpec((nr, part), lambda c, sc: (0, c)),
            pl.BlockSpec((nr, part), lambda c, sc: (0, c)),
            whole((nr, width)),
            pl.BlockSpec((1, part), lambda c, sc: (0, sc[10 + c])),
            whole((1, width)),
            whole((lanes, width)),
        ],
        scratch_shapes=[
            pltpu.VMEM((nr, width), bf16),
            pltpu.VMEM((nr, width), bf16),
            pltpu.VMEM((4, width, part), bf16),
            pltpu.VMEM((4, part, width), bf16),
            pltpu.VMEM((nr, width), f32),
            pltpu.VMEM((nr, width), f32),
            pltpu.VMEM((nr, 128), f32),
            pltpu.VMEM((nb, cap, width), bf16),
            pltpu.SemaphoreType.DMA((24,)),
            pltpu.SemaphoreType.DMA((nb,)),
        ],
    )
    out = pl.pallas_call(
        functools.partial(moe_kernel, tuple(places), cap, n_exp, hc, fresh),
        name="expert_rows",
        grid_spec=grid_spec,
        out_shape=[shape((n_exp, cap, width), bf16)]
        + [shape((cap, width), bf16)] * nb
        + [
            shape((nr, hidden), bf16),
            shape((nr, hidden), bf16),
            shape((nr, width), bf16),
            shape((1, hidden), f32),
            shape((1, width), f32),
            shape((lanes, width), f32),
        ],
        compiler_params=pltpu.CompilerParams(vmem_limit_bytes=60 * 1024 * 1024),
        cost_estimate=pl.CostEstimate(
            flops=1, bytes_accessed=1, transcendentals=0
        ),
        input_output_aliases={} if fresh else {14 + 2 * nb: 0},
    )(sc, *rows, *grads, *weights, in_bias, out_bias, router, *([] if fresh else [y_all]))
    return out[0], out[1 : 1 + nb], out[1 + nb :]


def weight_kernel(nb, cap, counts, sc, *refs):
    rows, gr, hid, gp = (
        refs[:nb],
        refs[nb : nb + len(counts)],
        refs[nb + len(counts) : nb + 2 * len(counts)],
        refs[nb + 2 * len(counts) : nb + 3 * len(counts)],
    )
    out, xt, gt, cat = refs[nb + 3 * len(counts) :]
    c = pl.program_id(0)
    width = xt.shape[0]
    half = width // 2

    def gather(parts):
        at = 0
        for one in parts:
            cat[at : at + one.shape[0], :] = one[...]
            at += one.shape[0]

    @pl.when(c == 0)
    def _():
        for source, turned in ((rows, xt), (gr, gt)):
            gather(source)
            turned[...] = cat[...].T

    for j, (turned, source) in enumerate(((xt, gp), (gt, hid))):
        gather(source)
        both = dot(turned[...], cat[...]).astype(bf16)
        out[0, 0, j] = both[:half, :]
        out[1, 0, j] = both[half:, :]


def split_kernel(both, first, second):
    first[0] = both[0].astype(f32)
    second[0] = both[1].astype(f32).T


def weight_grads(sc, rows, groups, cap):
    nb = len(rows)
    width = rows[0].shape[1]
    hidden = groups[0][1].shape[1]
    part = hidden // 4
    counts = [g[0].shape[0] for g in groups]
    total = nb * cap
    whole = lambda dims: pl.BlockSpec(dims, lambda c, sc: (0,) * len(dims))
    block = (2, 1, 2, width // 2, part)
    grid_spec = pltpu.PrefetchScalarGridSpec(
        num_scalar_prefetch=1,
        grid=(4,),
        in_specs=[whole((cap, width))] * nb
        + [whole((n, width)) for n in counts]
        + [pl.BlockSpec((n, part), lambda c, sc: (0, c)) for n in counts] * 2,
        out_specs=pl.BlockSpec(block, lambda c, sc: (0, sc[10 + c], 0, 0, 0)),
        scratch_shapes=[
            pltpu.VMEM((width, total), bf16),
            pltpu.VMEM((width, total), bf16),
            pltpu.VMEM((total, width), bf16),
        ],
    )
    return pl.pallas_call(
        functools.partial(weight_kernel, nb, cap, counts),
        name="expert_weights",
        grid_spec=grid_spec,
        out_shape=shape((2, 4, 2, width // 2, part), bf16),
        compiler_params=pltpu.CompilerParams(vmem_limit_bytes=60 * 1024 * 1024),
        cost_estimate=pl.CostEstimate(
            flops=1, bytes_accessed=1, transcendentals=0
        ),
    )(sc, *rows, *[g[0] for g in groups], *[g[1] for g in groups], *[g[2] for g in groups])


def attn_back(qkv, dctx, dqkv, pair_range, low, images):
    lo, hi = pair_range
    pairs = hi - lo

    def pair_step(step, carry):
        img, pair = step // pairs, lax.rem(step, pairs)
        rows = pl.ds(pl.multiple_of(img * SEQ_PAD, 16), SEQ_PAD)
        cols = pl.ds(pl.multiple_of((pair + lo) * PAIR, PAIR), PAIR)
        local = pl.ds(pl.multiple_of(pair * PAIR, PAIR), PAIR)
        q, k, v, gc = qkv[0, rows, cols], qkv[1, rows, cols], qkv[2, rows, cols], dctx[rows, cols]
        zero = jnp.zeros_like(q)
        outs = []
        for first in (True, False):
            mine = lambda t: jnp.where(low, t, zero) if first else jnp.where(low, zero, t)
            probs = attn_probs(mine(q), k)
            grad_p = dot(mine(gc), v, LAST)
            mean = jnp.sum(grad_p * probs, axis=1, keepdims=True)
            ds = (probs * (grad_p - mean)).astype(bf16)
            outs.append((dot(ds, k), dot(ds, q, FIRST), dot(probs.astype(bf16), gc, FIRST)))
        join = [jnp.where(low, a, b) for a, b in zip(*outs, strict=True)]
        dqkv[0, rows, local] = (join[0] * (HD**-0.5)).astype(bf16)
        dqkv[1, rows, local] = join[1].astype(bf16)
        dqkv[2, rows, local] = join[2].astype(bf16)
        return carry

    lax.fori_loop(0, images * pairs, pair_step, 0, unroll=2)


def store_slabs(sc, full, keep, send, zs):
    n = keep.shape[2]
    for i in range(4):
        for d in range(zs):
            z = lax.rem(sc[0] + d, zs) if zs > 1 else 0
            base = sc[2 + i] * (n * zs) + z * n
            near = pl.multiple_of(sc[1] * (n * zs * 4) + base, 8)
            keep[i, d] = full[pl.ds(near, n), :].astype(bf16)
            base = sc[6 + i] * (n * zs) + z * n
            far = pl.multiple_of((1 - sc[1]) * (n * zs * 4) + base, 8)
            send[i, d] = full[pl.ds(far, n), :].astype(bf16)


def back_one_kernel(
    n_exp, cap, zs, sc, slot_c, res, gain2, g_pad, ctx, wp, qkv, attn_in, *refs
):
    gm_in = refs[:n_exp]
    keep, send, grad_res, dctx, dqkv, small, full = refs[n_exp:]
    tp, width = res.shape
    images = tp // SEQ_PAD
    cols = slot_c[...]
    grad_moe = dot(pick_cols(cols, 0, cap), gm_in[0][...])
    for d in range(1, n_exp):
        grad_moe += dot(pick_cols(cols, d, cap), gm_in[d][...])
    normed, inverse = norm_rows(res[...])
    grad_res[...] = g_pad[...].astype(f32) + norm_back(grad_moe, normed, inverse, gain2[...].reshape(1, -1))
    small[0:1, :] = jnp.sum(grad_moe * normed, axis=0, keepdims=True)
    small[1:2, :] = jnp.sum(grad_moe, axis=0, keepdims=True)
    small[2:3, :] = jnp.sum(grad_res[...], axis=0, keepdims=True)
    mix = grad_res[...].astype(bf16)
    part = dqkv.shape[2]
    full[:, 3 * part :] = dot(ctx[...], mix, FIRST)
    dctx[...] = dot(mix, wp[...], LAST).astype(bf16)
    attn_back(qkv, dctx, dqkv, (0, part // PAIR), head_masks(SEQ_PAD), images)
    a = attn_in[...]
    for i in range(3):
        full[:, i * part : (i + 1) * part] = dot(a, dqkv[i], FIRST)
    store_slabs(sc, full, keep, send, zs)
    small[3:4, :part] = jnp.sum(dqkv[0].astype(f32), axis=0, keepdims=True)
    small[4:5, :part] = jnp.sum(dqkv[2].astype(f32), axis=0, keepdims=True)


def back_two_kernel(
    zs, n_exp, sc, qkv, attn_in, dctx, done, grad_res, w3, x_ref, gain1, small_one, router_g, in_b, out_b,
    keep, send, grad_tokens, full, dqkv, wide, small,
):
    tp, width = grad_res.shape
    images = tp // SEQ_PAD
    part = done.shape[2]
    rest = width - part
    attn_back(qkv, dctx, dqkv, (part // PAIR, width // PAIR), head_masks(SEQ_PAD), images)
    a = attn_in[...]
    for i in range(3):
        full[:, i * rest : (i + 1) * rest] = dot(a, dqkv[i], FIRST)
    small[...] = jnp.zeros_like(small)
    small[2:5, :] = small_one[0:3, :]
    for i in (0, 2):
        row = 5 + i // 2
        small[row : row + 1, :part] = small_one[3 + i // 2 : 4 + i // 2, :part]
        small[row : row + 1, part:] = jnp.sum(dqkv[i].astype(f32), axis=0, keepdims=True)
    small[7 : 7 + n_exp, :] = router_g[:n_exp, :]
    for k in range(4):
        small[pl.ds(7 + n_exp + 4 * sc[0] + k, 1), :] = in_b[k : k + 1, :]
    small[pl.ds(7 + 5 * n_exp + sc[0], 1), :] = out_b[...]
    grad_in = dot(done[0], w3[0, :, :part], LAST) + dot(dqkv[0], w3[0, :, part:], LAST)
    for i in (1, 2):
        grad_in += dot(done[i], w3[i, :, :part], LAST) + dot(dqkv[i], w3[i, :, part:], LAST)
    spread_images(wide, x_ref[...].astype(f32), images)
    normed, inverse = norm_rows(wide[...])
    small[0:1, :] = jnp.sum(grad_in * normed, axis=0, keepdims=True)
    small[1:2, :] = jnp.sum(grad_in, axis=0, keepdims=True)
    full[:, 3 * rest :] = small[...].T
    store_slabs(sc, full, keep, send, zs)
    wide[...] = grad_res[...] + norm_back(grad_in, normed, inverse, gain1[...].reshape(1, -1))
    for i in range(images):
        grad_tokens[i * SEQ : (i + 1) * SEQ, :] = wide[i * SEQ_PAD : i * SEQ_PAD + SEQ, :]


def out_kernel(n_exp, cap, sc, slot_c, moe_in, router, res, y_in, out, wide, tight):
    cols = slot_c[...]
    logits = dot(moe_in[...], router[...], LAST)
    lane = lax.broadcasted_iota(jnp.int32, logits.shape, 1)
    logits = jnp.where(lane < n_exp, logits, -1e30)
    powered = jnp.exp(logits - jnp.max(logits, axis=1, keepdims=True))
    probs = powered / jnp.sum(powered, axis=1, keepdims=True)
    total = res[...]
    for d in range(n_exp):
        total += probs[:, d : d + 1] * dot(pick_cols(cols, d, cap), y_in[lax.rem(sc[0] + d, n_exp)])
    wide[...] = total
    for i in range(res.shape[0] // SEQ_PAD):
        tight[i * SEQ : (i + 1) * SEQ, :] = wide[i * SEQ_PAD : i * SEQ_PAD + SEQ, :]
    out[...] = tight[...].astype(bf16)


def unpack_kernel(zs, n_exp, lanes, last, sc, ref, *refs):
    if last:
        _, w_out, *vectors, qv_g, router_g, in_b, out_b, w_qkv, sems, held, turned_s = refs
    else:
        w_out, held, w_qkv, sems = refs
    n = ref.shape[2]
    start = w_out.shape[2] - lanes if last else 0

    def places():
        for place in range(8):
            for d in range(zs):
                z = lax.rem(sc[0] - d + zs, zs) if zs > 1 else 0
                yield place, d, pl.ds(pl.multiple_of((place * zs + z) * n, 8), n)

    copies = []
    for p in range(3):
        for place, d, rows in places():
            w_qkv[p, rows, :] = ref[place, d, :, p * lanes : (p + 1) * lanes].astype(f32)
        one = pltpu.make_async_copy(w_qkv.at[p], w_out.at[p, :, start : start + lanes], sems.at[p])
        one.start()
        copies.append(one)
    for place, d, rows in places():
        held[rows, :] = ref[place, d, :, 3 * lanes :].astype(f32)
    if last:
        turned = held[...].T
        for i, vector in enumerate(vectors):
            vector[...] = turned[i : i + 1, :].reshape(-1)
        qv_g[...] = turned[5:7, :]
        router_g[...] = turned[7 : 7 + n_exp, :]
        turned_s[...] = turned
        for k in range(4):
            in_b[k : k + 1, :] = turned_s[pl.ds(7 + n_exp + 4 * sc[0] + k, 1), :]
        out_b[...] = turned_s[pl.ds(7 + 5 * n_exp + sc[0], 1), :]
    for one in copies:
        one.wait()


def unpack(sc, slabs, zs, n_exp, width, lanes, base=None):
    last = base is not None
    extra = slabs.shape[-1] - 3 * lanes
    whole = lambda dims: pl.BlockSpec(dims, lambda c, sc: (0,) * len(dims))
    more = [(width,)] * 5 + [(2, width), (n_exp, width), (4, width), (1, width)] if last else [(width, extra)]
    return pl.pallas_call(
        functools.partial(unpack_kernel, zs, n_exp, lanes, last),
        name="unpack",
        grid_spec=pltpu.PrefetchScalarGridSpec(
            num_scalar_prefetch=1,
            grid=(1,),
            in_specs=[whole(slabs.shape)] + ([pl.BlockSpec(memory_space=pl.ANY)] if last else []),
            out_specs=[
                pl.BlockSpec(memory_space=pl.ANY),
                *[whole(dims) for dims in more],
            ],
            scratch_shapes=[pltpu.VMEM((3, width, lanes), f32), pltpu.SemaphoreType.DMA((3,))]
            + ([pltpu.VMEM((width, extra), f32), pltpu.VMEM((extra, width), f32)] if last else []),
        ),
        out_shape=[shape((3, width, width), f32)] + [shape(dims, f32) for dims in more],
        input_output_aliases={2: 0} if last else {},
        compiler_params=pltpu.CompilerParams(vmem_limit_bytes=60 * 1024 * 1024),
        cost_estimate=pl.CostEstimate(flops=1, bytes_accessed=1, transcendentals=0),
    )(sc, slabs, *([base] if last else []))


def per_device(
    tokens, routes, cotangent, norm1_gain, norm1_shift, w_qkv, qv_bias, w_proj, proj_bias,
    norm2_gain, norm2_shift, router_w, expert_in, expert_in_bias, expert_out, expert_out_bias,
):
    n_ea, n_gx, n_gy = (lax.axis_size(a) for a in ("ea", "gx", "gy"))
    n_exp = expert_in.shape[0] * n_ea
    assert expert_in.shape[0] == 1 and n_gx == 2 and n_gy == 4
    t, width = tokens.shape
    images = t // SEQ
    tp = images * SEQ_PAD
    capacity = max(2, 8 * t // (3 * n_exp) + 1)
    cap = -(-capacity // 16) * 16
    half = width // 2
    part = expert_in.shape[2]
    zs = n_ea if (width // 8) % (8 * n_ea) == 0 else 1
    first = (HEADS // 6) * PAIR

    ea, gx, gy = (lax.axis_index(a) for a in ("ea", "gx", "gy"))
    near, far = 1 + gx, 2 - gx
    sc = jnp.stack([
        ea, gx, gy, gy ^ near, gy ^ far, gy ^ 3, gy, gy ^ far, gy ^ near, gy ^ 3,
        gy, gy ^ 1, gy ^ 2, gy ^ 3,
    ]).astype(jnp.int32)
    cross = [(0, 1), (1, 0)]
    perm_a = [(g * 4 + y, g * 4 + (y ^ (1 + g))) for g in range(2) for y in range(4)]
    perm_b = [(g * 4 + y, g * 4 + (y ^ (2 - g))) for g in range(2) for y in range(4)]

    def after(v, done):
        return lax.optimization_barrier((v, done))[0]

    def over_gx(v):
        return lax.ppermute(v, "gx", cross)

    def over_x(v):
        return lax.ppermute(v, "gy", [(y, y ^ 1) for y in range(4)])

    def over_y(v):
        return lax.ppermute(v, "gy", [(y, y ^ 2) for y in range(4)])

    def over_a(v):
        return lax.ppermute(v, ("gx", "gy"), perm_a)

    def over_b(v):
        return lax.ppermute(v, ("gx", "gy"), perm_b)

    def over_ea(v):
        return lax.all_to_all(v, "ea", 0, 0, tiled=True)

    def shift(v, d):
        return lax.ppermute(v, "ea", [(i, (i + d) % n_ea) for i in range(n_ea)])

    order = [1, 3, 2] if n_ea == 4 else list(range(1, n_ea))

    def dispatch(blocks):
        got = [blocks[0]] + [None] * (n_ea - 1)
        for d in order:
            got[d] = shift(blocks[d], d)
        return got

    own_w = jnp.stack([expert_in[0], jnp.concatenate([expert_out[0, :half], expert_out[0, half:]], axis=1)])
    x_w, y_w = over_x(own_w), over_y(own_w)

    lanes = -(-n_exp // 8) * 8
    block = shape((cap, width), bf16)
    w3 = w_qkv.transpose(1, 0, 2)
    row = lambda v: v
    slot_r, slot_c, g_pad, x_pad, qkv, attn_in, *g_sent = call(
        "route_project",
        functools.partial(prep_kernel, n_exp, cap),
        [
            shape((lanes, tp), f32), shape((tp, 128), f32), shape((tp, width), bf16),
            shape((tp, width), f32), shape((3, tp, width), bf16), shape((tp, width), bf16),
        ] + [block] * n_exp,
        (sc, routes.T, cotangent, tokens, row(norm1_gain), row(norm1_shift), w3, qv_bias),
        smem=1,
    )
    g_rows = dispatch(g_sent)
    res, ctx, moe_in, *m_sent = call(
        "attn_fwd",
        functools.partial(fwd_kernel, n_exp, cap),
        [shape((tp, width), f32), shape((tp, width), bf16), shape((tp, width), bf16)]
        + [block] * n_exp,
        (qkv, x_pad, w_proj, row(proj_bias), row(norm2_gain), row(norm2_shift), slot_r),
        flops=12_000_000_000,
    )
    x_w, y_w = after((x_w, y_w), moe_in)
    d_w = [over_x(y_w[0]), over_y(x_w[1])]
    m_rows = dispatch(after(tuple(m_sent), (tuple(g_rows), tuple(d_w))))
    mine = [after(own_w, moe_in), x_w, y_w, *d_w]
    weights = mine + [over_gx(v) for v in mine]

    router = jnp.pad(router_w.T, ((0, 128 - n_exp), (0, 0)))
    groups = [[0, 1], [3], [2]] if n_ea == 4 else [list(range(n_ea))]
    y_all, gm_back, local = None, [None] * n_ea, [None] * n_ea
    kept, in_bias_g, out_bias_g, router_g = [], 0.0, 0.0, 0.0
    for index, group in enumerate(groups):
        if index == 2:
            m_rows[group[0]] = after(m_rows[group[0]], gm_back[groups[0][-1]])
        y_all, gms, (hid, gp, gr, ib, ob, rg) = moe_rows(
            sc, group, [m_rows[d] for d in group], [g_rows[d] for d in group], weights,
            expert_in_bias, expert_out_bias, router, y_all, cap, n_exp,
        )
        kept.append((gr, hid, gp))
        in_bias_g, out_bias_g, router_g = in_bias_g + ib, out_bias_g + ob, router_g + rg
        for d, gm in zip(group, gms, strict=True):
            local[d] = gm
            if n_ea != 4 or index < 1:
                gm_back[d] = shift(gm, n_ea - d) if d else gm
    if n_ea == 4:
        for d in (3, 2):
            gm_back[d] = shift(after(local[d], local[2]), n_ea - d)
    partial = weight_grads(sc, [m_rows[d] for group in groups for d in group], kept, cap)

    def add(*parts):
        return functools.reduce(lambda a, b: a + b, [p.astype(f32) for p in parts]).astype(bf16)

    own_grads = lax.psum_scatter(
        partial.reshape(8, 2, half, part), ("gx", "gy"), scatter_dimension=0, tiled=False
    )
    in_w_grad, out_w_grad = call(
        "expert_grads",
        split_kernel,
        [shape((1, half, part), f32), shape((1, part, half), f32)],
        (own_grads,),
    )

    def sum_b(keep, got):
        return over_b(add(keep[2:], got[2:]))

    def sum_a(keep, got, got_b):
        return over_a(add(keep[1], got[1], got_b[1]))

    def sum_ea(slabs):
        return add(slabs[0], *[shift(slabs[d], d) for d in range(1, zs)]) if zs > 1 else slabs

    def all_ea(own):
        return jnp.stack([own] + [shift(own, d) for d in range(1, zs)]) if zs > 1 else lax.psum(own, "ea")

    gm_rows = gm_back
    n = width // (8 * zs)
    slabs = lambda l: [shape((4, zs, n, l), bf16)] * 2
    keep_one, send_one, grad_res, dctx, dqkv, small_one = call(
        "back_one",
        functools.partial(back_one_kernel, n_exp, cap, zs),
        slabs(3 * first + width) + [
            shape((tp, width), f32), shape((tp, width), bf16), shape((3, tp, first), bf16),
            shape((8, width), f32),
        ],
        (
            sc, after(slot_c, partial), res, row(norm2_gain), g_pad, ctx, w_proj, qkv, attn_in, *gm_rows,
        ),
        flops=400_000_000_000,
        scratch=[pltpu.VMEM((width, 3 * first + width), f32)],
        smem=1,
    )
    got_one = over_gx(send_one)
    rest = width - first
    columns = -(-(7 + 6 * n_exp) // 128) * 128
    keep_two, send_two, grad_tokens = call(
        "back_two",
        functools.partial(back_two_kernel, zs, n_exp),
        slabs(3 * rest + columns) + [shape((t, width), f32)],
        (
            sc, qkv, attn_in, dctx, dqkv, grad_res, w3, tokens, row(norm1_gain),
            small_one, router_g, in_bias_g.reshape(4, part), out_bias_g,
        ),
        scratch=[
            pltpu.VMEM((width, 3 * rest + columns), f32),
            pltpu.VMEM((3, tp, rest), bf16),
            pltpu.VMEM((tp, width), f32),
            pltpu.VMEM((columns, width), f32),
        ],
        smem=1,
    )
    y_rows = over_ea(after(y_all, m_rows[0]))
    got_two = over_gx(after(send_two, y_rows))
    got_one = after(got_one, grad_tokens)
    b_one = sum_b(keep_one, got_one)
    b_two = sum_b(keep_two, got_two)
    a_one = sum_a(keep_one, got_one, b_one)
    a_two = sum_a(keep_two, got_two, b_two)
    slabs_one = after(add(keep_one[0], got_one[0], b_one[0], a_one), b_two)
    own_one = after(sum_ea(slabs_one), a_two)
    own_two = sum_ea(add(keep_two[0], got_two[0], b_two[0], a_two))
    slabs_one = after(all_ea(own_one), (own_two, own_grads))
    slabs_two = all_ea(own_two)
    one = lax.all_gather(slabs_one, ("gx", "gy"), axis=0)
    two = lax.all_gather(slabs_two, ("gx", "gy"), axis=0)
    w_qkv_g, w_proj_g = unpack(sc, one, zs, n_exp, width, first)
    w_qkv_g, *vectors, qv_g, router_g, in_bias_g, out_bias_g = unpack(
        sc, two, zs, n_exp, width, rest, w_qkv_g
    )
    rolled = jnp.pad(
        lax.dynamic_slice_in_dim(jnp.concatenate([router_w.T, router_w.T]), ea, n_exp, 0),
        ((0, 128 - n_exp), (0, 0)),
    )
    output = call(
        "combine",
        functools.partial(out_kernel, n_exp, cap),
        shape((t, width), bf16),
        (sc, slot_c, moe_in, rolled, res, y_rows),
        scratch=[pltpu.VMEM((tp, width), f32), pltpu.VMEM((t, width), f32)],
        smem=1,
    )

    return (
        output,
        grad_tokens,
        vectors[0],
        vectors[1],
        w_qkv_g.transpose(1, 0, 2),
        qv_g,
        w_proj_g,
        vectors[4],
        vectors[2],
        vectors[3],
        router_g.T,
        in_w_grad,
        in_bias_g.reshape(1, 4 * part),
        out_w_grad,
        out_bias_g,
    )


def solution(mesh):
    tok = P(("ea", "gx", "gy"), None)
    in_specs = (
        tok, tok, tok, P(), P(), P(), P(), P(), P(), P(), P(), P(),
        P("ea", "gx", "gy"), P("ea", None), P("ea", "gy", "gx"), P("ea", None),
    )
    out_specs = (
        tok, tok, P(), P(), P(), P(), P(), P(), P(), P(), P(),
        P("ea", "gx", "gy"), P("ea", None), P("ea", "gy", "gx"), P("ea", None),
    )
    return jax.shard_map(per_device, mesh=mesh, in_specs=in_specs, out_specs=out_specs, check_vma=False)
```

```python
import functools
import math

import jax
import jax.numpy as jnp
from jax import lax
from jax.experimental import pallas as pl
from jax.experimental.pallas import tpu as pltpu
from jax.sharding import PartitionSpec as P

HEADS = 12
HD = 64
SEQ = 197
SEQ_PAD = 208
PAIR = 2 * HD
norm_eps = 1e-06

f32 = jnp.float32
bf16 = jnp.bfloat16
LAST = (((1,), (1,)), ((), ()))
FIRST = (((0,), (0,)), ((), ()))
K0 = math.sqrt(2.0 / math.pi)
C3 = 0.044715


def dot(a, b, dims=None):
    if dims is None:
        return jnp.dot(a, b, preferred_element_type=f32)
    return lax.dot_general(a, b, dims, preferred_element_type=f32)


def spec():
    return pl.BlockSpec(memory_space=pltpu.VMEM)


def call(name, kernel, out_shape, args, flops=1, scratch=(), smem=0):
    return pl.pallas_call(
        kernel,
        name=name,
        out_shape=out_shape,
        in_specs=[pl.BlockSpec(memory_space=pltpu.SMEM)] * smem
        + [spec()] * (len(args) - smem),
        out_specs=jax.tree.map(lambda _: spec(), out_shape),
        scratch_shapes=list(scratch),
        compiler_params=pltpu.CompilerParams(vmem_limit_bytes=60 * 1024 * 1024),
        cost_estimate=pl.CostEstimate(
            flops=flops, bytes_accessed=1, transcendentals=0
        ),
    )(*args)


def shape(dims, dtype):
    return jax.ShapeDtypeStruct(tuple(dims), dtype)


def norm_rows(values):
    centered = values - jnp.mean(values, axis=1, keepdims=True)
    inverse = lax.rsqrt(jnp.mean(centered * centered, axis=1, keepdims=True) + norm_eps)
    return centered * inverse, inverse


def norm_back(grad, normed, inverse, gain):
    scaled = grad * gain
    return inverse * (
        scaled
        - jnp.mean(scaled, axis=1, keepdims=True)
        - normed * jnp.mean(scaled * normed, axis=1, keepdims=True)
    )


def spread_images(dst, src, images):
    width = src.shape[1]
    for i in range(images):
        dst[i * SEQ_PAD : i * SEQ_PAD + SEQ, :] = src[i * SEQ : (i + 1) * SEQ, :]
        dst[i * SEQ_PAD + SEQ : (i + 1) * SEQ_PAD, :] = jnp.zeros((SEQ_PAD - SEQ, width), dst.dtype)


def pick_rows(slot_rows, d, cap):
    slots = lax.broadcasted_iota(jnp.int32, (cap, slot_rows.shape[1]), 0).astype(f32)
    return jnp.where(slots == slot_rows[d : d + 1, :], 1.0, 0.0).astype(bf16)


def pick_cols(slot_cols, d, cap):
    slots = lax.broadcasted_iota(jnp.int32, (slot_cols.shape[0], cap), 1).astype(f32)
    return jnp.where(slots == slot_cols[:, d : d + 1], 1.0, 0.0).astype(bf16)


def route_kernel(n_exp, cap, sc, routes, g_ref, slot_r, slot_c, g_pad, *refs):
    sent, wide = refs[:n_exp], refs[n_exp]
    t, tp = routes.shape[1], slot_r.shape[1]
    lanes = slot_r.shape[0]
    ids = lax.broadcasted_iota(jnp.int32, (lanes, t), 0) + sc[0]
    ids = jnp.where(ids >= n_exp, ids - n_exp, ids)
    real = lax.broadcasted_iota(jnp.int32, (lanes, t), 0) < n_exp
    chosen = ((routes[0:1, :] == ids) | (routes[1:2, :] == ids)) & real
    ti = lax.broadcasted_iota(jnp.int32, (t, tp), 0)
    tj = lax.broadcasted_iota(jnp.int32, (t, tp), 1)
    moved = jnp.where(ti + (ti // SEQ) * (SEQ_PAD - SEQ) == tj, 1.0, 0.0).astype(bf16)
    chosen = dot(jnp.where(chosen, 1.0, 0.0).astype(bf16), moved)
    ti = lax.broadcasted_iota(jnp.int32, (tp, tp), 0)
    tj = lax.broadcasted_iota(jnp.int32, (tp, tp), 1)
    before = jnp.where(ti < tj, 1.0, 0.0).astype(bf16)
    slots = jnp.where(chosen > 0.5, dot(chosen.astype(bf16), before), -1.0)
    slot_r[...] = slots
    slot_c[...] = jnp.full(slot_c.shape, -1.0, f32)
    slot_c[:, :lanes] = slots.T
    spread_images(wide, g_ref[...].astype(f32), tp // SEQ_PAD)
    g_pad[...] = wide[...].astype(bf16)
    rows = slot_r[...]
    for d in range(n_exp):
        sent[d][...] = dot(pick_rows(rows, d, cap), g_pad[...]).astype(bf16)


def project_kernel(x_ref, gain1, shift1, w3, qvb, wide, qkv, attn_in):
    spread_images(wide, x_ref[...].astype(f32), wide.shape[0] // SEQ_PAD)
    normed, _ = norm_rows(wide[...])
    attn_in[...] = (normed * gain1[...].reshape(1, -1) + shift1[...].reshape(1, -1)).astype(bf16)
    a = attn_in[...]
    qkv[0] = ((dot(a, w3[0]) + qvb[0:1, :]).astype(bf16).astype(f32) * (HD**-0.5)).astype(bf16)
    qkv[1] = dot(a, w3[1]).astype(bf16)
    qkv[2] = (dot(a, w3[2]) + qvb[1:2, :]).astype(bf16)


def head_masks(rows):
    lane = lax.broadcasted_iota(jnp.int32, (rows, PAIR), 1)
    return lane < HD


def attn_probs(q_head, k_pair):
    scores = dot(q_head, k_pair, LAST)
    keys = lax.broadcasted_iota(jnp.int32, scores.shape, 1)
    scores = jnp.where(keys < SEQ, scores, -1e30)
    powered = jnp.exp(scores - jnp.max(scores, axis=1, keepdims=True))
    return powered * (1.0 / jnp.sum(powered, axis=1, keepdims=True))


def fwd_kernel(n_exp, cap, qkv, wide, wp, pb, gain2, shift2, slot_r, res, ctx, moe_in, *sent):
    tp, width = res.shape
    images = tp // SEQ_PAD
    low = head_masks(SEQ_PAD)
    pairs = width // PAIR

    def pair_step(step, carry):
        img, pair = step // pairs, lax.rem(step, pairs)
        rows = pl.ds(pl.multiple_of(img * SEQ_PAD, 16), SEQ_PAD)
        cols = pl.ds(pl.multiple_of(pair * PAIR, PAIR), PAIR)
        q, k, v = qkv[0, rows, cols], qkv[1, rows, cols], qkv[2, rows, cols]
        zero = jnp.zeros_like(q)
        p0 = attn_probs(jnp.where(low, q, zero), k).astype(bf16)
        p1 = attn_probs(jnp.where(low, zero, q), k).astype(bf16)
        ctx[rows, cols] = jnp.where(low, dot(p0, v), dot(p1, v)).astype(bf16)
        return carry

    lax.fori_loop(0, images * pairs, pair_step, 0, unroll=2)
    res[...] = wide[...] + dot(ctx[...], wp[...]) + pb[...].reshape(1, -1)
    normed, _ = norm_rows(res[...])
    moe_in[...] = (normed * gain2[...].reshape(1, -1) + shift2[...].reshape(1, -1)).astype(bf16)
    rows = slot_r[...]
    for d in range(n_exp):
        sent[d][...] = dot(pick_rows(rows, d, cap), moe_in[...]).astype(bf16)


def moe_kernel(nb, cap, n_exp, hc, sc, *refs):
    rows_in, g_in = refs[:nb], refs[nb : 2 * nb]
    mine, other = refs[2 * nb : 2 * nb + 5], refs[2 * nb + 5 : 2 * nb + 7]
    r = 2 * nb + 7
    in_bias, out_bias, router = refs[r : r + 3]
    r += 3
    y_out, gm_out = refs[r : r + nb], refs[r + nb : r + 2 * nb]
    r += 2 * nb
    hid, gp_out, gr, in_b, out_b, router_g = refs[r : r + 6]
    r += 6
    x, gf, wi, wo, acc_y, acc_g, probs_s, sems = refs[r:]
    c = pl.program_id(0)
    width = x.shape[1]
    half = width // 2
    part = wi.shape[2]

    def copies(i):
        gx = sc[1]
        near = pl.ds(pl.multiple_of(gx * half, half), half)
        far = pl.ds(pl.multiple_of((1 - gx) * half, half), half)
        found = []
        if i < 3:
            halves = (mine[i].at[0], mine[i].at[1]), (other[0].at[i, 0], other[0].at[i, 1])
        else:
            halves = (mine[3], mine[4]), (other[1].at[0], other[1].at[1])
        for k, ((first, second), cols) in enumerate(zip(halves, (near, far), strict=True)):
            found.append(pltpu.make_async_copy(first, wi.at[i, cols, :], sems.at[6 * i + 3 * k]))
            for u in range(2):
                found.append(
                    pltpu.make_async_copy(
                        second.at[:, u * half : (u + 1) * half],
                        wo.at[i, u * half : (u + 1) * half, cols],
                        sems.at[6 * i + 3 * k + 1 + u],
                    )
                )
        return found

    @pl.when(c == 0)
    def _():
        for i in range(4):
            for one in copies(i):
                one.start()
        for b in range(nb):
            x[b * cap : (b + 1) * cap, :] = rows_in[b][...]
            gf[b * cap : (b + 1) * cap, :] = g_in[b][...]
        logits = dot(x[...], router[...], LAST)
        lane = lax.broadcasted_iota(jnp.int32, logits.shape, 1)
        logits = jnp.where(lane < n_exp, logits, -1e30)
        powered = jnp.exp(logits - jnp.max(logits, axis=1, keepdims=True))
        probs = powered / jnp.sum(powered, axis=1, keepdims=True)
        probs_s[...] = probs
        gate = jnp.sum(jnp.where(lane == sc[0], probs, 0.0), axis=1, keepdims=True)
        rows_g = (gate * gf[...].astype(f32)).astype(bf16)
        gr[...] = rows_g
        out_b[...] = jnp.sum(rows_g.astype(f32), axis=0, keepdims=True)
        acc_y[...] = jnp.zeros_like(acc_y)
        acc_g[...] = jnp.zeros_like(acc_g)

    for i in range(4):

        @pl.when(c == i)
        def _():
            for one in copies(i):
                one.wait()

    def step(s, carry):
        cols = pl.ds(pl.multiple_of(s * hc, hc), hc)
        w_in = wi[c, :, cols]
        w_out = wo[c, cols, :]
        pre = dot(x[...], w_in) + in_bias[:, cols]
        gh = dot(gr[...], w_out, LAST)
        sq = pre * pre
        h = 0.5 + 0.5 * jnp.tanh(pre * (K0 + (K0 * C3) * sq))
        low_hidden = (pre * h).astype(bf16)
        hid[:, cols] = low_hidden
        acc_y[...] += dot(low_hidden, w_out)
        slope = h + (h - h * h) * (pre * (2.0 * K0 + (6.0 * C3 * K0) * sq))
        gp = gh * slope
        in_b[:, cols] = jnp.sum(gp, axis=0, keepdims=True)
        gp = gp.astype(bf16)
        gp_out[:, cols] = gp
        acc_g[...] += dot(gp, w_in, LAST)
        return carry

    lax.fori_loop(0, part // hc, step, 0)

    @pl.when(c == 3)
    def _():
        y = (acc_y[...] + out_bias[...]).astype(bf16)
        grad_gate = jnp.sum(gf[...].astype(f32) * y.astype(f32), axis=1, keepdims=True)
        probs = probs_s[...]
        lane = lax.broadcasted_iota(jnp.int32, probs.shape, 1)
        own = jnp.where(lane == sc[0], 1.0, 0.0)
        gate = jnp.sum(own * probs, axis=1, keepdims=True)
        grad_logits = ((grad_gate * gate) * (own - probs)).astype(bf16)
        gm = (acc_g[...] + dot(grad_logits, router[...])).astype(bf16)
        router_g[...] = dot(grad_logits, x[...], FIRST)[: router_g.shape[0], :]
        for b in range(nb):
            y_out[b][...] = y[b * cap : (b + 1) * cap, :]
            gm_out[b][...] = gm[b * cap : (b + 1) * cap, :]


def moe_rows(sc, rows, grads, weights, in_bias, out_bias, router, cap, n_exp, flops):
    nb = len(rows)
    nr = nb * cap
    width = rows[0].shape[1]
    part = weights[0].shape[2]
    hidden = 4 * part
    lanes = -(-n_exp // 8) * 8
    hc = part
    whole = lambda dims: pl.BlockSpec(dims, lambda c, sc: (0,) * len(dims))
    grid_spec = pltpu.PrefetchScalarGridSpec(
        num_scalar_prefetch=1,
        grid=(4,),
        in_specs=[whole((cap, width))] * (2 * nb)
        + [pl.BlockSpec(memory_space=pl.ANY)] * 7
        + [
            pl.BlockSpec((1, part), lambda c, sc: (0, sc[10 + c])),
            whole((1, width)),
            whole((128, width)),
        ],
        out_specs=[whole((cap, width))] * (2 * nb)
        + [
            pl.BlockSpec((nr, part), lambda c, sc: (0, c)),
            pl.BlockSpec((nr, part), lambda c, sc: (0, c)),
            whole((nr, width)),
            pl.BlockSpec((1, part), lambda c, sc: (0, sc[10 + c])),
            whole((1, width)),
            whole((lanes, width)),
        ],
        scratch_shapes=[
            pltpu.VMEM((nr, width), bf16),
            pltpu.VMEM((nr, width), bf16),
            pltpu.VMEM((4, width, part), bf16),
            pltpu.VMEM((4, part, width), bf16),
            pltpu.VMEM((nr, width), f32),
            pltpu.VMEM((nr, width), f32),
            pltpu.VMEM((nr, 128), f32),
            pltpu.SemaphoreType.DMA((24,)),
        ],
    )
    out = pl.pallas_call(
        functools.partial(moe_kernel, nb, cap, n_exp, hc),
        name="expert_rows",
        grid_spec=grid_spec,
        out_shape=[shape((cap, width), bf16)] * (2 * nb)
        + [
            shape((nr, hidden), bf16),
            shape((nr, hidden), bf16),
            shape((nr, width), bf16),
            shape((1, hidden), f32),
            shape((1, width), f32),
            shape((lanes, width), f32),
        ],
        compiler_params=pltpu.CompilerParams(vmem_limit_bytes=60 * 1024 * 1024),
        cost_estimate=pl.CostEstimate(flops=flops, bytes_accessed=1, transcendentals=0),
    )(sc, *rows, *grads, *weights, in_bias, out_bias, router)
    return out[:nb], out[nb : 2 * nb], out[2 * nb :]


def weight_kernel(nb, cap, counts, sc, *refs):
    rows, gr, hid, gp = (
        refs[:nb],
        refs[nb : nb + len(counts)],
        refs[nb + len(counts) : nb + 2 * len(counts)],
        refs[nb + 2 * len(counts) : nb + 3 * len(counts)],
    )
    keep, send, xt, gt, cat = refs[nb + 3 * len(counts) :]
    c = pl.program_id(0)
    width = xt.shape[0]
    half = width // 2

    def gather(parts):
        at = 0
        for one in parts:
            cat[at : at + one.shape[0], :] = one[...]
            at += one.shape[0]

    @pl.when(c == 0)
    def _():
        near = pl.ds(pl.multiple_of(sc[1] * half, half), half)
        far = pl.ds(pl.multiple_of((1 - sc[1]) * half, half), half)
        for source, turned in ((rows, xt), (gr, gt)):
            gather(source)
            turned[:half, :] = cat[:, near].T
            turned[half:, :] = cat[:, far].T

    for j, (turned, source) in enumerate(((xt, gp), (gt, hid))):
        gather(source)
        both = dot(turned[...], cat[...]).astype(bf16)
        keep[0, j] = both[:half, :]
        send[0, j] = both[half:, :]


def split_kernel(own, got, from_x, from_y, first, second):
    total = [own[i].astype(f32) + got[i].astype(f32) + from_x[i].astype(f32) + from_y[i].astype(f32) for i in (0, 1)]
    first[0] = total[0]
    second[0] = total[1].T


def weight_grads(sc, rows, groups, cap):
    nb = len(rows)
    width = rows[0].shape[1]
    hidden = groups[0][1].shape[1]
    part = hidden // 4
    counts = [g[0].shape[0] for g in groups]
    total = nb * cap
    whole = lambda dims: pl.BlockSpec(dims, lambda c, sc: (0,) * len(dims))
    block = (1, 2, width // 2, part)
    grid_spec = pltpu.PrefetchScalarGridSpec(
        num_scalar_prefetch=1,
        grid=(4,),
        in_specs=[whole((cap, width))] * nb
        + [whole((n, width)) for n in counts]
        + [pl.BlockSpec((n, part), lambda c, sc: (0, c)) for n in counts] * 2,
        out_specs=[pl.BlockSpec(block, lambda c, sc: (c, 0, 0, 0))] * 2,
        scratch_shapes=[
            pltpu.VMEM((width, total), bf16),
            pltpu.VMEM((width, total), bf16),
            pltpu.VMEM((total, width), bf16),
        ],
    )
    return pl.pallas_call(
        functools.partial(weight_kernel, nb, cap, counts),
        name="expert_weights",
        grid_spec=grid_spec,
        out_shape=[shape((4, 2, width // 2, part), bf16)] * 2,
        compiler_params=pltpu.CompilerParams(vmem_limit_bytes=60 * 1024 * 1024),
        cost_estimate=pl.CostEstimate(
            flops=1, bytes_accessed=1, transcendentals=0
        ),
    )(sc, *rows, *[g[0] for g in groups], *[g[1] for g in groups], *[g[2] for g in groups])


def attn_back(qkv, dctx, dqkv, pair_range, low, images):
    lo, hi = pair_range
    pairs = hi - lo

    def pair_step(step, carry):
        img, pair = step // pairs, lax.rem(step, pairs)
        rows = pl.ds(pl.multiple_of(img * SEQ_PAD, 16), SEQ_PAD)
        cols = pl.ds(pl.multiple_of((pair + lo) * PAIR, PAIR), PAIR)
        local = pl.ds(pl.multiple_of(pair * PAIR, PAIR), PAIR)
        q, k, v, gc = qkv[0, rows, cols], qkv[1, rows, cols], qkv[2, rows, cols], dctx[rows, cols]
        zero = jnp.zeros_like(q)
        outs = []
        for first in (True, False):
            mine = lambda t: jnp.where(low, t, zero) if first else jnp.where(low, zero, t)
            probs = attn_probs(mine(q), k)
            grad_p = dot(mine(gc), v, LAST)
            mean = jnp.sum(grad_p * probs, axis=1, keepdims=True)
            ds = (probs * (grad_p - mean)).astype(bf16)
            outs.append((dot(ds, k), dot(ds, q, FIRST), dot(probs.astype(bf16), gc, FIRST)))
        join = [jnp.where(low, a, b) for a, b in zip(*outs, strict=True)]
        dqkv[0, rows, local] = (join[0] * (HD**-0.5)).astype(bf16)
        dqkv[1, rows, local] = join[1].astype(bf16)
        dqkv[2, rows, local] = join[2].astype(bf16)
        return carry

    lax.fori_loop(0, images * pairs, pair_step, 0, unroll=2)


def store_slabs(sc, full, keep, send, zs):
    n = keep.shape[2]
    for i in range(4):
        for d in range(zs):
            z = lax.rem(sc[0] + d, zs) if zs > 1 else 0
            base = sc[2 + i] * (n * zs) + z * n
            near = pl.multiple_of(sc[1] * (n * zs * 4) + base, 8)
            keep[i, d] = full[pl.ds(near, n), :].astype(bf16)
            base = sc[6 + i] * (n * zs) + z * n
            far = pl.multiple_of((1 - sc[1]) * (n * zs * 4) + base, 8)
            send[i, d] = full[pl.ds(far, n), :].astype(bf16)


def gather_kernel(cap, slot_c, *refs):
    gm_in, part = refs[:-1], refs[-1]
    cols = slot_c[...]
    total = dot(pick_cols(cols, 0, cap), gm_in[0][...])
    for d in range(1, len(gm_in)):
        total += dot(pick_cols(cols, d, cap), gm_in[d][...])
    part[...] = total


def norm_two_kernel(n_exp, cap, slot_c, res, gain2, g_pad, part, gm_last, grad_res, small):
    grad_moe = part[...] + dot(pick_cols(slot_c[...], n_exp - 1, cap), gm_last[...])
    normed, inverse = norm_rows(res[...])
    grad_res[...] = g_pad[...].astype(f32) + norm_back(grad_moe, normed, inverse, gain2[...].reshape(1, -1))
    small[0:1, :] = jnp.sum(grad_moe * normed, axis=0, keepdims=True)
    small[1:2, :] = jnp.sum(grad_moe, axis=0, keepdims=True)
    small[2:3, :] = jnp.sum(grad_res[...], axis=0, keepdims=True)


def back_one_kernel(zs, sc, grad_res, ctx, wp, qkv, attn_in, keep, send, dctx, dqkv, small, full):
    tp = grad_res.shape[0]
    images = tp // SEQ_PAD
    mix = grad_res[...].astype(bf16)
    part = dqkv.shape[2]
    full[:, 3 * part :] = dot(ctx[...], mix, FIRST)
    dctx[...] = dot(mix, wp[...], LAST).astype(bf16)
    attn_back(qkv, dctx, dqkv, (0, part // PAIR), head_masks(SEQ_PAD), images)
    a = attn_in[...]
    for i in range(3):
        full[:, i * part : (i + 1) * part] = dot(a, dqkv[i], FIRST)
    store_slabs(sc, full, keep, send, zs)
    small[0:1, :] = jnp.sum(dqkv[0].astype(f32), axis=0, keepdims=True)
    small[1:2, :] = jnp.sum(dqkv[2].astype(f32), axis=0, keepdims=True)


def back_two_kernel(
    zs, n_exp, sc, qkv, attn_in, dctx, done, grad_res, w3, x_ref, gain1, small_two, small_one, router_g, in_b, out_b,
    keep, send, grad_tokens, full, dqkv, wide, small,
):
    tp, width = grad_res.shape
    images = tp // SEQ_PAD
    part = done.shape[2]
    rest = width - part
    attn_back(qkv, dctx, dqkv, (part // PAIR, width // PAIR), head_masks(SEQ_PAD), images)
    a = attn_in[...]
    for i in range(3):
        full[:, i * rest : (i + 1) * rest] = dot(a, dqkv[i], FIRST)
    small[...] = jnp.zeros_like(small)
    small[2:5, :] = small_two[0:3, :]
    for i in (0, 2):
        row = 5 + i // 2
        small[row : row + 1, :part] = small_one[i // 2 : 1 + i // 2, :]
        small[row : row + 1, part:] = jnp.sum(dqkv[i].astype(f32), axis=0, keepdims=True)
    small[7 : 7 + n_exp, :] = router_g[:n_exp, :]
    for k in range(4):
        small[pl.ds(7 + n_exp + 4 * sc[0] + k, 1), :] = in_b[k : k + 1, :]
    small[pl.ds(7 + 5 * n_exp + sc[0], 1), :] = out_b[...]
    grad_in = dot(done[0], w3[0, :, :part], LAST) + dot(dqkv[0], w3[0, :, part:], LAST)
    for i in (1, 2):
        grad_in += dot(done[i], w3[i, :, :part], LAST) + dot(dqkv[i], w3[i, :, part:], LAST)
    spread_images(wide, x_ref[...].astype(f32), images)
    normed, inverse = norm_rows(wide[...])
    small[0:1, :] = jnp.sum(grad_in * normed, axis=0, keepdims=True)
    small[1:2, :] = jnp.sum(grad_in, axis=0, keepdims=True)
    full[:, 3 * rest :] = small[...].T
    store_slabs(sc, full, keep, send, zs)
    wide[...] = grad_res[...] + norm_back(grad_in, normed, inverse, gain1[...].reshape(1, -1))
    for i in range(images):
        grad_tokens[i * SEQ : (i + 1) * SEQ, :] = wide[i * SEQ_PAD : i * SEQ_PAD + SEQ, :]


def out_kernel(n_exp, cap, slot_c, moe_in, router, res, *refs):
    y_in, (out, wide, tight) = refs[:n_exp], refs[n_exp:]
    cols = slot_c[...]
    logits = dot(moe_in[...], router[...], LAST)
    lane = lax.broadcasted_iota(jnp.int32, logits.shape, 1)
    logits = jnp.where(lane < n_exp, logits, -1e30)
    powered = jnp.exp(logits - jnp.max(logits, axis=1, keepdims=True))
    probs = powered / jnp.sum(powered, axis=1, keepdims=True)
    total = res[...]
    for d in range(n_exp):
        total += probs[:, d : d + 1] * dot(pick_cols(cols, d, cap), y_in[d][...])
    wide[...] = total
    for i in range(res.shape[0] // SEQ_PAD):
        tight[i * SEQ : (i + 1) * SEQ, :] = wide[i * SEQ_PAD : i * SEQ_PAD + SEQ, :]
    out[...] = tight[...].astype(bf16)


def unpack_kernel(zs, n_exp, lanes, last, sc, *refs):
    parts, refs = refs[:4], refs[4:]
    if last:
        _, w_out, *vectors, qv_g, router_g, in_b, out_b, w_qkv, sems, held, turned_s = refs
    else:
        w_out, held, w_qkv, sems = refs
    n = parts[0].shape[2]
    start = w_out.shape[2] - lanes if last else 0

    def places():
        for q in range(2):
            for i in range(4):
                j = i if q == 0 else (0, 2, 1, 3)[i]
                place = (sc[1] if q == 0 else 1 - sc[1]) * 4 + sc[2 + i]
                for d in range(zs):
                    z = lax.rem(sc[0] - d + zs, zs) if zs > 1 else 0
                    yield parts[2 * q + j // 2].at[j % 2, d], pl.ds(pl.multiple_of((place * zs + z) * n, 8), n)

    copies = []
    for p in range(3):
        for ref, rows in places():
            w_qkv[p, rows, :] = ref[:, p * lanes : (p + 1) * lanes].astype(f32)
        one = pltpu.make_async_copy(w_qkv.at[p], w_out.at[p, :, start : start + lanes], sems.at[p])
        one.start()
        copies.append(one)
    for ref, rows in places():
        held[rows, :] = ref[:, 3 * lanes :].astype(f32)
    if last:
        turned = held[...].T
        for i, vector in enumerate(vectors):
            vector[...] = turned[i : i + 1, :].reshape(-1)
        qv_g[...] = turned[5:7, :]
        router_g[...] = turned[7 : 7 + n_exp, :]
        turned_s[...] = turned
        for k in range(4):
            in_b[:, k * turned.shape[1] : (k + 1) * turned.shape[1]] = turned_s[pl.ds(7 + n_exp + 4 * sc[0] + k, 1), :]
        out_b[...] = turned_s[pl.ds(7 + 5 * n_exp + sc[0], 1), :]
    for one in copies:
        one.wait()


def unpack(sc, slabs, zs, n_exp, width, lanes, base=None):
    last = base is not None
    extra = slabs[0].shape[-1] - 3 * lanes
    whole = lambda dims: pl.BlockSpec(dims, lambda c, sc: (0,) * len(dims))
    more = [(width,)] * 5 + [(2, width), (n_exp, width), (1, 4 * width), (1, width)] if last else [(width, extra)]
    return pl.pallas_call(
        functools.partial(unpack_kernel, zs, n_exp, lanes, last),
        name="unpack",
        grid_spec=pltpu.PrefetchScalarGridSpec(
            num_scalar_prefetch=1,
            grid=(1,),
            in_specs=[whole(v.shape) for v in slabs] + ([pl.BlockSpec(memory_space=pl.ANY)] if last else []),
            out_specs=[
                pl.BlockSpec(memory_space=pl.ANY),
                *[whole(dims) for dims in more],
            ],
            scratch_shapes=[pltpu.VMEM((3, width, lanes), f32), pltpu.SemaphoreType.DMA((3,))]
            + ([pltpu.VMEM((width, extra), f32), pltpu.VMEM((extra, width), f32)] if last else []),
        ),
        out_shape=[shape((3, width, width), f32)] + [shape(dims, f32) for dims in more],
        input_output_aliases={5: 0} if last else {},
        compiler_params=pltpu.CompilerParams(vmem_limit_bytes=60 * 1024 * 1024),
        cost_estimate=pl.CostEstimate(flops=1, bytes_accessed=1, transcendentals=0),
    )(sc, *slabs, *([base] if last else []))


def per_device(
    tokens, routes, cotangent, norm1_gain, norm1_shift, w_qkv, qv_bias, w_proj, proj_bias,
    norm2_gain, norm2_shift, router_w, expert_in, expert_in_bias, expert_out, expert_out_bias,
):
    n_ea, n_gx, n_gy = (lax.axis_size(a) for a in ("ea", "gx", "gy"))
    n_exp = expert_in.shape[0] * n_ea
    assert expert_in.shape[0] == 1 and n_gx == 2 and n_gy == 4
    t, width = tokens.shape
    images = t // SEQ
    tp = images * SEQ_PAD
    capacity = max(2, 8 * t // (3 * n_exp) + 1)
    cap = -(-capacity // 16) * 16
    half = width // 2
    part = expert_in.shape[2]
    zs = n_ea if (width // 8) % (8 * n_ea) == 0 else 1
    first = (HEADS // 6) * PAIR

    ea, gx, gy = (lax.axis_index(a) for a in ("ea", "gx", "gy"))
    near, far = 1 + gx, 2 - gx
    sc = jnp.stack([
        ea, gx, gy, gy ^ near, gy ^ far, gy ^ 3, gy, gy ^ far, gy ^ near, gy ^ 3,
        gy, gy ^ 1, gy ^ 2, gy ^ 3,
    ]).astype(jnp.int32)
    cross = [(0, 1), (1, 0)]
    perm_a = [(g * 4 + y, g * 4 + (y ^ (1 + g))) for g in range(2) for y in range(4)]
    perm_b = [(g * 4 + y, g * 4 + (y ^ (2 - g))) for g in range(2) for y in range(4)]

    def after(v, done):
        return lax.optimization_barrier((v, done))[0]

    def over_gx(v):
        return lax.ppermute(v, "gx", cross)

    def over_x(v):
        return lax.ppermute(v, "gy", [(y, y ^ 1) for y in range(4)])

    def over_y(v):
        return lax.ppermute(v, "gy", [(y, y ^ 2) for y in range(4)])

    def over_a(v):
        return lax.ppermute(v, ("gx", "gy"), perm_a)

    def over_b(v):
        return lax.ppermute(v, ("gx", "gy"), perm_b)

    def over_ea(v):
        return lax.all_to_all(v, "ea", 0, 0, tiled=True)

    def shift(v, d):
        return lax.ppermute(v, "ea", [(i, (i + d) % n_ea) for i in range(n_ea)])

    order = list(range(1, n_ea))

    def dispatch(blocks):
        got = [blocks[0]] + [None] * (n_ea - 1)
        for d in order:
            got[d] = shift(blocks[d], d)
        return got

    own_w = jnp.stack([expert_in[0], jnp.concatenate([expert_out[0, :half], expert_out[0, half:]], axis=1)])
    x_w, y_w = over_x(own_w), over_y(own_w)

    lanes = -(-n_exp // 8) * 8
    block = shape((cap, width), bf16)
    w3 = w_qkv.transpose(1, 0, 2)
    slot_r, slot_c, g_pad, *g_sent = call(
        "route",
        functools.partial(route_kernel, n_exp, cap),
        [shape((lanes, tp), f32), shape((tp, 128), f32), shape((tp, width), bf16)] + [block] * n_exp,
        (sc, routes.T, cotangent),
        scratch=[pltpu.VMEM((tp, width), f32)],
        smem=1,
    )
    g_rows = dispatch(g_sent)
    x_pad, qkv, attn_in = call(
        "project",
        project_kernel,
        [shape((tp, width), f32), shape((3, tp, width), bf16), shape((tp, width), bf16)],
        (tokens, norm1_gain, norm1_shift, w3, qv_bias),
    )
    res, ctx, moe_in, *m_sent = call(
        "attn_fwd",
        functools.partial(fwd_kernel, n_exp, cap),
        [shape((tp, width), f32), shape((tp, width), bf16), shape((tp, width), bf16)]
        + [block] * n_exp,
        (qkv, x_pad, w_proj, proj_bias, norm2_gain, norm2_shift, slot_r),
        flops=12_000_000_000,
    )
    own_l, x_w, y_w, *m_sent = after((own_w, x_w, y_w, *m_sent), (moe_in, tuple(g_rows)))
    d_w = [over_x(y_w[0]), over_y(x_w[1])]
    m_rows = dispatch(m_sent)
    other_d = over_gx(jnp.stack(after(tuple(d_w), m_rows[1])))
    weights = [own_l, x_w, y_w, *d_w, over_gx(jnp.stack([own_l, x_w, y_w])), other_d]

    router = jnp.pad(router_w.T, ((0, 128 - n_exp), (0, 0)))
    groups = [[d] for d in range(4)] if n_ea == 4 else [list(range(n_ea))]
    y_local, gm_local, gm_back = [None] * n_ea, [None] * n_ea, [None] * n_ea
    kept, in_bias_g, out_bias_g, router_g = [], 0.0, 0.0, 0.0
    for index, group in enumerate(groups):
        if index == 1:
            m_rows[1] = after(m_rows[1], gm_local[0])
        if index == 3:
            m_rows[3] = after(m_rows[3], gm_back[1])
        ys, gms, (hid, gp, gr, ib, ob, rg) = moe_rows(
            sc, [m_rows[d] for d in group], [g_rows[d] for d in group], weights,
            expert_in_bias, expert_out_bias, router, cap, n_exp, 12_000_000_000 if index > 1 else 1,
        )
        kept.append((gr, hid, gp))
        in_bias_g, out_bias_g, router_g = in_bias_g + ib, out_bias_g + ob, router_g + rg
        for d, y, gm in zip(group, ys, gms, strict=True):
            y_local[d], gm_local[d] = y, gm
            gm_back[d] = shift(gm, n_ea - d) if d else gm
    rows_all = [m_rows[d] for group in groups for d in group]
    keep, send = weight_grads(sc, rows_all, kept, cap)

    def add(*parts):
        return functools.reduce(lambda a, b: a + b, [p.astype(f32) for p in parts]).astype(bf16)

    def sum_b(keep, got):
        return over_b(add(keep[2:], got[2:]))

    def sum_a(keep, got, got_b):
        return over_a(add(keep[1], got[1], got_b[1]))

    def shifts(parts):
        return [shift(v, d) for d, v in enumerate(parts, 1)]

    gathered = call(
        "gather_rows",
        functools.partial(gather_kernel, cap),
        shape((tp, width), f32),
        (slot_c, *gm_back[:-1]),
        flops=4_000_000_000,
    )
    send, slot_l, gathered, gm_last = after((send, slot_c, gathered, gm_back[-1]), keep)
    got = over_gx(send)
    grad_res, small_two = call(
        "norm_two",
        functools.partial(norm_two_kernel, n_exp, cap),
        [shape((tp, width), f32), shape((8, width), f32)],
        (slot_l, res, norm2_gain, g_pad, gathered, gm_last),
    )
    back = list(range(1, n_ea))
    got, grad_res, *y_local = after((got, grad_res, *y_local), small_two)
    got_x = over_x(add(keep[3, 0], got[3, 0]))
    got_y = over_y(add(keep[3, 1], got[3, 1]))
    y_rows = {1: shift(y_local[1], n_ea - 1)}
    n = width // (8 * zs)
    slabs = lambda l: [shape((4, zs, n, l), bf16)] * 2
    keep_one, send_one, dctx, dqkv, small_one = call(
        "back_one",
        functools.partial(back_one_kernel, zs),
        slabs(3 * first + width) + [
            shape((tp, width), bf16), shape((3, tp, first), bf16), shape((2, first), f32),
        ],
        (sc, grad_res, ctx, w_proj, qkv, attn_in),
        flops=12_000_000_000,
        scratch=[pltpu.VMEM((width, 3 * first + width), f32)],
        smem=1,
    )
    got_x, got_y, send_one, dctx, y_rows[1], *y_later = after(
        (got_x, got_y, send_one, dctx, y_rows[1], *y_local[2:]), small_one
    )
    y_rows[2] = shift(y_later[0], n_ea - 2)
    from_x = over_x(jnp.stack([add(keep[1, 0], got[1, 0]), add(keep[1, 1], got[1, 1], got_y)]))
    from_y = over_y(jnp.stack([add(keep[2, 0], got[2, 0], got_x), add(keep[2, 1], got[2, 1])]))
    got_one = over_gx(send_one)
    rest = width - first
    columns = -(-(7 + 6 * n_exp) // 128) * 128
    keep_two, send_two, grad_tokens = call(
        "back_two",
        functools.partial(back_two_kernel, zs, n_exp),
        slabs(3 * rest + columns) + [shape((t, width), f32)],
        (
            sc, qkv, attn_in, dctx, dqkv, grad_res, w3, tokens, norm1_gain,
            small_two, small_one, router_g, in_bias_g.reshape(4, part), out_bias_g,
        ),
        flops=30_000_000_000,
        scratch=[
            pltpu.VMEM((width, 3 * rest + columns), f32),
            pltpu.VMEM((3, tp, rest), bf16),
            pltpu.VMEM((tp, width), f32),
            pltpu.VMEM((columns, width), f32),
        ],
        smem=1,
    )
    got_one, send_two, from_x, from_y, y_rows[2], *y_later = after(
        (got_one, send_two, from_x, from_y, y_rows[2], *y_later[1:]), grad_tokens
    )
    y_rows.update({d: shift(y, n_ea - d) for d, y in enumerate(y_later, 3)})
    got_two = over_gx(send_two)
    b_one = sum_b(keep_one, got_one)
    b_one, got_two = after((b_one, got_two), keep_two)
    a_one = sum_a(keep_one, got_one, b_one)
    b_two = sum_b(keep_two, got_two)
    in_w_grad, out_w_grad = call(
        "expert_grads",
        split_kernel,
        [shape((1, half, part), f32), shape((1, part, half), f32)],
        (keep[0], got[0], from_x, from_y),
    )
    a_one, b_two, in_w_grad, out_w_grad, y_late = after(
        (a_one, b_two, in_w_grad, out_w_grad, tuple(y_rows[d] for d in back)), got_two
    )
    rolled = jnp.pad(
        lax.dynamic_slice_in_dim(jnp.concatenate([router_w.T, router_w.T]), ea, n_exp, 0),
        ((0, 128 - n_exp), (0, 0)),
    )
    output = call(
        "combine",
        functools.partial(out_kernel, n_exp, cap),
        shape((t, width), bf16),
        (slot_c, moe_in, rolled, res, y_local[0], *y_late),
        scratch=[pltpu.VMEM((tp, width), f32), pltpu.VMEM((t, width), f32)],
    )
    slabs_one = [add(keep_one[0, d], got_one[0, d], b_one[0, d], a_one[d]) for d in range(zs)]
    a_two = sum_a(keep_two, got_two, b_two)
    if zs > 1:
        z_one = shifts(slabs_one[1:])
        z_one, a_two = after((z_one, a_two), b_two)
        own_one = add(slabs_one[0], *z_one)
        slabs_two = [add(keep_two[0, d], got_two[0, d], b_two[0, d], a_two[d]) for d in range(zs)]
        g_one = shifts([own_one] * (zs - 1))
        z_two = shifts(slabs_two[1:])
        g_one, z_two, output = after((g_one, z_two, output), a_two)
        all_one = jnp.stack([own_one, *g_one])
        own_two = add(slabs_two[0], *z_two)
        g_two = shifts([own_two] * (zs - 1))
    else:
        slabs_two = [add(keep_two[0, 0], got_two[0, 0], b_two[0, 0], a_two[0])]
        all_one, all_two = (lax.psum(v[0], "ea")[None] for v in (slabs_one, slabs_two))
        g_two = [all_two]
    one_a = over_a(all_one)
    one_a, g_two = after((one_a, g_two), all_one)
    one_01 = jnp.stack([all_one, one_a])
    one_23 = over_b(one_01)
    if zs > 1:
        all_two = jnp.stack([own_two, *g_two])
    two_a = over_a(all_two)
    one_23, two_a = after((one_23, two_a), all_two)
    two_01 = jnp.stack([all_two, two_a])
    one = [one_01, one_23, over_gx(one_01), over_gx(one_23)]
    two_23 = over_b(two_01)
    w_qkv_g, w_proj_g = unpack(sc, one, zs, n_exp, width, first)
    two_23 = after(two_23, w_proj_g)
    two = [two_01, two_23, over_gx(two_01), over_gx(two_23)]
    w_qkv_g, *vectors, qv_g, router_g, in_bias_g, out_bias_g = unpack(
        sc, two, zs, n_exp, width, rest, w_qkv_g
    )
    return (
        output,
        grad_tokens,
        vectors[0],
        vectors[1],
        w_qkv_g.transpose(1, 0, 2),
        qv_g,
        w_proj_g,
        vectors[4],
        vectors[2],
        vectors[3],
        router_g.T,
        in_w_grad,
        in_bias_g,
        out_w_grad,
        out_bias_g,
    )


def solution(mesh):
    tok = P(("ea", "gx", "gy"), None)
    in_specs = (
        tok, tok, tok, P(), P(), P(), P(), P(), P(), P(), P(), P(),
        P("ea", "gx", "gy"), P("ea", None), P("ea", "gy", "gx"), P("ea", None),
    )
    out_specs = (
        tok, tok, P(), P(), P(), P(), P(), P(), P(), P(), P(),
        P("ea", "gx", "gy"), P("ea", None), P("ea", "gy", "gx"), P("ea", None),
    )
    return jax.shard_map(per_device, mesh=mesh, in_specs=in_specs, out_specs=out_specs, check_vma=False)
```

```python
import functools
import math

import jax
import jax.numpy as jnp
from jax import lax
from jax.experimental import pallas as pl
from jax.experimental.pallas import tpu as pltpu
from jax.sharding import PartitionSpec as P

HEADS = 12
HD = 64
SEQ = 197
SEQ_PAD = 208
PAIR = 2 * HD
norm_eps = 1e-06

f32 = jnp.float32
bf16 = jnp.bfloat16
LAST = (((1,), (1,)), ((), ()))
FIRST = (((0,), (0,)), ((), ()))
K0 = math.sqrt(2.0 / math.pi)
C3 = 0.044715


def dot(a, b, dims=None):
    if dims is None:
        return jnp.dot(a, b, preferred_element_type=f32)
    return lax.dot_general(a, b, dims, preferred_element_type=f32)


def spec():
    return pl.BlockSpec(memory_space=pltpu.VMEM)


def call(name, kernel, out_shape, args, flops=1, scratch=(), smem=0):
    return pl.pallas_call(
        kernel,
        name=name,
        out_shape=out_shape,
        in_specs=[pl.BlockSpec(memory_space=pltpu.SMEM)] * smem
        + [spec()] * (len(args) - smem),
        out_specs=jax.tree.map(lambda _: spec(), out_shape),
        scratch_shapes=list(scratch),
        compiler_params=pltpu.CompilerParams(vmem_limit_bytes=30 * 1024 * 1024),
        cost_estimate=pl.CostEstimate(
            flops=flops, bytes_accessed=1, transcendentals=0
        ),
    )(*args)


def shape(dims, dtype):
    return jax.ShapeDtypeStruct(tuple(dims), dtype)


def norm_rows(values):
    centered = values - jnp.mean(values, axis=1, keepdims=True)
    inverse = lax.rsqrt(jnp.mean(centered * centered, axis=1, keepdims=True) + norm_eps)
    return centered * inverse, inverse


def norm_back(grad, normed, inverse, gain):
    scaled = grad * gain
    return inverse * (
        scaled
        - jnp.mean(scaled, axis=1, keepdims=True)
        - normed * jnp.mean(scaled * normed, axis=1, keepdims=True)
    )


def spread_images(dst, src, images):
    width = src.shape[1]
    for i in range(images):
        dst[i * SEQ_PAD : i * SEQ_PAD + SEQ, :] = src[i * SEQ : (i + 1) * SEQ, :]
        dst[i * SEQ_PAD + SEQ : (i + 1) * SEQ_PAD, :] = jnp.zeros((SEQ_PAD - SEQ, width), dst.dtype)


def pick_rows(slot_rows, d, cap):
    slots = lax.broadcasted_iota(jnp.int32, (cap, slot_rows.shape[1]), 0).astype(f32)
    return jnp.where(slots == slot_rows[d : d + 1, :], 1.0, 0.0).astype(bf16)


def pick_cols(slot_cols, d, cap):
    slots = lax.broadcasted_iota(jnp.int32, (slot_cols.shape[0], cap), 1).astype(f32)
    return jnp.where(slots == slot_cols[:, d : d + 1], 1.0, 0.0).astype(bf16)


def route_kernel(n_exp, cap, sc, routes, g_ref, slot_r, slot_c, g_pad, sent, wide):
    t, tp = routes.shape[1], slot_r.shape[1]
    lanes = slot_r.shape[0]
    ids = lax.broadcasted_iota(jnp.int32, (lanes, t), 0) + sc[0]
    ids = jnp.where(ids >= n_exp, ids - n_exp, ids)
    real = lax.broadcasted_iota(jnp.int32, (lanes, t), 0) < n_exp
    chosen = ((routes[0:1, :] == ids) | (routes[1:2, :] == ids)) & real
    ti = lax.broadcasted_iota(jnp.int32, (t, tp), 0)
    tj = lax.broadcasted_iota(jnp.int32, (t, tp), 1)
    moved = jnp.where(ti + (ti // SEQ) * (SEQ_PAD - SEQ) == tj, 1.0, 0.0).astype(bf16)
    chosen = dot(jnp.where(chosen, 1.0, 0.0).astype(bf16), moved)
    ti = lax.broadcasted_iota(jnp.int32, (tp, tp), 0)
    tj = lax.broadcasted_iota(jnp.int32, (tp, tp), 1)
    before = jnp.where(ti < tj, 1.0, 0.0).astype(bf16)
    slots = jnp.where(chosen > 0.5, dot(chosen.astype(bf16), before), -1.0)
    slot_r[...] = slots
    slot_c[...] = jnp.full(slot_c.shape, -1.0, f32)
    slot_c[:, :lanes] = slots.T
    spread_images(wide, g_ref[...].astype(f32), tp // SEQ_PAD)
    g_pad[...] = wide[...].astype(bf16)
    rows = slot_r[...]
    for d in range(n_exp):
        sent[lax.rem(sc[0] + d, n_exp)] = dot(pick_rows(rows, d, cap), g_pad[...]).astype(bf16)


def project_kernel(x_ref, gain1, shift1, w3, qvb, wide, qkv, attn_in):
    spread_images(wide, x_ref[...].astype(f32), wide.shape[0] // SEQ_PAD)
    normed, _ = norm_rows(wide[...])
    attn_in[...] = (normed * gain1[...].reshape(1, -1) + shift1[...].reshape(1, -1)).astype(bf16)
    a = attn_in[...]
    qkv[0] = ((dot(a, w3[0]) + qvb[0:1, :]).astype(bf16).astype(f32) * (HD**-0.5)).astype(bf16)
    qkv[1] = dot(a, w3[1]).astype(bf16)
    qkv[2] = (dot(a, w3[2]) + qvb[1:2, :]).astype(bf16)


def head_masks(rows):
    lane = lax.broadcasted_iota(jnp.int32, (rows, PAIR), 1)
    return lane < HD


def attn_probs(q_head, k_pair):
    scores = dot(q_head, k_pair, LAST)
    keys = lax.broadcasted_iota(jnp.int32, scores.shape, 1)
    scores = jnp.where(keys < SEQ, scores, -1e30)
    powered = jnp.exp(scores - jnp.max(scores, axis=1, keepdims=True))
    return powered * (1.0 / jnp.sum(powered, axis=1, keepdims=True))


def fwd_kernel(n_exp, cap, qkv, wide, wp, pb, gain2, shift2, slot_r, res, ctx, moe_in, *sent):
    tp, width = res.shape
    images = tp // SEQ_PAD
    low = head_masks(SEQ_PAD)
    pairs = width // PAIR

    def pair_step(step, carry):
        img, pair = step // pairs, lax.rem(step, pairs)
        rows = pl.ds(pl.multiple_of(img * SEQ_PAD, 16), SEQ_PAD)
        cols = pl.ds(pl.multiple_of(pair * PAIR, PAIR), PAIR)
        q, k, v = qkv[0, rows, cols], qkv[1, rows, cols], qkv[2, rows, cols]
        zero = jnp.zeros_like(q)
        p0 = attn_probs(jnp.where(low, q, zero), k).astype(bf16)
        p1 = attn_probs(jnp.where(low, zero, q), k).astype(bf16)
        ctx[rows, cols] = jnp.where(low, dot(p0, v), dot(p1, v)).astype(bf16)
        return carry

    lax.fori_loop(0, images * pairs, pair_step, 0, unroll=2)
    res[...] = wide[...] + dot(ctx[...], wp[...]) + pb[...].reshape(1, -1)
    normed, _ = norm_rows(res[...])
    moe_in[...] = (normed * gain2[...].reshape(1, -1) + shift2[...].reshape(1, -1)).astype(bf16)
    rows = slot_r[...]
    for d in range(n_exp):
        sent[d][...] = dot(pick_rows(rows, d, cap), moe_in[...]).astype(bf16)


def moe_kernel(nb, cap, n_exp, hc, sc, *refs):
    rows_in, g_in = refs[:nb], refs[nb : 2 * nb]
    mine, other = refs[2 * nb : 2 * nb + 5], refs[2 * nb + 5 : 2 * nb + 10]
    r = 2 * nb + 10
    in_bias, out_bias, router = refs[r : r + 3]
    r += 3
    y_out, gm_out = refs[r : r + nb], refs[r + nb : r + 2 * nb]
    r += 2 * nb
    hid, gp_out, gr, in_b, out_b, router_g = refs[r : r + 6]
    r += 6
    x, gf, wi, wo, acc_y, acc_g, probs_s, sems = refs[r:]
    c = pl.program_id(0)
    width = x.shape[1]
    half = width // 2
    part = wi.shape[2]

    def copies(i):
        gx = sc[1]
        near = pl.ds(pl.multiple_of(gx * half, half), half)
        far = pl.ds(pl.multiple_of((1 - gx) * half, half), half)
        found = []
        for k, (held, cols) in enumerate(((mine, near), (other, far))):
            first, second = (held[i].at[0], held[i].at[1]) if i < 3 else held[3:]
            found.append(pltpu.make_async_copy(first, wi.at[i, cols, :], sems.at[6 * i + 3 * k]))
            for u in range(2):
                found.append(
                    pltpu.make_async_copy(
                        second.at[:, u * half : (u + 1) * half],
                        wo.at[i, u * half : (u + 1) * half, cols],
                        sems.at[6 * i + 3 * k + 1 + u],
                    )
                )
        return found

    @pl.when(c == 0)
    def _():
        for i in range(4):
            for one in copies(i):
                one.start()
        for b in range(nb):
            x[b * cap : (b + 1) * cap, :] = rows_in[b][...]
            gf[b * cap : (b + 1) * cap, :] = g_in[b][0]
        logits = dot(x[...], router[...], LAST)
        lane = lax.broadcasted_iota(jnp.int32, logits.shape, 1)
        logits = jnp.where(lane < n_exp, logits, -1e30)
        powered = jnp.exp(logits - jnp.max(logits, axis=1, keepdims=True))
        probs = powered / jnp.sum(powered, axis=1, keepdims=True)
        probs_s[...] = probs
        gate = jnp.sum(jnp.where(lane == sc[0], probs, 0.0), axis=1, keepdims=True)
        rows_g = (gate * gf[...].astype(f32)).astype(bf16)
        gr[...] = rows_g
        out_b[...] = jnp.sum(rows_g.astype(f32), axis=0, keepdims=True)
        acc_y[...] = jnp.zeros_like(acc_y)
        acc_g[...] = jnp.zeros_like(acc_g)

    for i in range(4):

        @pl.when(c == i)
        def _():
            for one in copies(i):
                one.wait()

    def step(s, carry):
        cols = pl.ds(pl.multiple_of(s * hc, hc), hc)
        w_in = wi[c, :, cols]
        w_out = wo[c, cols, :]
        pre = dot(x[...], w_in) + in_bias[:, cols]
        gh = dot(gr[...], w_out, LAST)
        sq = pre * pre
        h = 0.5 + 0.5 * jnp.tanh(pre * (K0 + (K0 * C3) * sq))
        low_hidden = (pre * h).astype(bf16)
        hid[:, cols] = low_hidden
        acc_y[...] += dot(low_hidden, w_out)
        slope = h + (h - h * h) * (pre * (2.0 * K0 + (6.0 * C3 * K0) * sq))
        gp = gh * slope
        in_b[:, cols] = jnp.sum(gp, axis=0, keepdims=True)
        gp = gp.astype(bf16)
        gp_out[:, cols] = gp
        acc_g[...] += dot(gp, w_in, LAST)
        return carry

    lax.fori_loop(0, part // hc, step, 0)

    @pl.when(c == 3)
    def _():
        y = (acc_y[...] + out_bias[...]).astype(bf16)
        grad_gate = jnp.sum(gf[...].astype(f32) * y.astype(f32), axis=1, keepdims=True)
        probs = probs_s[...]
        lane = lax.broadcasted_iota(jnp.int32, probs.shape, 1)
        own = jnp.where(lane == sc[0], 1.0, 0.0)
        gate = jnp.sum(own * probs, axis=1, keepdims=True)
        grad_logits = ((grad_gate * gate) * (own - probs)).astype(bf16)
        gm = (acc_g[...] + dot(grad_logits, router[...])).astype(bf16)
        router_g[...] = dot(grad_logits, x[...], FIRST)[: router_g.shape[0], :]
        for b in range(nb):
            y_out[b][...] = y[b * cap : (b + 1) * cap, :]
            gm_out[b][...] = gm[b * cap : (b + 1) * cap, :]


def moe_rows(sc, places, rows, grads, weights, in_bias, out_bias, router, cap, n_exp, flops):
    nb = len(rows)
    nr = nb * cap
    width = rows[0].shape[1]
    part = weights[0].shape[2]
    hidden = 4 * part
    lanes = -(-n_exp // 8) * 8
    hc = part
    whole = lambda dims: pl.BlockSpec(dims, lambda c, sc: (0,) * len(dims))
    grid_spec = pltpu.PrefetchScalarGridSpec(
        num_scalar_prefetch=1,
        grid=(4,),
        in_specs=[whole((cap, width))] * nb
        + [
            pl.BlockSpec((1, cap, width), lambda c, sc, d=d: (lax.rem(sc[0] + n_exp - d, n_exp), 0, 0))
            for d in places
        ]
        + [pl.BlockSpec(memory_space=pl.ANY)] * 10
        + [
            pl.BlockSpec((1, part), lambda c, sc: (0, sc[10 + c])),
            whole((1, width)),
            whole((128, width)),
        ],
        out_specs=[whole((cap, width))] * (2 * nb)
        + [
            pl.BlockSpec((nr, part), lambda c, sc: (0, c)),
            pl.BlockSpec((nr, part), lambda c, sc: (0, c)),
            whole((nr, width)),
            pl.BlockSpec((1, part), lambda c, sc: (0, sc[10 + c])),
            whole((1, width)),
            whole((lanes, width)),
        ],
        scratch_shapes=[
            pltpu.VMEM((nr, width), bf16),
            pltpu.VMEM((nr, width), bf16),
            pltpu.VMEM((4, width, part), bf16),
            pltpu.VMEM((4, part, width), bf16),
            pltpu.VMEM((nr, width), f32),
            pltpu.VMEM((nr, width), f32),
            pltpu.VMEM((nr, 128), f32),
            pltpu.SemaphoreType.DMA((24,)),
        ],
    )
    out = pl.pallas_call(
        functools.partial(moe_kernel, nb, cap, n_exp, hc),
        name="expert_rows",
        grid_spec=grid_spec,
        out_shape=[shape((cap, width), bf16)] * (2 * nb)
        + [
            shape((nr, hidden), bf16),
            shape((nr, hidden), bf16),
            shape((nr, width), bf16),
            shape((1, hidden), f32),
            shape((1, width), f32),
            shape((lanes, width), f32),
        ],
        compiler_params=pltpu.CompilerParams(vmem_limit_bytes=(30 if nr < 600 else 60) * 1024 * 1024),
        cost_estimate=pl.CostEstimate(flops=flops, bytes_accessed=1, transcendentals=0),
    )(sc, *rows, *([grads] * nb), *weights, in_bias, out_bias, router)
    return out[:nb], out[nb : 2 * nb], out[2 * nb :]


def weight_kernel(nb, cap, counts, sc, *refs):
    rows, gr, hid, gp = (
        refs[:nb],
        refs[nb : nb + len(counts)],
        refs[nb + len(counts) : nb + 2 * len(counts)],
        refs[nb + 2 * len(counts) : nb + 3 * len(counts)],
    )
    keep, send, xt, gt, cat = refs[nb + 3 * len(counts) :]
    c = pl.program_id(0)
    width = xt.shape[0]
    half = width // 2

    def gather(parts):
        at = 0
        for one in parts:
            cat[at : at + one.shape[0], :] = one[...]
            at += one.shape[0]

    @pl.when(c == 0)
    def _():
        near = pl.ds(pl.multiple_of(sc[1] * half, half), half)
        far = pl.ds(pl.multiple_of((1 - sc[1]) * half, half), half)
        for source, turned in ((rows, xt), (gr, gt)):
            gather(source)
            turned[:half, :] = cat[:, near].T
            turned[half:, :] = cat[:, far].T

    for j, (turned, source) in enumerate(((xt, gp), (gt, hid))):
        gather(source)
        both = dot(turned[...], cat[...]).astype(bf16)
        keep[0, j] = both[:half, :]
        send[0, j] = both[half:, :]


def split_kernel(own, got, from_x, from_y, first, second):
    total = [own[i].astype(f32) + got[i].astype(f32) + from_x[i].astype(f32) + from_y[i].astype(f32) for i in (0, 1)]
    first[0] = total[0]
    second[0] = total[1].T


def weight_grads(sc, rows, groups, cap):
    nb = len(rows)
    width = rows[0].shape[1]
    hidden = groups[0][1].shape[1]
    part = hidden // 4
    counts = [g[0].shape[0] for g in groups]
    total = nb * cap
    whole = lambda dims: pl.BlockSpec(dims, lambda c, sc: (0,) * len(dims))
    block = (1, 2, width // 2, part)
    grid_spec = pltpu.PrefetchScalarGridSpec(
        num_scalar_prefetch=1,
        grid=(4,),
        in_specs=[whole((cap, width))] * nb
        + [whole((n, width)) for n in counts]
        + [pl.BlockSpec((n, part), lambda c, sc: (0, c)) for n in counts] * 2,
        out_specs=[pl.BlockSpec(block, lambda c, sc: (c, 0, 0, 0))] * 2,
        scratch_shapes=[
            pltpu.VMEM((width, total), bf16),
            pltpu.VMEM((width, total), bf16),
            pltpu.VMEM((total, width), bf16),
        ],
    )
    return pl.pallas_call(
        functools.partial(weight_kernel, nb, cap, counts),
        name="expert_weights",
        grid_spec=grid_spec,
        out_shape=[shape((4, 2, width // 2, part), bf16)] * 2,
        compiler_params=pltpu.CompilerParams(vmem_limit_bytes=(30 if total < 1200 else 60) * 1024 * 1024),
        cost_estimate=pl.CostEstimate(
            flops=1, bytes_accessed=1, transcendentals=0
        ),
    )(sc, *rows, *[g[0] for g in groups], *[g[1] for g in groups], *[g[2] for g in groups])


def attn_back(qkv, dctx, dqkv, pair_range, low, images):
    lo, hi = pair_range
    pairs = hi - lo

    def pair_step(step, carry):
        img, pair = step // pairs, lax.rem(step, pairs)
        rows = pl.ds(pl.multiple_of(img * SEQ_PAD, 16), SEQ_PAD)
        cols = pl.ds(pl.multiple_of((pair + lo) * PAIR, PAIR), PAIR)
        local = pl.ds(pl.multiple_of(pair * PAIR, PAIR), PAIR)
        q, k, v, gc = qkv[0, rows, cols], qkv[1, rows, cols], qkv[2, rows, cols], dctx[rows, cols]
        zero = jnp.zeros_like(q)
        outs = []
        for first in (True, False):
            mine = lambda t: jnp.where(low, t, zero) if first else jnp.where(low, zero, t)
            probs = attn_probs(mine(q), k)
            grad_p = dot(mine(gc), v, LAST)
            mean = jnp.sum(grad_p * probs, axis=1, keepdims=True)
            ds = (probs * (grad_p - mean)).astype(bf16)
            outs.append((dot(ds, k), dot(ds, q, FIRST), dot(probs.astype(bf16), gc, FIRST)))
        join = [jnp.where(low, a, b) for a, b in zip(*outs, strict=True)]
        dqkv[0, rows, local] = (join[0] * (HD**-0.5)).astype(bf16)
        dqkv[1, rows, local] = join[1].astype(bf16)
        dqkv[2, rows, local] = join[2].astype(bf16)
        return carry

    lax.fori_loop(0, images * pairs, pair_step, 0, unroll=2)


def store_slabs(sc, full, keep, send, zs):
    n = keep.shape[2]
    for i in range(4):
        for d in range(zs):
            z = lax.rem(sc[0] + d, zs) if zs > 1 else 0
            base = sc[2 + i] * (n * zs) + z * n
            near = pl.multiple_of(sc[1] * (n * zs * 4) + base, 8)
            keep[i, d] = full[pl.ds(near, n), :].astype(bf16)
            base = sc[6 + i] * (n * zs) + z * n
            far = pl.multiple_of((1 - sc[1]) * (n * zs * 4) + base, 8)
            send[i, d] = full[pl.ds(far, n), :].astype(bf16)


def gather_kernel(cap, slot_c, *refs):
    gm_in, part = refs[:-1], refs[-1]
    cols = slot_c[...]
    total = dot(pick_cols(cols, 0, cap), gm_in[0][...])
    for d in range(1, len(gm_in)):
        total += dot(pick_cols(cols, d, cap), gm_in[d][...])
    part[...] = total


def norm_two_kernel(n_exp, cap, slot_c, res, gain2, g_pad, part, gm_last, grad_res, small):
    grad_moe = part[...] + dot(pick_cols(slot_c[...], n_exp - 1, cap), gm_last[...])
    normed, inverse = norm_rows(res[...])
    grad_res[...] = g_pad[...].astype(f32) + norm_back(grad_moe, normed, inverse, gain2[...].reshape(1, -1))
    small[0:1, :] = jnp.sum(grad_moe * normed, axis=0, keepdims=True)
    small[1:2, :] = jnp.sum(grad_moe, axis=0, keepdims=True)
    small[2:3, :] = jnp.sum(grad_res[...], axis=0, keepdims=True)


def back_one_kernel(zs, sc, grad_res, ctx, wp, qkv, attn_in, keep, send, dctx, dqkv, small, full):
    tp = grad_res.shape[0]
    images = tp // SEQ_PAD
    mix = grad_res[...].astype(bf16)
    part = dqkv.shape[2]
    full[:, 3 * part :] = dot(ctx[...], mix, FIRST)
    dctx[...] = dot(mix, wp[...], LAST).astype(bf16)
    attn_back(qkv, dctx, dqkv, (0, part // PAIR), head_masks(SEQ_PAD), images)
    a = attn_in[...]
    for i in range(3):
        full[:, i * part : (i + 1) * part] = dot(a, dqkv[i], FIRST)
    store_slabs(sc, full, keep, send, zs)
    small[0:1, :] = jnp.sum(dqkv[0].astype(f32), axis=0, keepdims=True)
    small[1:2, :] = jnp.sum(dqkv[2].astype(f32), axis=0, keepdims=True)


def back_two_kernel(
    zs, n_exp, sc, qkv, attn_in, dctx, done, grad_res, w3, x_ref, gain1, small_two, small_one, router_g, in_b, out_b,
    keep, send, grad_tokens, full, dqkv, wide, small,
):
    tp, width = grad_res.shape
    images = tp // SEQ_PAD
    part = done.shape[2]
    rest = width - part
    attn_back(qkv, dctx, dqkv, (part // PAIR, width // PAIR), head_masks(SEQ_PAD), images)
    a = attn_in[...]
    for i in range(3):
        full[:, i * rest : (i + 1) * rest] = dot(a, dqkv[i], FIRST)
    small[...] = jnp.zeros_like(small)
    small[2:5, :] = small_two[0:3, :]
    for i in (0, 2):
        row = 5 + i // 2
        small[row : row + 1, :part] = small_one[i // 2 : 1 + i // 2, :]
        small[row : row + 1, part:] = jnp.sum(dqkv[i].astype(f32), axis=0, keepdims=True)
    small[7 : 7 + n_exp, :] = router_g[:n_exp, :]
    for k in range(4):
        small[pl.ds(7 + n_exp + 4 * sc[0] + k, 1), :] = in_b[k : k + 1, :]
    small[pl.ds(7 + 5 * n_exp + sc[0], 1), :] = out_b[...]
    grad_in = dot(done[0], w3[0, :, :part], LAST) + dot(dqkv[0], w3[0, :, part:], LAST)
    for i in (1, 2):
        grad_in += dot(done[i], w3[i, :, :part], LAST) + dot(dqkv[i], w3[i, :, part:], LAST)
    spread_images(wide, x_ref[...].astype(f32), images)
    normed, inverse = norm_rows(wide[...])
    small[0:1, :] = jnp.sum(grad_in * normed, axis=0, keepdims=True)
    small[1:2, :] = jnp.sum(grad_in, axis=0, keepdims=True)
    full[:, 3 * rest :] = small[...].T
    store_slabs(sc, full, keep, send, zs)
    wide[...] = grad_res[...] + norm_back(grad_in, normed, inverse, gain1[...].reshape(1, -1))
    for i in range(images):
        grad_tokens[i * SEQ : (i + 1) * SEQ, :] = wide[i * SEQ_PAD : i * SEQ_PAD + SEQ, :]


def out_kernel(n_exp, cap, slot_c, moe_in, router, res, *refs):
    y_in, (out, wide, tight) = refs[:n_exp], refs[n_exp:]
    cols = slot_c[...]
    logits = dot(moe_in[...], router[...], LAST)
    lane = lax.broadcasted_iota(jnp.int32, logits.shape, 1)
    logits = jnp.where(lane < n_exp, logits, -1e30)
    powered = jnp.exp(logits - jnp.max(logits, axis=1, keepdims=True))
    probs = powered / jnp.sum(powered, axis=1, keepdims=True)
    total = res[...]
    for d in range(n_exp):
        total += probs[:, d : d + 1] * dot(pick_cols(cols, d, cap), y_in[d][...])
    wide[...] = total
    for i in range(res.shape[0] // SEQ_PAD):
        tight[i * SEQ : (i + 1) * SEQ, :] = wide[i * SEQ_PAD : i * SEQ_PAD + SEQ, :]
    out[...] = tight[...].astype(bf16)


def unpack_kernel(zs, n_exp, lanes, last, sc, *refs):
    parts, refs = refs[:4], refs[4:]
    if last:
        _, w_out, *vectors, qv_g, router_g, in_b, out_b, w_qkv, sems, held, turned_s = refs
    else:
        w_out, held, w_qkv, sems = refs
    n = parts[0].shape[2]
    start = w_out.shape[2] - lanes if last else 0

    def places():
        for q in range(2):
            for i in range(4):
                j = i if q == 0 else (0, 2, 1, 3)[i]
                place = (sc[1] if q == 0 else 1 - sc[1]) * 4 + sc[2 + i]
                for d in range(zs):
                    z = lax.rem(sc[0] - d + zs, zs) if zs > 1 else 0
                    yield parts[2 * q + j // 2].at[j % 2, d], pl.ds(pl.multiple_of((place * zs + z) * n, 8), n)

    copies = []
    for p in range(3):
        for ref, rows in places():
            w_qkv[p, rows, :] = ref[:, p * lanes : (p + 1) * lanes].astype(f32)
        one = pltpu.make_async_copy(w_qkv.at[p], w_out.at[p, :, start : start + lanes], sems.at[p])
        one.start()
        copies.append(one)
    for ref, rows in places():
        held[rows, :] = ref[:, 3 * lanes :].astype(f32)
    if last:
        turned = held[...].T
        for i, vector in enumerate(vectors):
            vector[...] = turned[i : i + 1, :].reshape(-1)
        qv_g[...] = turned[5:7, :]
        router_g[...] = turned[7 : 7 + n_exp, :]
        turned_s[...] = turned
        for k in range(4):
            in_b[:, k * turned.shape[1] : (k + 1) * turned.shape[1]] = turned_s[pl.ds(7 + n_exp + 4 * sc[0] + k, 1), :]
        out_b[...] = turned_s[pl.ds(7 + 5 * n_exp + sc[0], 1), :]
    for one in copies:
        one.wait()


def unpack(sc, slabs, zs, n_exp, width, lanes, base=None):
    last = base is not None
    extra = slabs[0].shape[-1] - 3 * lanes
    whole = lambda dims: pl.BlockSpec(dims, lambda c, sc: (0,) * len(dims))
    more = [(width,)] * 5 + [(2, width), (n_exp, width), (1, 4 * width), (1, width)] if last else [(width, extra)]
    return pl.pallas_call(
        functools.partial(unpack_kernel, zs, n_exp, lanes, last),
        name="unpack",
        grid_spec=pltpu.PrefetchScalarGridSpec(
            num_scalar_prefetch=1,
            grid=(1,),
            in_specs=[whole(v.shape) for v in slabs] + ([pl.BlockSpec(memory_space=pl.ANY)] if last else []),
            out_specs=[
                pl.BlockSpec(memory_space=pl.ANY),
                *[whole(dims) for dims in more],
            ],
            scratch_shapes=[pltpu.VMEM((3, width, lanes), f32), pltpu.SemaphoreType.DMA((3,))]
            + ([pltpu.VMEM((width, extra), f32), pltpu.VMEM((extra, width), f32)] if last else []),
        ),
        out_shape=[shape((3, width, width), f32)] + [shape(dims, f32) for dims in more],
        input_output_aliases={5: 0} if last else {},
        compiler_params=pltpu.CompilerParams(vmem_limit_bytes=30 * 1024 * 1024),
        cost_estimate=pl.CostEstimate(flops=1, bytes_accessed=1, transcendentals=0),
    )(sc, *slabs, *([base] if last else []))


def per_device(
    tokens, routes, cotangent, norm1_gain, norm1_shift, w_qkv, qv_bias, w_proj, proj_bias,
    norm2_gain, norm2_shift, router_w, expert_in, expert_in_bias, expert_out, expert_out_bias,
):
    n_ea, n_gx, n_gy = (lax.axis_size(a) for a in ("ea", "gx", "gy"))
    n_exp = expert_in.shape[0] * n_ea
    assert expert_in.shape[0] == 1 and n_gx == 2 and n_gy == 4
    t, width = tokens.shape
    images = t // SEQ
    tp = images * SEQ_PAD
    capacity = max(2, 8 * t // (3 * n_exp) + 1)
    cap = -(-capacity // 16) * 16
    half = width // 2
    part = expert_in.shape[2]
    zs = n_ea if (width // 8) % (8 * n_ea) == 0 else 1
    first = (HEADS // 6) * PAIR

    ea, gx, gy = (lax.axis_index(a) for a in ("ea", "gx", "gy"))
    near, far = 1 + gx, 2 - gx
    sc = jnp.stack([
        ea, gx, gy, gy ^ near, gy ^ far, gy ^ 3, gy, gy ^ far, gy ^ near, gy ^ 3,
        gy, gy ^ 1, gy ^ 2, gy ^ 3,
    ]).astype(jnp.int32)
    cross = [(0, 1), (1, 0)]
    perm_a = [(g * 4 + y, g * 4 + (y ^ (1 + g))) for g in range(2) for y in range(4)]
    perm_b = [(g * 4 + y, g * 4 + (y ^ (2 - g))) for g in range(2) for y in range(4)]

    def after(v, done):
        return lax.optimization_barrier((v, done))[0]

    def over_gx(v):
        return lax.ppermute(v, "gx", cross)

    def over_x(v):
        return lax.ppermute(v, "gy", [(y, y ^ 1) for y in range(4)])

    def over_y(v):
        return lax.ppermute(v, "gy", [(y, y ^ 2) for y in range(4)])

    def over_a(v):
        return lax.ppermute(v, ("gx", "gy"), perm_a)

    def over_b(v):
        return lax.ppermute(v, ("gx", "gy"), perm_b)

    def over_ea(v):
        return lax.all_to_all(v, "ea", 0, 0, tiled=True)

    def shift(v, d):
        return lax.ppermute(v, "ea", [(i, (i + d) % n_ea) for i in range(n_ea)])

    order = list(range(1, n_ea))

    def dispatch(blocks):
        got = [blocks[0]] + [None] * (n_ea - 1)
        for d in order:
            got[d] = shift(blocks[d], d)
        return got

    own_w = jnp.stack([expert_in[0], jnp.concatenate([expert_out[0, :half], expert_out[0, half:]], axis=1)])
    x_w, y_w = over_x(own_w), over_y(own_w)

    lanes = -(-n_exp // 8) * 8
    block = shape((cap, width), bf16)
    w3 = w_qkv.transpose(1, 0, 2)
    slot_r, slot_c, g_pad, g_sent = call(
        "route",
        functools.partial(route_kernel, n_exp, cap),
        [shape((lanes, tp), f32), shape((tp, 128), f32), shape((tp, width), bf16), shape((n_exp, cap, width), bf16)],
        (sc, routes.T, cotangent),
        scratch=[pltpu.VMEM((tp, width), f32)],
        smem=1,
    )
    g_rows = lax.all_to_all(g_sent, "ea", 0, 0, tiled=True)
    x_pad, qkv, attn_in = call(
        "project",
        project_kernel,
        [shape((tp, width), f32), shape((3, tp, width), bf16), shape((tp, width), bf16)],
        (tokens, norm1_gain, norm1_shift, w3, qv_bias),
    )
    res, ctx, moe_in, *m_sent = call(
        "attn_fwd",
        functools.partial(fwd_kernel, n_exp, cap),
        [shape((tp, width), f32), shape((tp, width), bf16), shape((tp, width), bf16)]
        + [block] * n_exp,
        (qkv, x_pad, w_proj, proj_bias, norm2_gain, norm2_shift, slot_r),
        flops=12_000_000_000,
    )
    other_own = over_gx(own_w)
    x_w, y_w = after((x_w, y_w), (moe_in, other_own))
    mine = [own_w, x_w, y_w, over_x(y_w[0]), over_y(x_w[1])]
    weights = mine + [other_own] + [over_gx(v) for v in mine[1:]]
    own_m, *m_sent = after(tuple(m_sent), g_rows)
    first_m = shift(m_sent[0], 1)
    m_rows = [own_m, first_m] + [shift(v, d) for d, v in enumerate(after(tuple(m_sent[1:]), first_m), 2)]

    router = jnp.pad(router_w.T, ((0, 128 - n_exp), (0, 0)))
    groups = [[d] for d in range(4)] if n_ea == 4 else [list(range(n_ea))]
    y_local, gm_local, gm_back = [None] * n_ea, [None] * n_ea, [None] * n_ea
    kept, in_bias_g, out_bias_g, router_g = [], 0.0, 0.0, 0.0
    for index, group in enumerate(groups):
        if index == 1:
            m_rows[1] = after(m_rows[1], gm_local[0])
        ys, gms, (hid, gp, gr, ib, ob, rg) = moe_rows(
            sc, group, [m_rows[d] for d in group], g_rows, weights,
            expert_in_bias, expert_out_bias, router, cap, n_exp, 12_000_000_000 if index > 1 else 1,
        )
        kept.append((gr, hid, gp))
        in_bias_g, out_bias_g, router_g = in_bias_g + ib, out_bias_g + ob, router_g + rg
        for d, y, gm in zip(group, ys, gms, strict=True):
            y_local[d], gm_local[d] = y, gm
            gm_back[d] = shift(gm, n_ea - d) if d else gm
    rows_all = [m_rows[d] for group in groups for d in group]
    keep, send = weight_grads(sc, rows_all, kept, cap)

    def add(*parts):
        return functools.reduce(lambda a, b: a + b, [p.astype(f32) for p in parts]).astype(bf16)

    def sum_b(keep, got):
        return over_b(add(keep[2:], got[2:]))

    def sum_a(keep, got, got_b):
        return over_a(add(keep[1], got[1], got_b[1]))

    def shifts(parts):
        return [shift(v, d) for d, v in enumerate(parts, 1)]

    gathered = call(
        "gather_rows",
        functools.partial(gather_kernel, cap),
        shape((tp, width), f32),
        (slot_c, *gm_back[:-1]),
        flops=4_000_000_000,
    )
    send, slot_l, gathered, gm_last = after((send, slot_c, gathered, gm_back[-1]), keep)
    got = over_gx(send)
    grad_res, small_two = call(
        "norm_two",
        functools.partial(norm_two_kernel, n_exp, cap),
        [shape((tp, width), f32), shape((8, width), f32)],
        (slot_l, res, norm2_gain, g_pad, gathered, gm_last),
    )
    back = list(range(1, n_ea))
    got, grad_res, *y_local = after((got, grad_res, *y_local), small_two)
    got_x = over_x(add(keep[3, 0], got[3, 0]))
    got_y = over_y(add(keep[3, 1], got[3, 1]))
    y_rows = {}
    n = width // (8 * zs)
    slabs = lambda l: [shape((4, zs, n, l), bf16)] * 2
    keep_one, send_one, dctx, dqkv, small_one = call(
        "back_one",
        functools.partial(back_one_kernel, zs),
        slabs(3 * first + width) + [
            shape((tp, width), bf16), shape((3, tp, first), bf16), shape((2, first), f32),
        ],
        (sc, grad_res, ctx, w_proj, qkv, attn_in),
        flops=12_000_000_000,
        scratch=[pltpu.VMEM((width, 3 * first + width), f32)],
        smem=1,
    )
    got_x, got_y, send_one, dctx, *y_later = after((got_x, got_y, send_one, dctx, *y_local[1:]), small_one)
    y_rows = {d: shift(y, n_ea - d) for d, y in enumerate(y_later, 1) if n_ea != 4 or d != 2}
    early = list(y_rows)
    from_x = over_x(jnp.stack([add(keep[1, 0], got[1, 0]), add(keep[1, 1], got[1, 1], got_y)]))
    from_y = over_y(jnp.stack([add(keep[2, 0], got[2, 0], got_x), add(keep[2, 1], got[2, 1])]))
    got_one = over_gx(send_one)
    rest = width - first
    columns = -(-(7 + 6 * n_exp) // 128) * 128
    keep_two, send_two, grad_tokens = call(
        "back_two",
        functools.partial(back_two_kernel, zs, n_exp),
        slabs(3 * rest + columns) + [shape((t, width), f32)],
        (
            sc, qkv, attn_in, dctx, dqkv, grad_res, w3, tokens, norm1_gain,
            small_two, small_one, router_g, in_bias_g.reshape(4, part), out_bias_g,
        ),
        flops=30_000_000_000,
        scratch=[
            pltpu.VMEM((width, 3 * rest + columns), f32),
            pltpu.VMEM((3, tp, rest), bf16),
            pltpu.VMEM((tp, width), f32),
            pltpu.VMEM((columns, width), f32),
        ],
        smem=1,
    )
    got_one, send_two, from_x, from_y, y_two, *y_early = after(
        (got_one, send_two, from_x, from_y, y_later[1], *(y_rows[d] for d in early)), grad_tokens
    )
    y_rows = dict(zip(early, y_early, strict=True))
    if n_ea == 4:
        y_rows[2] = shift(y_two, 2)
    got_two = over_gx(send_two)
    b_one = sum_b(keep_one, got_one)
    b_one, got_two = after((b_one, got_two), keep_two)
    a_one = sum_a(keep_one, got_one, b_one)
    b_two = sum_b(keep_two, got_two)
    in_w_grad, out_w_grad = call(
        "expert_grads",
        split_kernel,
        [shape((1, half, part), f32), shape((1, part, half), f32)],
        (keep[0], got[0], from_x, from_y),
    )
    a_one, b_two, in_w_grad, out_w_grad, y_late = after(
        (a_one, b_two, in_w_grad, out_w_grad, tuple(y_rows[d] for d in back)), got_two
    )
    rolled = jnp.pad(
        lax.dynamic_slice_in_dim(jnp.concatenate([router_w.T, router_w.T]), ea, n_exp, 0),
        ((0, 128 - n_exp), (0, 0)),
    )
    output = call(
        "combine",
        functools.partial(out_kernel, n_exp, cap),
        shape((t, width), bf16),
        (slot_c, moe_in, rolled, res, y_local[0], *y_late),
        scratch=[pltpu.VMEM((tp, width), f32), pltpu.VMEM((t, width), f32)],
    )
    slabs_one = [add(keep_one[0, d], got_one[0, d], b_one[0, d], a_one[d]) for d in range(zs)]
    a_two = sum_a(keep_two, got_two, b_two)
    if zs > 1:
        z_one = shifts(slabs_one[1:])
        z_one, a_two = after((z_one, a_two), b_two)
        own_one = add(slabs_one[0], *z_one)
        slabs_two = [add(keep_two[0, d], got_two[0, d], b_two[0, d], a_two[d]) for d in range(zs)]
        g_one = shifts([own_one] * (zs - 1))
        z_two = shifts(slabs_two[1:])
        g_one, z_two, output = after((g_one, z_two, output), a_two)
        all_one = jnp.stack([own_one, *g_one])
        own_two = add(slabs_two[0], *z_two)
        g_two = shifts([own_two] * (zs - 1))
    else:
        slabs_two = [add(keep_two[0, 0], got_two[0, 0], b_two[0, 0], a_two[0])]
        all_one, all_two = (lax.psum(v[0], "ea")[None] for v in (slabs_one, slabs_two))
        g_two = [all_two]
    one_a = over_a(all_one)
    one_a, g_two = after((one_a, g_two), all_one)
    one_01 = jnp.stack([all_one, one_a])
    one_23 = over_b(one_01)
    if zs > 1:
        all_two = jnp.stack([own_two, *g_two])
    two_a = over_a(all_two)
    one_23, two_a = after((one_23, two_a), all_two)
    two_01 = jnp.stack([all_two, two_a])
    one = [one_01, one_23, over_gx(one_01), over_gx(one_23)]
    two_23 = over_b(two_01)
    w_qkv_g, w_proj_g = unpack(sc, one, zs, n_exp, width, first)
    two_23 = after(two_23, w_proj_g)
    two = [two_01, two_23, over_gx(two_01), over_gx(two_23)]
    w_qkv_g, *vectors, qv_g, router_g, in_bias_g, out_bias_g = unpack(
        sc, two, zs, n_exp, width, rest, w_qkv_g
    )
    return (
        output,
        grad_tokens,
        vectors[0],
        vectors[1],
        w_qkv_g.transpose(1, 0, 2),
        qv_g,
        w_proj_g,
        vectors[4],
        vectors[2],
        vectors[3],
        router_g.T,
        in_w_grad,
        in_bias_g,
        out_w_grad,
        out_bias_g,
    )


def solution(mesh):
    tok = P(("ea", "gx", "gy"), None)
    in_specs = (
        tok, tok, tok, P(), P(), P(), P(), P(), P(), P(), P(), P(),
        P("ea", "gx", "gy"), P("ea", None), P("ea", "gy", "gx"), P("ea", None),
    )
    out_specs = (
        tok, tok, P(), P(), P(), P(), P(), P(), P(), P(), P(),
        P("ea", "gx", "gy"), P("ea", None), P("ea", "gy", "gx"), P("ea", None),
    )
    return jax.shard_map(per_device, mesh=mesh, in_specs=in_specs, out_specs=out_specs, check_vma=False)
```

```python
import functools
import math

import jax
import jax.numpy as jnp
from jax import lax
from jax.experimental import pallas as pl
from jax.experimental.pallas import tpu as pltpu
from jax.sharding import PartitionSpec as P

HEADS = 12
HD = 64
SEQ = 197
SEQ_PAD = 208
PAIR = 2 * HD
norm_eps = 1e-06

f32 = jnp.float32
bf16 = jnp.bfloat16
LAST = (((1,), (1,)), ((), ()))
FIRST = (((0,), (0,)), ((), ()))
K0 = math.sqrt(2.0 / math.pi)
C3 = 0.044715


def dot(a, b, dims=None):
    if dims is None:
        return jnp.dot(a, b, preferred_element_type=f32)
    return lax.dot_general(a, b, dims, preferred_element_type=f32)


def spec():
    return pl.BlockSpec(memory_space=pltpu.VMEM)


def call(name, kernel, out_shape, args, flops=1, scratch=(), smem=0):
    return pl.pallas_call(
        kernel,
        name=name,
        out_shape=out_shape,
        in_specs=[pl.BlockSpec(memory_space=pltpu.SMEM)] * smem
        + [spec()] * (len(args) - smem),
        out_specs=jax.tree.map(lambda _: spec(), out_shape),
        scratch_shapes=list(scratch),
        compiler_params=pltpu.CompilerParams(vmem_limit_bytes=30 * 1024 * 1024),
        cost_estimate=pl.CostEstimate(
            flops=flops, bytes_accessed=1, transcendentals=0
        ),
    )(*args)


def shape(dims, dtype):
    return jax.ShapeDtypeStruct(tuple(dims), dtype)


def norm_rows(values):
    centered = values - jnp.mean(values, axis=1, keepdims=True)
    inverse = lax.rsqrt(jnp.mean(centered * centered, axis=1, keepdims=True) + norm_eps)
    return centered * inverse, inverse


def norm_back(grad, normed, inverse, gain):
    scaled = grad * gain
    return inverse * (
        scaled
        - jnp.mean(scaled, axis=1, keepdims=True)
        - normed * jnp.mean(scaled * normed, axis=1, keepdims=True)
    )


def spread_images(dst, src, images):
    width = src.shape[1]
    for i in range(images):
        dst[i * SEQ_PAD : i * SEQ_PAD + SEQ, :] = src[i * SEQ : (i + 1) * SEQ, :]
        dst[i * SEQ_PAD + SEQ : (i + 1) * SEQ_PAD, :] = jnp.zeros((SEQ_PAD - SEQ, width), dst.dtype)


def pick_rows(slot_rows, d, cap):
    slots = lax.broadcasted_iota(jnp.int32, (cap, slot_rows.shape[1]), 0).astype(f32)
    return jnp.where(slots == slot_rows[d : d + 1, :], 1.0, 0.0).astype(bf16)


def pick_cols(slot_cols, d, cap):
    slots = lax.broadcasted_iota(jnp.int32, (slot_cols.shape[0], cap), 1).astype(f32)
    return jnp.where(slots == slot_cols[:, d : d + 1], 1.0, 0.0).astype(bf16)


def route_kernel(n_exp, cap, sc, routes, g_ref, slot_r, slot_c, g_pad, sent, wide):
    t, tp = routes.shape[1], slot_r.shape[1]
    lanes = slot_r.shape[0]
    ids = lax.broadcasted_iota(jnp.int32, (lanes, t), 0) + sc[0]
    ids = jnp.where(ids >= n_exp, ids - n_exp, ids)
    real = lax.broadcasted_iota(jnp.int32, (lanes, t), 0) < n_exp
    chosen = ((routes[0:1, :] == ids) | (routes[1:2, :] == ids)) & real
    ti = lax.broadcasted_iota(jnp.int32, (t, tp), 0)
    tj = lax.broadcasted_iota(jnp.int32, (t, tp), 1)
    moved = jnp.where(ti + (ti // SEQ) * (SEQ_PAD - SEQ) == tj, 1.0, 0.0).astype(bf16)
    chosen = dot(jnp.where(chosen, 1.0, 0.0).astype(bf16), moved)
    ti = lax.broadcasted_iota(jnp.int32, (tp, tp), 0)
    tj = lax.broadcasted_iota(jnp.int32, (tp, tp), 1)
    before = jnp.where(ti < tj, 1.0, 0.0).astype(bf16)
    slots = jnp.where(chosen > 0.5, dot(chosen.astype(bf16), before), -1.0)
    slot_r[...] = slots
    slot_c[...] = jnp.full(slot_c.shape, -1.0, f32)
    slot_c[:, :lanes] = slots.T
    spread_images(wide, g_ref[...].astype(f32), tp // SEQ_PAD)
    g_pad[...] = wide[...].astype(bf16)
    rows = slot_r[...]
    for d in range(n_exp):
        sent[lax.rem(sc[0] + d, n_exp)] = dot(pick_rows(rows, d, cap), g_pad[...]).astype(bf16)


def project_kernel(x_ref, gain1, shift1, w3, qvb, wide, qkv, attn_in):
    spread_images(wide, x_ref[...].astype(f32), wide.shape[0] // SEQ_PAD)
    normed, _ = norm_rows(wide[...])
    attn_in[...] = (normed * gain1[...].reshape(1, -1) + shift1[...].reshape(1, -1)).astype(bf16)
    a = attn_in[...]
    qkv[0] = ((dot(a, w3[0]) + qvb[0:1, :]).astype(bf16).astype(f32) * (HD**-0.5)).astype(bf16)
    qkv[1] = dot(a, w3[1]).astype(bf16)
    qkv[2] = (dot(a, w3[2]) + qvb[1:2, :]).astype(bf16)


def head_masks(rows):
    lane = lax.broadcasted_iota(jnp.int32, (rows, PAIR), 1)
    return lane < HD


def attn_probs(q_head, k_pair):
    scores = dot(q_head, k_pair, LAST)
    keys = lax.broadcasted_iota(jnp.int32, scores.shape, 1)
    scores = jnp.where(keys < SEQ, scores, -1e30)
    powered = jnp.exp(scores - jnp.max(scores, axis=1, keepdims=True))
    return powered * (1.0 / jnp.sum(powered, axis=1, keepdims=True))


def fwd_kernel(n_exp, cap, qkv, wide, wp, pb, gain2, shift2, slot_r, res, ctx, moe_in, probs, *sent):
    tp, width = res.shape
    images = tp // SEQ_PAD
    low = head_masks(SEQ_PAD)
    pairs = width // PAIR

    def pair_step(step, carry):
        img, pair = step // pairs, lax.rem(step, pairs)
        rows = pl.ds(pl.multiple_of(img * SEQ_PAD, 16), SEQ_PAD)
        cols = pl.ds(pl.multiple_of(pair * PAIR, PAIR), PAIR)
        q, k, v = qkv[0, rows, cols], qkv[1, rows, cols], qkv[2, rows, cols]
        zero = jnp.zeros_like(q)
        p0 = attn_probs(jnp.where(low, q, zero), k).astype(bf16)
        p1 = attn_probs(jnp.where(low, zero, q), k).astype(bf16)
        probs[step, 0], probs[step, 1] = p0, p1
        ctx[rows, cols] = jnp.where(low, dot(p0, v), dot(p1, v)).astype(bf16)
        return carry

    lax.fori_loop(0, images * pairs, pair_step, 0, unroll=2)
    res[...] = wide[...] + dot(ctx[...], wp[...]) + pb[...].reshape(1, -1)
    normed, _ = norm_rows(res[...])
    moe_in[...] = (normed * gain2[...].reshape(1, -1) + shift2[...].reshape(1, -1)).astype(bf16)
    rows = slot_r[...]
    for d in range(n_exp):
        sent[d][...] = dot(pick_rows(rows, d, cap), moe_in[...]).astype(bf16)


def moe_kernel(nb, cap, n_exp, hc, sc, *refs):
    rows_in, g_in = refs[:nb], refs[nb : 2 * nb]
    mine, other = refs[2 * nb : 2 * nb + 5], refs[2 * nb + 5 : 2 * nb + 10]
    r = 2 * nb + 10
    in_bias, out_bias, router = refs[r : r + 3]
    r += 3
    y_out, gm_out = refs[r : r + nb], refs[r + nb : r + 2 * nb]
    r += 2 * nb
    hid, gp_out, gr, in_b, out_b, router_g = refs[r : r + 6]
    r += 6
    x, gf, wi, wo, acc_y, acc_g, probs_s, sems = refs[r:]
    c = pl.program_id(0)
    width = x.shape[1]
    half = width // 2
    part = wi.shape[2]

    def copies(i):
        gx = sc[1]
        near = pl.ds(pl.multiple_of(gx * half, half), half)
        far = pl.ds(pl.multiple_of((1 - gx) * half, half), half)
        found = []
        for k, (held, cols) in enumerate(((mine, near), (other, far))):
            first, second = (held[i].at[0], held[i].at[1]) if i < 3 else held[3:]
            found.append(pltpu.make_async_copy(first, wi.at[i, cols, :], sems.at[6 * i + 3 * k]))
            for u in range(2):
                found.append(
                    pltpu.make_async_copy(
                        second.at[:, u * half : (u + 1) * half],
                        wo.at[i, u * half : (u + 1) * half, cols],
                        sems.at[6 * i + 3 * k + 1 + u],
                    )
                )
        return found

    @pl.when(c == 0)
    def _():
        for i in range(4):
            for one in copies(i):
                one.start()
        for b in range(nb):
            x[b * cap : (b + 1) * cap, :] = rows_in[b][...]
            gf[b * cap : (b + 1) * cap, :] = g_in[b][0]
        logits = dot(x[...], router[...], LAST)
        lane = lax.broadcasted_iota(jnp.int32, logits.shape, 1)
        logits = jnp.where(lane < n_exp, logits, -1e30)
        powered = jnp.exp(logits - jnp.max(logits, axis=1, keepdims=True))
        probs = powered / jnp.sum(powered, axis=1, keepdims=True)
        probs_s[...] = probs
        gate = jnp.sum(jnp.where(lane == sc[0], probs, 0.0), axis=1, keepdims=True)
        rows_g = (gate * gf[...].astype(f32)).astype(bf16)
        gr[...] = rows_g
        out_b[...] = jnp.sum(rows_g.astype(f32), axis=0, keepdims=True)
        acc_y[...] = jnp.zeros_like(acc_y)
        acc_g[...] = jnp.zeros_like(acc_g)

    for i in range(4):

        @pl.when(c == i)
        def _():
            for one in copies(i):
                one.wait()

    def step(s, carry):
        cols = pl.ds(pl.multiple_of(s * hc, hc), hc)
        w_in = wi[c, :, cols]
        w_out = wo[c, cols, :]
        pre = dot(x[...], w_in) + in_bias[:, cols]
        gh = dot(gr[...], w_out, LAST)
        sq = pre * pre
        h = 0.5 + 0.5 * jnp.tanh(pre * (K0 + (K0 * C3) * sq))
        low_hidden = (pre * h).astype(bf16)
        hid[:, cols] = low_hidden
        acc_y[...] += dot(low_hidden, w_out)
        slope = h + (h - h * h) * (pre * (2.0 * K0 + (6.0 * C3 * K0) * sq))
        gp = gh * slope
        in_b[:, cols] = jnp.sum(gp, axis=0, keepdims=True)
        gp = gp.astype(bf16)
        gp_out[:, cols] = gp
        acc_g[...] += dot(gp, w_in, LAST)
        return carry

    lax.fori_loop(0, part // hc, step, 0)

    @pl.when(c == 3)
    def _():
        y = (acc_y[...] + out_bias[...]).astype(bf16)
        grad_gate = jnp.sum(gf[...].astype(f32) * y.astype(f32), axis=1, keepdims=True)
        probs = probs_s[...]
        lane = lax.broadcasted_iota(jnp.int32, probs.shape, 1)
        own = jnp.where(lane == sc[0], 1.0, 0.0)
        gate = jnp.sum(own * probs, axis=1, keepdims=True)
        grad_logits = ((grad_gate * gate) * (own - probs)).astype(bf16)
        gm = (acc_g[...] + dot(grad_logits, router[...])).astype(bf16)
        router_g[...] = dot(grad_logits, x[...], FIRST)[: router_g.shape[0], :]
        for b in range(nb):
            y_out[b][...] = y[b * cap : (b + 1) * cap, :]
            gm_out[b][...] = gm[b * cap : (b + 1) * cap, :]


def moe_rows(sc, places, rows, grads, weights, in_bias, out_bias, router, cap, n_exp, flops):
    nb = len(rows)
    nr = nb * cap
    width = rows[0].shape[1]
    part = weights[0].shape[2]
    hidden = 4 * part
    lanes = -(-n_exp // 8) * 8
    hc = part
    whole = lambda dims: pl.BlockSpec(dims, lambda c, sc: (0,) * len(dims))
    grid_spec = pltpu.PrefetchScalarGridSpec(
        num_scalar_prefetch=1,
        grid=(4,),
        in_specs=[whole((cap, width))] * nb
        + [
            pl.BlockSpec((1, cap, width), lambda c, sc, d=d: (lax.rem(sc[0] + n_exp - d, n_exp), 0, 0))
            for d in places
        ]
        + [pl.BlockSpec(memory_space=pl.ANY)] * 10
        + [
            pl.BlockSpec((1, part), lambda c, sc: (0, sc[10 + c])),
            whole((1, width)),
            whole((128, width)),
        ],
        out_specs=[whole((cap, width))] * (2 * nb)
        + [
            pl.BlockSpec((nr, part), lambda c, sc: (0, c)),
            pl.BlockSpec((nr, part), lambda c, sc: (0, c)),
            whole((nr, width)),
            pl.BlockSpec((1, part), lambda c, sc: (0, sc[10 + c])),
            whole((1, width)),
            whole((lanes, width)),
        ],
        scratch_shapes=[
            pltpu.VMEM((nr, width), bf16),
            pltpu.VMEM((nr, width), bf16),
            pltpu.VMEM((4, width, part), bf16),
            pltpu.VMEM((4, part, width), bf16),
            pltpu.VMEM((nr, width), f32),
            pltpu.VMEM((nr, width), f32),
            pltpu.VMEM((nr, 128), f32),
            pltpu.SemaphoreType.DMA((24,)),
        ],
    )
    out = pl.pallas_call(
        functools.partial(moe_kernel, nb, cap, n_exp, hc),
        name="expert_rows",
        grid_spec=grid_spec,
        out_shape=[shape((cap, width), bf16)] * (2 * nb)
        + [
            shape((nr, hidden), bf16),
            shape((nr, hidden), bf16),
            shape((nr, width), bf16),
            shape((1, hidden), f32),
            shape((1, width), f32),
            shape((lanes, width), f32),
        ],
        compiler_params=pltpu.CompilerParams(vmem_limit_bytes=(30 if nr < 600 else 60) * 1024 * 1024),
        cost_estimate=pl.CostEstimate(flops=flops, bytes_accessed=1, transcendentals=0),
    )(sc, *rows, *([grads] * nb), *weights, in_bias, out_bias, router)
    return out[:nb], out[nb : 2 * nb], out[2 * nb :]


def weight_kernel(nb, cap, counts, sc, *refs):
    rows, gr, hid, gp = (
        refs[:nb],
        refs[nb : nb + len(counts)],
        refs[nb + len(counts) : nb + 2 * len(counts)],
        refs[nb + 2 * len(counts) : nb + 3 * len(counts)],
    )
    keep, send, xt, gt, cat = refs[nb + 3 * len(counts) :]
    c = pl.program_id(0)
    width = xt.shape[0]
    half = width // 2

    def gather(parts):
        at = 0
        for one in parts:
            cat[at : at + one.shape[0], :] = one[...]
            at += one.shape[0]

    @pl.when(c == 0)
    def _():
        near = pl.ds(pl.multiple_of(sc[1] * half, half), half)
        far = pl.ds(pl.multiple_of((1 - sc[1]) * half, half), half)
        for source, turned in ((rows, xt), (gr, gt)):
            gather(source)
            turned[:half, :] = cat[:, near].T
            turned[half:, :] = cat[:, far].T

    for j, (turned, source) in enumerate(((xt, gp), (gt, hid))):
        gather(source)
        both = dot(turned[...], cat[...]).astype(bf16)
        keep[0, j] = both[:half, :]
        send[0, j] = both[half:, :]


def split_kernel(own, got, from_x, from_y, first, second):
    total = [own[i].astype(f32) + got[i].astype(f32) + from_x[i].astype(f32) + from_y[i].astype(f32) for i in (0, 1)]
    first[0] = total[0]
    second[0] = total[1].T


def weight_grads(sc, rows, groups, cap):
    nb = len(rows)
    width = rows[0].shape[1]
    hidden = groups[0][1].shape[1]
    part = hidden // 4
    counts = [g[0].shape[0] for g in groups]
    total = nb * cap
    whole = lambda dims: pl.BlockSpec(dims, lambda c, sc: (0,) * len(dims))
    block = (1, 2, width // 2, part)
    grid_spec = pltpu.PrefetchScalarGridSpec(
        num_scalar_prefetch=1,
        grid=(4,),
        in_specs=[whole((cap, width))] * nb
        + [whole((n, width)) for n in counts]
        + [pl.BlockSpec((n, part), lambda c, sc: (0, c)) for n in counts] * 2,
        out_specs=[pl.BlockSpec(block, lambda c, sc: (c, 0, 0, 0))] * 2,
        scratch_shapes=[
            pltpu.VMEM((width, total), bf16),
            pltpu.VMEM((width, total), bf16),
            pltpu.VMEM((total, width), bf16),
        ],
    )
    return pl.pallas_call(
        functools.partial(weight_kernel, nb, cap, counts),
        name="expert_weights",
        grid_spec=grid_spec,
        out_shape=[shape((4, 2, width // 2, part), bf16)] * 2,
        compiler_params=pltpu.CompilerParams(vmem_limit_bytes=(30 if total < 1200 else 60) * 1024 * 1024),
        cost_estimate=pl.CostEstimate(
            flops=1, bytes_accessed=1, transcendentals=0
        ),
    )(sc, *rows, *[g[0] for g in groups], *[g[1] for g in groups], *[g[2] for g in groups])


def attn_back(probs, qkv, dctx, dqkv, pair_range, low, images):
    lo, hi = pair_range
    pairs = hi - lo

    def pair_step(step, carry):
        img, pair = step // pairs, lax.rem(step, pairs)
        rows = pl.ds(pl.multiple_of(img * SEQ_PAD, 16), SEQ_PAD)
        cols = pl.ds(pl.multiple_of((pair + lo) * PAIR, PAIR), PAIR)
        local = pl.ds(pl.multiple_of(pair * PAIR, PAIR), PAIR)
        q, k, v, gc = qkv[0, rows, cols], qkv[1, rows, cols], qkv[2, rows, cols], dctx[rows, cols]
        zero = jnp.zeros_like(q)
        outs = []
        for head in range(2):
            kept = probs[img * (qkv.shape[2] // PAIR) + pair + lo, head]
            weight = kept.astype(f32)
            grad_p = dot(jnp.where(low, gc, zero) if head == 0 else jnp.where(low, zero, gc), v, LAST)
            mean = jnp.sum(grad_p * weight, axis=1, keepdims=True)
            ds = (weight * (grad_p - mean)).astype(bf16)
            outs.append((dot(ds, k), dot(ds, q, FIRST), dot(kept, gc, FIRST)))
        join = [jnp.where(low, a, b) for a, b in zip(*outs, strict=True)]
        dqkv[0, rows, local] = (join[0] * (HD**-0.5)).astype(bf16)
        dqkv[1, rows, local] = join[1].astype(bf16)
        dqkv[2, rows, local] = join[2].astype(bf16)
        return carry

    lax.fori_loop(0, images * pairs, pair_step, 0, unroll=2)


def store_slabs(sc, full, keep, send, zs):
    n = keep.shape[2]
    for i in range(4):
        for d in range(zs):
            z = lax.rem(sc[0] + d, zs) if zs > 1 else 0
            base = sc[2 + i] * (n * zs) + z * n
            near = pl.multiple_of(sc[1] * (n * zs * 4) + base, 8)
            keep[i, d] = full[pl.ds(near, n), :].astype(bf16)
            base = sc[6 + i] * (n * zs) + z * n
            far = pl.multiple_of((1 - sc[1]) * (n * zs * 4) + base, 8)
            send[i, d] = full[pl.ds(far, n), :].astype(bf16)


def gather_kernel(cap, slot_c, *refs):
    gm_in, part = refs[:-1], refs[-1]
    cols = slot_c[...]
    total = dot(pick_cols(cols, 0, cap), gm_in[0][...])
    for d in range(1, len(gm_in)):
        total += dot(pick_cols(cols, d, cap), gm_in[d][...])
    part[...] = total


def norm_two_kernel(n_exp, cap, slot_c, res, gain2, g_pad, part, gm_last, grad_res, small):
    grad_moe = part[...] + dot(pick_cols(slot_c[...], n_exp - 1, cap), gm_last[...])
    normed, inverse = norm_rows(res[...])
    grad_res[...] = g_pad[...].astype(f32) + norm_back(grad_moe, normed, inverse, gain2[...].reshape(1, -1))
    small[0:1, :] = jnp.sum(grad_moe * normed, axis=0, keepdims=True)
    small[1:2, :] = jnp.sum(grad_moe, axis=0, keepdims=True)
    small[2:3, :] = jnp.sum(grad_res[...], axis=0, keepdims=True)


def back_one_kernel(zs, sc, grad_res, ctx, wp, probs, qkv, attn_in, keep, send, dctx, dqkv, small, full):
    tp = grad_res.shape[0]
    images = tp // SEQ_PAD
    mix = grad_res[...].astype(bf16)
    part = dqkv.shape[2]
    full[:, 3 * part :] = dot(ctx[...], mix, FIRST)
    dctx[...] = dot(mix, wp[...], LAST).astype(bf16)
    attn_back(probs, qkv, dctx, dqkv, (0, part // PAIR), head_masks(SEQ_PAD), images)
    a = attn_in[...]
    for i in range(3):
        full[:, i * part : (i + 1) * part] = dot(a, dqkv[i], FIRST)
    store_slabs(sc, full, keep, send, zs)
    small[0:1, :] = jnp.sum(dqkv[0].astype(f32), axis=0, keepdims=True)
    small[1:2, :] = jnp.sum(dqkv[2].astype(f32), axis=0, keepdims=True)


def back_two_kernel(
    zs, n_exp, sc, probs, qkv, attn_in, dctx, done, grad_res, w3, x_ref, gain1, small_two, small_one, router_g, in_b, out_b,
    keep, send, grad_tokens, full, dqkv, wide, small,
):
    tp, width = grad_res.shape
    images = tp // SEQ_PAD
    part = done.shape[2]
    rest = width - part
    attn_back(probs, qkv, dctx, dqkv, (part // PAIR, width // PAIR), head_masks(SEQ_PAD), images)
    a = attn_in[...]
    for i in range(3):
        full[:, i * rest : (i + 1) * rest] = dot(a, dqkv[i], FIRST)
    small[...] = jnp.zeros_like(small)
    small[2:5, :] = small_two[0:3, :]
    for i in (0, 2):
        row = 5 + i // 2
        small[row : row + 1, :part] = small_one[i // 2 : 1 + i // 2, :]
        small[row : row + 1, part:] = jnp.sum(dqkv[i].astype(f32), axis=0, keepdims=True)
    small[7 : 7 + n_exp, :] = router_g[:n_exp, :]
    for k in range(4):
        small[pl.ds(7 + n_exp + 4 * sc[0] + k, 1), :] = in_b[k : k + 1, :]
    small[pl.ds(7 + 5 * n_exp + sc[0], 1), :] = out_b[...]
    grad_in = dot(done[0], w3[0, :, :part], LAST) + dot(dqkv[0], w3[0, :, part:], LAST)
    for i in (1, 2):
        grad_in += dot(done[i], w3[i, :, :part], LAST) + dot(dqkv[i], w3[i, :, part:], LAST)
    spread_images(wide, x_ref[...].astype(f32), images)
    normed, inverse = norm_rows(wide[...])
    small[0:1, :] = jnp.sum(grad_in * normed, axis=0, keepdims=True)
    small[1:2, :] = jnp.sum(grad_in, axis=0, keepdims=True)
    full[:, 3 * rest :] = small[...].T
    store_slabs(sc, full, keep, send, zs)
    wide[...] = grad_res[...] + norm_back(grad_in, normed, inverse, gain1[...].reshape(1, -1))
    for i in range(images):
        grad_tokens[i * SEQ : (i + 1) * SEQ, :] = wide[i * SEQ_PAD : i * SEQ_PAD + SEQ, :]


def out_kernel(n_exp, cap, slot_c, moe_in, router, res, *refs):
    y_in, (out, wide, tight) = refs[:n_exp], refs[n_exp:]
    cols = slot_c[...]
    logits = dot(moe_in[...], router[...], LAST)
    lane = lax.broadcasted_iota(jnp.int32, logits.shape, 1)
    logits = jnp.where(lane < n_exp, logits, -1e30)
    powered = jnp.exp(logits - jnp.max(logits, axis=1, keepdims=True))
    probs = powered / jnp.sum(powered, axis=1, keepdims=True)
    total = res[...]
    for d in range(n_exp):
        total += probs[:, d : d + 1] * dot(pick_cols(cols, d, cap), y_in[d][...])
    wide[...] = total
    for i in range(res.shape[0] // SEQ_PAD):
        tight[i * SEQ : (i + 1) * SEQ, :] = wide[i * SEQ_PAD : i * SEQ_PAD + SEQ, :]
    out[...] = tight[...].astype(bf16)


def unpack_kernel(zs, n_exp, lanes, last, sc, *refs):
    parts, refs = refs[:4], refs[4:]
    if last:
        _, w_out, *vectors, qv_g, router_g, in_b, out_b, w_qkv, sems, held, turned_s = refs
    else:
        w_out, held, w_qkv, sems = refs
    n = parts[0].shape[2]
    start = w_out.shape[2] - lanes if last else 0

    def places():
        for q in range(2):
            for i in range(4):
                j = i if q == 0 else (0, 2, 1, 3)[i]
                place = (sc[1] if q == 0 else 1 - sc[1]) * 4 + sc[2 + i]
                for d in range(zs):
                    z = lax.rem(sc[0] - d + zs, zs) if zs > 1 else 0
                    yield parts[2 * q + j // 2].at[j % 2, d], pl.ds(pl.multiple_of((place * zs + z) * n, 8), n)

    copies = []
    for p in range(3):
        for ref, rows in places():
            w_qkv[p, rows, :] = ref[:, p * lanes : (p + 1) * lanes].astype(f32)
        one = pltpu.make_async_copy(w_qkv.at[p], w_out.at[p, :, start : start + lanes], sems.at[p])
        one.start()
        copies.append(one)
    for ref, rows in places():
        held[rows, :] = ref[:, 3 * lanes :].astype(f32)
    if last:
        turned = held[...].T
        for i, vector in enumerate(vectors):
            vector[...] = turned[i : i + 1, :].reshape(-1)
        qv_g[...] = turned[5:7, :]
        router_g[...] = turned[7 : 7 + n_exp, :]
        turned_s[...] = turned
        for k in range(4):
            in_b[:, k * turned.shape[1] : (k + 1) * turned.shape[1]] = turned_s[pl.ds(7 + n_exp + 4 * sc[0] + k, 1), :]
        out_b[...] = turned_s[pl.ds(7 + 5 * n_exp + sc[0], 1), :]
    for one in copies:
        one.wait()


def unpack(sc, slabs, zs, n_exp, width, lanes, base=None):
    last = base is not None
    extra = slabs[0].shape[-1] - 3 * lanes
    whole = lambda dims: pl.BlockSpec(dims, lambda c, sc: (0,) * len(dims))
    more = [(width,)] * 5 + [(2, width), (n_exp, width), (1, 4 * width), (1, width)] if last else [(width, extra)]
    return pl.pallas_call(
        functools.partial(unpack_kernel, zs, n_exp, lanes, last),
        name="unpack",
        grid_spec=pltpu.PrefetchScalarGridSpec(
            num_scalar_prefetch=1,
            grid=(1,),
            in_specs=[whole(v.shape) for v in slabs] + ([pl.BlockSpec(memory_space=pl.ANY)] if last else []),
            out_specs=[
                pl.BlockSpec(memory_space=pl.ANY),
                *[whole(dims) for dims in more],
            ],
            scratch_shapes=[pltpu.VMEM((3, width, lanes), f32), pltpu.SemaphoreType.DMA((3,))]
            + ([pltpu.VMEM((width, extra), f32), pltpu.VMEM((extra, width), f32)] if last else []),
        ),
        out_shape=[shape((3, width, width), f32)] + [shape(dims, f32) for dims in more],
        input_output_aliases={5: 0} if last else {},
        compiler_params=pltpu.CompilerParams(vmem_limit_bytes=30 * 1024 * 1024),
        cost_estimate=pl.CostEstimate(flops=1, bytes_accessed=1, transcendentals=0),
    )(sc, *slabs, *([base] if last else []))


def per_device(
    tokens, routes, cotangent, norm1_gain, norm1_shift, w_qkv, qv_bias, w_proj, proj_bias,
    norm2_gain, norm2_shift, router_w, expert_in, expert_in_bias, expert_out, expert_out_bias,
):
    n_ea, n_gx, n_gy = (lax.axis_size(a) for a in ("ea", "gx", "gy"))
    n_exp = expert_in.shape[0] * n_ea
    assert expert_in.shape[0] == 1 and n_gx == 2 and n_gy == 4
    t, width = tokens.shape
    images = t // SEQ
    tp = images * SEQ_PAD
    capacity = max(2, 8 * t // (3 * n_exp) + 1)
    cap = -(-capacity // 16) * 16
    half = width // 2
    part = expert_in.shape[2]
    zs = n_ea if (width // 8) % (8 * n_ea) == 0 else 1
    first = (HEADS // 4) * PAIR

    ea, gx, gy = (lax.axis_index(a) for a in ("ea", "gx", "gy"))
    near, far = 1 + gx, 2 - gx
    sc = jnp.stack([
        ea, gx, gy, gy ^ near, gy ^ far, gy ^ 3, gy, gy ^ far, gy ^ near, gy ^ 3,
        gy, gy ^ 1, gy ^ 2, gy ^ 3,
    ]).astype(jnp.int32)
    cross = [(0, 1), (1, 0)]
    perm_a = [(g * 4 + y, g * 4 + (y ^ (1 + g))) for g in range(2) for y in range(4)]
    perm_b = [(g * 4 + y, g * 4 + (y ^ (2 - g))) for g in range(2) for y in range(4)]

    def after(v, done):
        return lax.optimization_barrier((v, done))[0]

    def over_gx(v):
        return lax.ppermute(v, "gx", cross)

    def over_x(v):
        return lax.ppermute(v, "gy", [(y, y ^ 1) for y in range(4)])

    def over_y(v):
        return lax.ppermute(v, "gy", [(y, y ^ 2) for y in range(4)])

    def over_a(v):
        return lax.ppermute(v, ("gx", "gy"), perm_a)

    def over_b(v):
        return lax.ppermute(v, ("gx", "gy"), perm_b)

    def over_ea(v):
        return lax.all_to_all(v, "ea", 0, 0, tiled=True)

    def shift(v, d):
        return lax.ppermute(v, "ea", [(i, (i + d) % n_ea) for i in range(n_ea)])

    order = list(range(1, n_ea))

    def dispatch(blocks):
        got = [blocks[0]] + [None] * (n_ea - 1)
        for d in order:
            got[d] = shift(blocks[d], d)
        return got

    own_w = jnp.stack([expert_in[0], jnp.concatenate([expert_out[0, :half], expert_out[0, half:]], axis=1)])
    x_w, y_w = over_x(own_w), over_y(own_w)

    lanes = -(-n_exp // 8) * 8
    block = shape((cap, width), bf16)
    w3 = w_qkv.transpose(1, 0, 2)
    slot_r, slot_c, g_pad, g_sent = call(
        "route",
        functools.partial(route_kernel, n_exp, cap),
        [shape((lanes, tp), f32), shape((tp, 128), f32), shape((tp, width), bf16), shape((n_exp, cap, width), bf16)],
        (sc, routes.T, cotangent),
        scratch=[pltpu.VMEM((tp, width), f32)],
        smem=1,
    )
    g_rows = lax.all_to_all(g_sent, "ea", 0, 0, tiled=True)
    x_pad, qkv, attn_in = call(
        "project",
        project_kernel,
        [shape((tp, width), f32), shape((3, tp, width), bf16), shape((tp, width), bf16)],
        (tokens, norm1_gain, norm1_shift, w3, qv_bias),
    )
    res, ctx, moe_in, probs, *m_sent = call(
        "attn_fwd",
        functools.partial(fwd_kernel, n_exp, cap),
        [
            shape((tp, width), f32), shape((tp, width), bf16), shape((tp, width), bf16),
            shape((images * width // PAIR, 2, SEQ_PAD, SEQ_PAD), bf16),
        ]
        + [block] * n_exp,
        (qkv, x_pad, w_proj, proj_bias, norm2_gain, norm2_shift, slot_r),
        flops=12_000_000_000,
    )
    other_own = over_gx(own_w)
    x_w, y_w = after((x_w, y_w), (moe_in, other_own))
    mine = [own_w, x_w, y_w, over_x(y_w[0]), over_y(x_w[1])]
    weights = mine + [other_own] + [over_gx(v) for v in mine[1:]]
    own_m, *m_sent = after(tuple(m_sent), g_rows)
    first_m = shift(m_sent[0], 1)
    m_rows = [own_m, first_m] + [shift(v, d) for d, v in enumerate(after(tuple(m_sent[1:]), first_m), 2)]

    router = jnp.pad(router_w.T, ((0, 128 - n_exp), (0, 0)))
    groups = [[d] for d in range(4)] if n_ea == 4 else [list(range(n_ea))]
    y_local, gm_local, gm_back = [None] * n_ea, [None] * n_ea, [None] * n_ea
    kept, in_bias_g, out_bias_g, router_g = [], 0.0, 0.0, 0.0
    for index, group in enumerate(groups):
        if index == 1:
            m_rows[1] = after(m_rows[1], gm_local[0])
        ys, gms, (hid, gp, gr, ib, ob, rg) = moe_rows(
            sc, group, [m_rows[d] for d in group], g_rows, weights,
            expert_in_bias, expert_out_bias, router, cap, n_exp, 12_000_000_000 if index > 1 else 1,
        )
        kept.append((gr, hid, gp))
        in_bias_g, out_bias_g, router_g = in_bias_g + ib, out_bias_g + ob, router_g + rg
        for d, y, gm in zip(group, ys, gms, strict=True):
            y_local[d], gm_local[d] = y, gm
            gm_back[d] = shift(gm, n_ea - d) if d else gm
    rows_all = [m_rows[d] for group in groups for d in group]
    keep, send = weight_grads(sc, rows_all, kept, cap)

    def add(*parts):
        return functools.reduce(lambda a, b: a + b, [p.astype(f32) for p in parts]).astype(bf16)

    def sum_b(keep, got):
        return over_b(add(keep[2:], got[2:]))

    def sum_a(keep, got, got_b):
        return over_a(add(keep[1], got[1], got_b[1]))

    def shifts(parts):
        return [shift(v, d) for d, v in enumerate(parts, 1)]

    gathered = call(
        "gather_rows",
        functools.partial(gather_kernel, cap),
        shape((tp, width), f32),
        (slot_c, *gm_back[:-1]),
        flops=4_000_000_000,
    )
    send, slot_l, gathered, gm_last = after((send, slot_c, gathered, gm_back[-1]), keep)
    got = over_gx(send)
    grad_res, small_two = call(
        "norm_two",
        functools.partial(norm_two_kernel, n_exp, cap),
        [shape((tp, width), f32), shape((8, width), f32)],
        (slot_l, res, norm2_gain, g_pad, gathered, gm_last),
    )
    back = list(range(1, n_ea))
    got, grad_res, *y_local = after((got, grad_res, *y_local), small_two)
    got_x = over_x(add(keep[3, 0], got[3, 0]))
    got_y = over_y(add(keep[3, 1], got[3, 1]))
    y_one = shift(y_local[1], n_ea - 1)
    n = width // (8 * zs)
    slabs = lambda l: [shape((4, zs, n, l), bf16)] * 2
    keep_one, send_one, dctx, dqkv, small_one = call(
        "back_one",
        functools.partial(back_one_kernel, zs),
        slabs(3 * first + width) + [
            shape((tp, width), bf16), shape((3, tp, first), bf16), shape((2, first), f32),
        ],
        (sc, grad_res, ctx, w_proj, probs, qkv, attn_in),
        flops=12_000_000_000,
        scratch=[pltpu.VMEM((width, 3 * first + width), f32)],
        smem=1,
    )
    got_x, got_y, send_one, dctx, y_one, *y_later = after(
        (got_x, got_y, send_one, dctx, y_one, *y_local[2:]), small_one
    )
    y_rows = {d: shift(y, n_ea - d) for d, y in enumerate(y_later, 2) if n_ea != 4 or d != 2}
    early = list(y_rows)
    from_x = over_x(jnp.stack([add(keep[1, 0], got[1, 0]), add(keep[1, 1], got[1, 1], got_y)]))
    from_y = over_y(jnp.stack([add(keep[2, 0], got[2, 0], got_x), add(keep[2, 1], got[2, 1])]))
    got_one = over_gx(send_one)
    rest = width - first
    columns = -(-(7 + 6 * n_exp) // 128) * 128
    keep_two, send_two, grad_tokens = call(
        "back_two",
        functools.partial(back_two_kernel, zs, n_exp),
        slabs(3 * rest + columns) + [shape((t, width), f32)],
        (
            sc, probs, qkv, attn_in, dctx, dqkv, grad_res, w3, tokens, norm1_gain,
            small_two, small_one, router_g, in_bias_g.reshape(4, part), out_bias_g,
        ),
        flops=30_000_000_000,
        scratch=[
            pltpu.VMEM((width, 3 * rest + columns), f32),
            pltpu.VMEM((3, tp, rest), bf16),
            pltpu.VMEM((tp, width), f32),
            pltpu.VMEM((columns, width), f32),
        ],
        smem=1,
    )
    got_one, send_two, y_two, *y_early = after(
        (got_one, send_two, y_later[0], *(y_rows[d] for d in early)), grad_tokens
    )
    y_rows = {1: y_one, **dict(zip(early, y_early, strict=True))}
    if n_ea == 4:
        y_rows[2] = shift(y_two, 2)
    got_two = over_gx(send_two)
    b_one = sum_b(keep_one, got_one)
    b_one, got_two, from_x, from_y = after((b_one, got_two, from_x, from_y), keep_two)
    a_one = sum_a(keep_one, got_one, b_one)
    b_two = sum_b(keep_two, got_two)
    in_w_grad, out_w_grad = call(
        "expert_grads",
        split_kernel,
        [shape((1, half, part), f32), shape((1, part, half), f32)],
        (keep[0], got[0], from_x, from_y),
    )
    a_one, b_two, in_w_grad, out_w_grad, y_late = after(
        (a_one, b_two, in_w_grad, out_w_grad, tuple(y_rows[d] for d in back)), got_two
    )
    rolled = jnp.pad(
        lax.dynamic_slice_in_dim(jnp.concatenate([router_w.T, router_w.T]), ea, n_exp, 0),
        ((0, 128 - n_exp), (0, 0)),
    )
    output = call(
        "combine",
        functools.partial(out_kernel, n_exp, cap),
        shape((t, width), bf16),
        (slot_c, moe_in, rolled, res, y_local[0], *y_late),
        scratch=[pltpu.VMEM((tp, width), f32), pltpu.VMEM((t, width), f32)],
    )
    slabs_one = [add(keep_one[0, d], got_one[0, d], b_one[0, d], a_one[d]) for d in range(zs)]
    a_two = sum_a(keep_two, got_two, b_two)
    if zs > 1:
        z_one = shifts(slabs_one[1:])
        z_one, a_two = after((z_one, a_two), b_two)
        own_one = add(slabs_one[0], *z_one)
        slabs_two = [add(keep_two[0, d], got_two[0, d], b_two[0, d], a_two[d]) for d in range(zs)]
        g_one = shifts([own_one] * (zs - 1))
        z_two = shifts(slabs_two[1:])
        g_one, z_two, output = after((g_one, z_two, output), a_two)
        all_one = jnp.stack([own_one, *g_one])
        own_two = add(slabs_two[0], *z_two)
        g_two = shifts([own_two] * (zs - 1))
    else:
        slabs_two = [add(keep_two[0, 0], got_two[0, 0], b_two[0, 0], a_two[0])]
        all_one, all_two = (lax.psum(v[0], "ea")[None] for v in (slabs_one, slabs_two))
        g_two = [all_two]
    one_a = over_a(all_one)
    one_a, g_two = after((one_a, g_two), all_one)
    one_01 = jnp.stack([all_one, one_a])
    one_23 = over_b(one_01)
    if zs > 1:
        all_two = jnp.stack([own_two, *g_two])
    two_a = over_a(all_two)
    one_23, two_a = after((one_23, two_a), all_two)
    two_01 = jnp.stack([all_two, two_a])
    one = [one_01, one_23, over_gx(one_01), over_gx(one_23)]
    two_23 = over_b(two_01)
    w_qkv_g, w_proj_g = unpack(sc, one, zs, n_exp, width, first)
    two_23 = after(two_23, w_proj_g)
    two = [two_01, two_23, over_gx(two_01), over_gx(two_23)]
    w_qkv_g, *vectors, qv_g, router_g, in_bias_g, out_bias_g = unpack(
        sc, two, zs, n_exp, width, rest, w_qkv_g
    )
    return (
        output,
        grad_tokens,
        vectors[0],
        vectors[1],
        w_qkv_g.transpose(1, 0, 2),
        qv_g,
        w_proj_g,
        vectors[4],
        vectors[2],
        vectors[3],
        router_g.T,
        in_w_grad,
        in_bias_g,
        out_w_grad,
        out_bias_g,
    )


def solution(mesh):
    tok = P(("ea", "gx", "gy"), None)
    in_specs = (
        tok, tok, tok, P(), P(), P(), P(), P(), P(), P(), P(), P(),
        P("ea", "gx", "gy"), P("ea", None), P("ea", "gy", "gx"), P("ea", None),
    )
    out_specs = (
        tok, tok, P(), P(), P(), P(), P(), P(), P(), P(), P(),
        P("ea", "gx", "gy"), P("ea", None), P("ea", "gy", "gx"), P("ea", None),
    )
    return jax.shard_map(per_device, mesh=mesh, in_specs=in_specs, out_specs=out_specs, check_vma=False)
```

```python
import functools
import math

import jax
import jax.numpy as jnp
from jax import lax
from jax.experimental import pallas as pl
from jax.experimental.pallas import tpu as pltpu
from jax.sharding import PartitionSpec as P

HEADS = 12
HD = 64
SEQ = 197
SEQ_PAD = 208
PAIR = 2 * HD
norm_eps = 1e-06

f32 = jnp.float32
bf16 = jnp.bfloat16
LAST = (((1,), (1,)), ((), ()))
FIRST = (((0,), (0,)), ((), ()))
K0 = math.sqrt(2.0 / math.pi)
C3 = 0.044715


def dot(a, b, dims=None):
    if dims is None:
        return jnp.dot(a, b, preferred_element_type=f32)
    return lax.dot_general(a, b, dims, preferred_element_type=f32)


def spec():
    return pl.BlockSpec(memory_space=pltpu.VMEM)


def call(name, kernel, out_shape, args, flops=1, scratch=(), smem=0):
    return pl.pallas_call(
        kernel,
        name=name,
        out_shape=out_shape,
        in_specs=[pl.BlockSpec(memory_space=pltpu.SMEM)] * smem
        + [spec()] * (len(args) - smem),
        out_specs=jax.tree.map(lambda _: spec(), out_shape),
        scratch_shapes=list(scratch),
        compiler_params=pltpu.CompilerParams(vmem_limit_bytes=24 * 1024 * 1024),
        cost_estimate=pl.CostEstimate(
            flops=flops, bytes_accessed=1, transcendentals=0
        ),
    )(*args)


def shape(dims, dtype):
    return jax.ShapeDtypeStruct(tuple(dims), dtype)


def norm_rows(values):
    centered = values - jnp.mean(values, axis=1, keepdims=True)
    inverse = lax.rsqrt(jnp.mean(centered * centered, axis=1, keepdims=True) + norm_eps)
    return centered * inverse, inverse


def norm_back(grad, normed, inverse, gain):
    scaled = grad * gain
    return inverse * (
        scaled
        - jnp.mean(scaled, axis=1, keepdims=True)
        - normed * jnp.mean(scaled * normed, axis=1, keepdims=True)
    )


def spread_images(dst, src, images):
    width = src.shape[1]
    for i in range(images):
        dst[i * SEQ_PAD : i * SEQ_PAD + SEQ, :] = src[i * SEQ : (i + 1) * SEQ, :]
        dst[i * SEQ_PAD + SEQ : (i + 1) * SEQ_PAD, :] = jnp.zeros((SEQ_PAD - SEQ, width), dst.dtype)


def pick_rows(slot_rows, d, cap):
    slots = lax.broadcasted_iota(jnp.int32, (cap, slot_rows.shape[1]), 0).astype(f32)
    return jnp.where(slots == slot_rows[d : d + 1, :], 1.0, 0.0).astype(bf16)


def pick_cols(slot_cols, d, cap):
    slots = lax.broadcasted_iota(jnp.int32, (slot_cols.shape[0], cap), 1).astype(f32)
    return jnp.where(slots == slot_cols[:, d : d + 1], 1.0, 0.0).astype(bf16)


def route_kernel(n_exp, cap, sc, routes, g_ref, slot_r, slot_c, g_pad, sent, wide):
    t, tp = routes.shape[1], slot_r.shape[1]
    lanes = slot_r.shape[0]
    ids = lax.broadcasted_iota(jnp.int32, (lanes, t), 0) + sc[0]
    ids = jnp.where(ids >= n_exp, ids - n_exp, ids)
    real = lax.broadcasted_iota(jnp.int32, (lanes, t), 0) < n_exp
    chosen = ((routes[0:1, :] == ids) | (routes[1:2, :] == ids)) & real
    ti = lax.broadcasted_iota(jnp.int32, (t, tp), 0)
    tj = lax.broadcasted_iota(jnp.int32, (t, tp), 1)
    moved = jnp.where(ti + (ti // SEQ) * (SEQ_PAD - SEQ) == tj, 1.0, 0.0).astype(bf16)
    chosen = dot(jnp.where(chosen, 1.0, 0.0).astype(bf16), moved)
    ti = lax.broadcasted_iota(jnp.int32, (tp, tp), 0)
    tj = lax.broadcasted_iota(jnp.int32, (tp, tp), 1)
    before = jnp.where(ti < tj, 1.0, 0.0).astype(bf16)
    slots = jnp.where(chosen > 0.5, dot(chosen.astype(bf16), before), -1.0)
    slot_r[...] = slots
    slot_c[...] = jnp.full(slot_c.shape, -1.0, f32)
    slot_c[:, :lanes] = slots.T
    spread_images(wide, g_ref[...].astype(f32), tp // SEQ_PAD)
    g_pad[...] = wide[...].astype(bf16)
    rows = slot_r[...]
    for d in range(n_exp):
        sent[lax.rem(sc[0] + d, n_exp)] = dot(pick_rows(rows, d, cap), g_pad[...]).astype(bf16)


def project_kernel(x_ref, gain1, shift1, w3, qvb, wide, qkv, attn_in):
    spread_images(wide, x_ref[...].astype(f32), wide.shape[0] // SEQ_PAD)
    normed, _ = norm_rows(wide[...])
    attn_in[...] = (normed * gain1[...].reshape(1, -1) + shift1[...].reshape(1, -1)).astype(bf16)
    a = attn_in[...]
    qkv[0] = ((dot(a, w3[0]) + qvb[0:1, :]).astype(bf16).astype(f32) * (HD**-0.5)).astype(bf16)
    qkv[1] = dot(a, w3[1]).astype(bf16)
    qkv[2] = (dot(a, w3[2]) + qvb[1:2, :]).astype(bf16)


def head_masks(rows):
    lane = lax.broadcasted_iota(jnp.int32, (rows, PAIR), 1)
    return lane < HD


def attn_probs(q_head, k_pair):
    scores = dot(q_head, k_pair, LAST)
    keys = lax.broadcasted_iota(jnp.int32, scores.shape, 1)
    scores = jnp.where(keys < SEQ, scores, -1e30)
    powered = jnp.exp(scores - jnp.max(scores, axis=1, keepdims=True))
    return powered * (1.0 / jnp.sum(powered, axis=1, keepdims=True))


def fwd_kernel(n_exp, cap, qkv, wide, wp, pb, gain2, shift2, slot_r, res, ctx, moe_in, probs, *sent):
    tp, width = res.shape
    images = tp // SEQ_PAD
    low = head_masks(SEQ_PAD)
    pairs = width // PAIR

    def pair_step(step, carry):
        img, pair = step // pairs, lax.rem(step, pairs)
        rows = pl.ds(pl.multiple_of(img * SEQ_PAD, 16), SEQ_PAD)
        cols = pl.ds(pl.multiple_of(pair * PAIR, PAIR), PAIR)
        q, k, v = qkv[0, rows, cols], qkv[1, rows, cols], qkv[2, rows, cols]
        zero = jnp.zeros_like(q)
        p0 = attn_probs(jnp.where(low, q, zero), k).astype(bf16)
        p1 = attn_probs(jnp.where(low, zero, q), k).astype(bf16)
        probs[step, 0], probs[step, 1] = p0, p1
        ctx[rows, cols] = jnp.where(low, dot(p0, v), dot(p1, v)).astype(bf16)
        return carry

    lax.fori_loop(0, images * pairs, pair_step, 0, unroll=2)
    res[...] = wide[...] + dot(ctx[...], wp[...]) + pb[...].reshape(1, -1)
    normed, _ = norm_rows(res[...])
    moe_in[...] = (normed * gain2[...].reshape(1, -1) + shift2[...].reshape(1, -1)).astype(bf16)
    rows = slot_r[...]
    for d in range(n_exp):
        sent[d][...] = dot(pick_rows(rows, d, cap), moe_in[...]).astype(bf16)


def moe_kernel(nb, cap, n_exp, hc, sc, *refs):
    rows_in, g_in = refs[:nb], refs[nb : 2 * nb]
    mine, other = refs[2 * nb : 2 * nb + 5], refs[2 * nb + 5 : 2 * nb + 10]
    r = 2 * nb + 10
    in_bias, out_bias, router = refs[r : r + 3]
    r += 3
    y_out, gm_out = refs[r : r + nb], refs[r + nb : r + 2 * nb]
    r += 2 * nb
    hid, gp_out, gr, in_b, out_b, router_g = refs[r : r + 6]
    r += 6
    x, gf, wi, wo, acc_y, acc_g, probs_s, sems = refs[r:]
    c = pl.program_id(0)
    width = x.shape[1]
    half = width // 2
    part = wi.shape[2]

    def copies(i):
        gx = sc[1]
        near = pl.ds(pl.multiple_of(gx * half, half), half)
        far = pl.ds(pl.multiple_of((1 - gx) * half, half), half)
        found = []
        for k, (held, cols) in enumerate(((mine, near), (other, far))):
            first, second = (held[i].at[0], held[i].at[1]) if i < 3 else held[3:]
            found.append(pltpu.make_async_copy(first, wi.at[i, cols, :], sems.at[6 * i + 3 * k]))
            for u in range(2):
                found.append(
                    pltpu.make_async_copy(
                        second.at[:, u * half : (u + 1) * half],
                        wo.at[i, u * half : (u + 1) * half, cols],
                        sems.at[6 * i + 3 * k + 1 + u],
                    )
                )
        return found

    @pl.when(c == 0)
    def _():
        for i in range(4):
            for one in copies(i):
                one.start()
        for b in range(nb):
            x[b * cap : (b + 1) * cap, :] = rows_in[b][...]
            gf[b * cap : (b + 1) * cap, :] = g_in[b][0]
        logits = dot(x[...], router[...], LAST)
        lane = lax.broadcasted_iota(jnp.int32, logits.shape, 1)
        logits = jnp.where(lane < n_exp, logits, -1e30)
        powered = jnp.exp(logits - jnp.max(logits, axis=1, keepdims=True))
        probs = powered / jnp.sum(powered, axis=1, keepdims=True)
        probs_s[...] = probs
        gate = jnp.sum(jnp.where(lane == sc[0], probs, 0.0), axis=1, keepdims=True)
        rows_g = (gate * gf[...].astype(f32)).astype(bf16)
        gr[...] = rows_g
        out_b[...] = jnp.sum(rows_g.astype(f32), axis=0, keepdims=True)
        acc_y[...] = jnp.zeros_like(acc_y)
        acc_g[...] = jnp.zeros_like(acc_g)

    for i in range(4):

        @pl.when(c == i)
        def _():
            for one in copies(i):
                one.wait()

    def step(s, carry):
        cols = pl.ds(pl.multiple_of(s * hc, hc), hc)
        w_in = wi[c, :, cols]
        w_out = wo[c, cols, :]
        pre = dot(x[...], w_in) + in_bias[:, cols]
        gh = dot(gr[...], w_out, LAST)
        sq = pre * pre
        h = 0.5 + 0.5 * jnp.tanh(pre * (K0 + (K0 * C3) * sq))
        low_hidden = (pre * h).astype(bf16)
        hid[:, cols] = low_hidden
        acc_y[...] += dot(low_hidden, w_out)
        slope = h + (h - h * h) * (pre * (2.0 * K0 + (6.0 * C3 * K0) * sq))
        gp = gh * slope
        in_b[:, cols] = jnp.sum(gp, axis=0, keepdims=True)
        gp = gp.astype(bf16)
        gp_out[:, cols] = gp
        acc_g[...] += dot(gp, w_in, LAST)
        return carry

    lax.fori_loop(0, part // hc, step, 0)

    @pl.when(c == 3)
    def _():
        y = (acc_y[...] + out_bias[...]).astype(bf16)
        grad_gate = jnp.sum(gf[...].astype(f32) * y.astype(f32), axis=1, keepdims=True)
        probs = probs_s[...]
        lane = lax.broadcasted_iota(jnp.int32, probs.shape, 1)
        own = jnp.where(lane == sc[0], 1.0, 0.0)
        gate = jnp.sum(own * probs, axis=1, keepdims=True)
        grad_logits = ((grad_gate * gate) * (own - probs)).astype(bf16)
        gm = (acc_g[...] + dot(grad_logits, router[...])).astype(bf16)
        router_g[...] = dot(grad_logits, x[...], FIRST)[: router_g.shape[0], :]
        for b in range(nb):
            y_out[b][...] = y[b * cap : (b + 1) * cap, :]
            gm_out[b][...] = gm[b * cap : (b + 1) * cap, :]


def moe_rows(sc, places, rows, grads, weights, in_bias, out_bias, router, cap, n_exp, flops):
    nb = len(rows)
    nr = nb * cap
    width = rows[0].shape[1]
    part = weights[0].shape[2]
    hidden = 4 * part
    lanes = -(-n_exp // 8) * 8
    hc = part
    whole = lambda dims: pl.BlockSpec(dims, lambda c, sc: (0,) * len(dims))
    grid_spec = pltpu.PrefetchScalarGridSpec(
        num_scalar_prefetch=1,
        grid=(4,),
        in_specs=[whole((cap, width))] * nb
        + [
            pl.BlockSpec((1, cap, width), lambda c, sc, d=d: (lax.rem(sc[0] + n_exp - d, n_exp), 0, 0))
            for d in places
        ]
        + [pl.BlockSpec(memory_space=pl.ANY)] * 10
        + [
            pl.BlockSpec((1, part), lambda c, sc: (0, sc[10 + c])),
            whole((1, width)),
            whole((128, width)),
        ],
        out_specs=[whole((cap, width))] * (2 * nb)
        + [
            pl.BlockSpec((nr, part), lambda c, sc: (0, c)),
            pl.BlockSpec((nr, part), lambda c, sc: (0, c)),
            whole((nr, width)),
            pl.BlockSpec((1, part), lambda c, sc: (0, sc[10 + c])),
            whole((1, width)),
            whole((lanes, width)),
        ],
        scratch_shapes=[
            pltpu.VMEM((nr, width), bf16),
            pltpu.VMEM((nr, width), bf16),
            pltpu.VMEM((4, width, part), bf16),
            pltpu.VMEM((4, part, width), bf16),
            pltpu.VMEM((nr, width), f32),
            pltpu.VMEM((nr, width), f32),
            pltpu.VMEM((nr, 128), f32),
            pltpu.SemaphoreType.DMA((24,)),
        ],
    )
    out = pl.pallas_call(
        functools.partial(moe_kernel, nb, cap, n_exp, hc),
        name="expert_rows",
        grid_spec=grid_spec,
        out_shape=[shape((cap, width), bf16)] * (2 * nb)
        + [
            shape((nr, hidden), bf16),
            shape((nr, hidden), bf16),
            shape((nr, width), bf16),
            shape((1, hidden), f32),
            shape((1, width), f32),
            shape((lanes, width), f32),
        ],
        compiler_params=pltpu.CompilerParams(vmem_limit_bytes=(24 if nr < 600 else 60) * 1024 * 1024),
        cost_estimate=pl.CostEstimate(flops=flops, bytes_accessed=1, transcendentals=0),
    )(sc, *rows, *([grads] * nb), *weights, in_bias, out_bias, router)
    return out[:nb], out[nb : 2 * nb], out[2 * nb :]


def weight_kernel(nb, cap, counts, sc, *refs):
    rows, gr, hid, gp = (
        refs[:nb],
        refs[nb : nb + len(counts)],
        refs[nb + len(counts) : nb + 2 * len(counts)],
        refs[nb + 2 * len(counts) : nb + 3 * len(counts)],
    )
    keep, send, xt, gt, cat = refs[nb + 3 * len(counts) :]
    c = pl.program_id(0)
    width = xt.shape[0]
    half = width // 2

    def gather(parts):
        at = 0
        for one in parts:
            cat[at : at + one.shape[0], :] = one[...]
            at += one.shape[0]

    @pl.when(c == 0)
    def _():
        near = pl.ds(pl.multiple_of(sc[1] * half, half), half)
        far = pl.ds(pl.multiple_of((1 - sc[1]) * half, half), half)
        for source, turned in ((rows, xt), (gr, gt)):
            gather(source)
            turned[:half, :] = cat[:, near].T
            turned[half:, :] = cat[:, far].T

    for j, (turned, source) in enumerate(((xt, gp), (gt, hid))):
        gather(source)
        both = dot(turned[...], cat[...]).astype(bf16)
        keep[0, j] = both[:half, :]
        send[0, j] = both[half:, :]


def split_kernel(own, got, from_x, from_y, first, second):
    total = [own[i].astype(f32) + got[i].astype(f32) + from_x[i].astype(f32) + from_y[i].astype(f32) for i in (0, 1)]
    first[0] = total[0]
    second[0] = total[1].T


def weight_grads(sc, rows, groups, cap):
    nb = len(rows)
    width = rows[0].shape[1]
    hidden = groups[0][1].shape[1]
    part = hidden // 4
    counts = [g[0].shape[0] for g in groups]
    total = nb * cap
    whole = lambda dims: pl.BlockSpec(dims, lambda c, sc: (0,) * len(dims))
    block = (1, 2, width // 2, part)
    grid_spec = pltpu.PrefetchScalarGridSpec(
        num_scalar_prefetch=1,
        grid=(4,),
        in_specs=[whole((cap, width))] * nb
        + [whole((n, width)) for n in counts]
        + [pl.BlockSpec((n, part), lambda c, sc: (0, c)) for n in counts] * 2,
        out_specs=[pl.BlockSpec(block, lambda c, sc: (c, 0, 0, 0))] * 2,
        scratch_shapes=[
            pltpu.VMEM((width, total), bf16),
            pltpu.VMEM((width, total), bf16),
            pltpu.VMEM((total, width), bf16),
        ],
    )
    return pl.pallas_call(
        functools.partial(weight_kernel, nb, cap, counts),
        name="expert_weights",
        grid_spec=grid_spec,
        out_shape=[shape((4, 2, width // 2, part), bf16)] * 2,
        compiler_params=pltpu.CompilerParams(vmem_limit_bytes=(24 if total < 1200 else 60) * 1024 * 1024),
        cost_estimate=pl.CostEstimate(
            flops=1, bytes_accessed=1, transcendentals=0
        ),
    )(sc, *rows, *[g[0] for g in groups], *[g[1] for g in groups], *[g[2] for g in groups])


def attn_back(probs, qkv, dctx, dqkv, pair_range, low, images):
    lo, hi = pair_range
    pairs = hi - lo

    def pair_step(step, carry):
        img, pair = step // pairs, lax.rem(step, pairs)
        rows = pl.ds(pl.multiple_of(img * SEQ_PAD, 16), SEQ_PAD)
        cols = pl.ds(pl.multiple_of((pair + lo) * PAIR, PAIR), PAIR)
        local = pl.ds(pl.multiple_of(pair * PAIR, PAIR), PAIR)
        q, k, v, gc = qkv[0, rows, cols], qkv[1, rows, cols], qkv[2, rows, cols], dctx[rows, cols]
        zero = jnp.zeros_like(q)
        outs = []
        for head in range(2):
            kept = probs[img * (qkv.shape[2] // PAIR) + pair + lo, head]
            weight = kept.astype(f32)
            grad_p = dot(jnp.where(low, gc, zero) if head == 0 else jnp.where(low, zero, gc), v, LAST)
            mean = jnp.sum(grad_p * weight, axis=1, keepdims=True)
            ds = (weight * (grad_p - mean)).astype(bf16)
            outs.append((dot(ds, k), dot(ds, q, FIRST), dot(kept, gc, FIRST)))
        join = [jnp.where(low, a, b) for a, b in zip(*outs, strict=True)]
        dqkv[0, rows, local] = (join[0] * (HD**-0.5)).astype(bf16)
        dqkv[1, rows, local] = join[1].astype(bf16)
        dqkv[2, rows, local] = join[2].astype(bf16)
        return carry

    lax.fori_loop(0, images * pairs, pair_step, 0, unroll=2)


def store_slabs(sc, full, keep, send, zs):
    n = keep.shape[2]
    for i in range(4):
        for d in range(zs):
            z = lax.rem(sc[0] + d, zs) if zs > 1 else 0
            base = sc[2 + i] * (n * zs) + z * n
            near = pl.multiple_of(sc[1] * (n * zs * 4) + base, 8)
            keep[i, d] = full[pl.ds(near, n), :].astype(bf16)
            base = sc[6 + i] * (n * zs) + z * n
            far = pl.multiple_of((1 - sc[1]) * (n * zs * 4) + base, 8)
            send[i, d] = full[pl.ds(far, n), :].astype(bf16)


def gather_kernel(cap, slot_c, *refs):
    gm_in, part = refs[:-1], refs[-1]
    cols = slot_c[...]
    total = dot(pick_cols(cols, 0, cap), gm_in[0][...])
    for d in range(1, len(gm_in)):
        total += dot(pick_cols(cols, d, cap), gm_in[d][...])
    part[...] = total


def norm_two_kernel(n_exp, cap, slot_c, res, gain2, g_pad, part, gm_last, grad_res, small):
    grad_moe = part[...] + dot(pick_cols(slot_c[...], n_exp - 1, cap), gm_last[...])
    normed, inverse = norm_rows(res[...])
    grad_res[...] = g_pad[...].astype(f32) + norm_back(grad_moe, normed, inverse, gain2[...].reshape(1, -1))
    small[0:1, :] = jnp.sum(grad_moe * normed, axis=0, keepdims=True)
    small[1:2, :] = jnp.sum(grad_moe, axis=0, keepdims=True)
    small[2:3, :] = jnp.sum(grad_res[...], axis=0, keepdims=True)


def back_one_kernel(zs, sc, grad_res, ctx, wp, probs, qkv, attn_in, keep, send, dctx, dqkv, small, full):
    tp = grad_res.shape[0]
    images = tp // SEQ_PAD
    mix = grad_res[...].astype(bf16)
    part = dqkv.shape[2]
    full[:, 3 * part :] = dot(ctx[...], mix, FIRST)
    dctx[...] = dot(mix, wp[...], LAST).astype(bf16)
    attn_back(probs, qkv, dctx, dqkv, (0, part // PAIR), head_masks(SEQ_PAD), images)
    a = attn_in[...]
    for i in range(3):
        full[:, i * part : (i + 1) * part] = dot(a, dqkv[i], FIRST)
    store_slabs(sc, full, keep, send, zs)
    small[0:1, :] = jnp.sum(dqkv[0].astype(f32), axis=0, keepdims=True)
    small[1:2, :] = jnp.sum(dqkv[2].astype(f32), axis=0, keepdims=True)


def back_two_kernel(
    zs, n_exp, sc, probs, qkv, attn_in, dctx, done, grad_res, w3, x_ref, gain1, small_two, small_one, router_g, in_b, out_b,
    keep, send, grad_tokens, full, dqkv, wide, small,
):
    tp, width = grad_res.shape
    images = tp // SEQ_PAD
    part = done.shape[2]
    rest = width - part
    attn_back(probs, qkv, dctx, dqkv, (part // PAIR, width // PAIR), head_masks(SEQ_PAD), images)
    a = attn_in[...]
    for i in range(3):
        full[:, i * rest : (i + 1) * rest] = dot(a, dqkv[i], FIRST)
    small[...] = jnp.zeros_like(small)
    small[2:5, :] = small_two[0:3, :]
    for i in (0, 2):
        row = 5 + i // 2
        small[row : row + 1, :part] = small_one[i // 2 : 1 + i // 2, :]
        small[row : row + 1, part:] = jnp.sum(dqkv[i].astype(f32), axis=0, keepdims=True)
    small[7 : 7 + n_exp, :] = router_g[:n_exp, :]
    for k in range(4):
        small[pl.ds(7 + n_exp + 4 * sc[0] + k, 1), :] = in_b[k : k + 1, :]
    small[pl.ds(7 + 5 * n_exp + sc[0], 1), :] = out_b[...]
    grad_in = dot(done[0], w3[0, :, :part], LAST) + dot(dqkv[0], w3[0, :, part:], LAST)
    for i in (1, 2):
        grad_in += dot(done[i], w3[i, :, :part], LAST) + dot(dqkv[i], w3[i, :, part:], LAST)
    spread_images(wide, x_ref[...].astype(f32), images)
    normed, inverse = norm_rows(wide[...])
    small[0:1, :] = jnp.sum(grad_in * normed, axis=0, keepdims=True)
    small[1:2, :] = jnp.sum(grad_in, axis=0, keepdims=True)
    full[:, 3 * rest :] = small[...].T
    store_slabs(sc, full, keep, send, zs)
    wide[...] = grad_res[...] + norm_back(grad_in, normed, inverse, gain1[...].reshape(1, -1))
    for i in range(images):
        grad_tokens[i * SEQ : (i + 1) * SEQ, :] = wide[i * SEQ_PAD : i * SEQ_PAD + SEQ, :]


def out_kernel(n_exp, cap, slot_c, moe_in, router, res, *refs):
    y_in, (out, wide, tight) = refs[:n_exp], refs[n_exp:]
    cols = slot_c[...]
    logits = dot(moe_in[...], router[...], LAST)
    lane = lax.broadcasted_iota(jnp.int32, logits.shape, 1)
    logits = jnp.where(lane < n_exp, logits, -1e30)
    powered = jnp.exp(logits - jnp.max(logits, axis=1, keepdims=True))
    probs = powered / jnp.sum(powered, axis=1, keepdims=True)
    total = res[...]
    for d in range(n_exp):
        total += probs[:, d : d + 1] * dot(pick_cols(cols, d, cap), y_in[d][...])
    wide[...] = total
    for i in range(res.shape[0] // SEQ_PAD):
        tight[i * SEQ : (i + 1) * SEQ, :] = wide[i * SEQ_PAD : i * SEQ_PAD + SEQ, :]
    out[...] = tight[...].astype(bf16)


def unpack_kernel(zs, n_exp, lanes, last, sc, *refs):
    parts, refs = refs[:4], refs[4:]
    if last:
        _, w_out, *vectors, qv_g, router_g, in_b, out_b, w_qkv, sems, held, turned_s = refs
    else:
        w_out, held, w_qkv, sems = refs
    n = parts[0].shape[2]
    start = w_out.shape[2] - lanes if last else 0

    def places():
        for q in range(2):
            for i in range(4):
                j = i if q == 0 else (0, 2, 1, 3)[i]
                place = (sc[1] if q == 0 else 1 - sc[1]) * 4 + sc[2 + i]
                for d in range(zs):
                    z = lax.rem(sc[0] - d + zs, zs) if zs > 1 else 0
                    yield parts[2 * q + j // 2].at[j % 2, d], pl.ds(pl.multiple_of((place * zs + z) * n, 8), n)

    copies = []
    for p in range(3):
        for ref, rows in places():
            w_qkv[p, rows, :] = ref[:, p * lanes : (p + 1) * lanes].astype(f32)
        one = pltpu.make_async_copy(w_qkv.at[p], w_out.at[p, :, start : start + lanes], sems.at[p])
        one.start()
        copies.append(one)
    for ref, rows in places():
        held[rows, :] = ref[:, 3 * lanes :].astype(f32)
    if last:
        turned = held[...].T
        for i, vector in enumerate(vectors):
            vector[...] = turned[i : i + 1, :].reshape(-1)
        qv_g[...] = turned[5:7, :]
        router_g[...] = turned[7 : 7 + n_exp, :]
        turned_s[...] = turned
        for k in range(4):
            in_b[:, k * turned.shape[1] : (k + 1) * turned.shape[1]] = turned_s[pl.ds(7 + n_exp + 4 * sc[0] + k, 1), :]
        out_b[...] = turned_s[pl.ds(7 + 5 * n_exp + sc[0], 1), :]
    for one in copies:
        one.wait()


def unpack(sc, slabs, zs, n_exp, width, lanes, base=None):
    last = base is not None
    extra = slabs[0].shape[-1] - 3 * lanes
    whole = lambda dims: pl.BlockSpec(dims, lambda c, sc: (0,) * len(dims))
    more = [(width,)] * 5 + [(2, width), (n_exp, width), (1, 4 * width), (1, width)] if last else [(width, extra)]
    return pl.pallas_call(
        functools.partial(unpack_kernel, zs, n_exp, lanes, last),
        name="unpack",
        grid_spec=pltpu.PrefetchScalarGridSpec(
            num_scalar_prefetch=1,
            grid=(1,),
            in_specs=[whole(v.shape) for v in slabs] + ([pl.BlockSpec(memory_space=pl.ANY)] if last else []),
            out_specs=[
                pl.BlockSpec(memory_space=pl.ANY),
                *[whole(dims) for dims in more],
            ],
            scratch_shapes=[pltpu.VMEM((3, width, lanes), f32), pltpu.SemaphoreType.DMA((3,))]
            + ([pltpu.VMEM((width, extra), f32), pltpu.VMEM((extra, width), f32)] if last else []),
        ),
        out_shape=[shape((3, width, width), f32)] + [shape(dims, f32) for dims in more],
        input_output_aliases={5: 0} if last else {},
        compiler_params=pltpu.CompilerParams(vmem_limit_bytes=24 * 1024 * 1024),
        cost_estimate=pl.CostEstimate(flops=1, bytes_accessed=1, transcendentals=0),
    )(sc, *slabs, *([base] if last else []))


def per_device(
    tokens, routes, cotangent, norm1_gain, norm1_shift, w_qkv, qv_bias, w_proj, proj_bias,
    norm2_gain, norm2_shift, router_w, expert_in, expert_in_bias, expert_out, expert_out_bias,
):
    n_ea, n_gx, n_gy = (lax.axis_size(a) for a in ("ea", "gx", "gy"))
    n_exp = expert_in.shape[0] * n_ea
    assert expert_in.shape[0] == 1 and n_gx == 2 and n_gy == 4
    t, width = tokens.shape
    images = t // SEQ
    tp = images * SEQ_PAD
    capacity = max(2, 8 * t // (3 * n_exp) + 1)
    cap = -(-capacity // 16) * 16
    half = width // 2
    part = expert_in.shape[2]
    zs = n_ea if (width // 8) % (8 * n_ea) == 0 else 1
    first = (HEADS // 4) * PAIR

    ea, gx, gy = (lax.axis_index(a) for a in ("ea", "gx", "gy"))
    near, far = 1 + gx, 2 - gx
    sc = jnp.stack([
        ea, gx, gy, gy ^ near, gy ^ far, gy ^ 3, gy, gy ^ far, gy ^ near, gy ^ 3,
        gy, gy ^ 1, gy ^ 2, gy ^ 3,
    ]).astype(jnp.int32)
    cross = [(0, 1), (1, 0)]
    perm_a = [(g * 4 + y, g * 4 + (y ^ (1 + g))) for g in range(2) for y in range(4)]
    perm_b = [(g * 4 + y, g * 4 + (y ^ (2 - g))) for g in range(2) for y in range(4)]

    def after(v, done):
        return lax.optimization_barrier((v, done))[0]

    def over_gx(v):
        return lax.ppermute(v, "gx", cross)

    def over_x(v):
        return lax.ppermute(v, "gy", [(y, y ^ 1) for y in range(4)])

    def over_y(v):
        return lax.ppermute(v, "gy", [(y, y ^ 2) for y in range(4)])

    def over_a(v):
        return lax.ppermute(v, ("gx", "gy"), perm_a)

    def over_b(v):
        return lax.ppermute(v, ("gx", "gy"), perm_b)

    def over_ea(v):
        return lax.all_to_all(v, "ea", 0, 0, tiled=True)

    def shift(v, d):
        return lax.ppermute(v, "ea", [(i, (i + d) % n_ea) for i in range(n_ea)])

    order = list(range(1, n_ea))

    def dispatch(blocks):
        got = [blocks[0]] + [None] * (n_ea - 1)
        for d in order:
            got[d] = shift(blocks[d], d)
        return got

    own_w = jnp.stack([expert_in[0], jnp.concatenate([expert_out[0, :half], expert_out[0, half:]], axis=1)])
    x_w, y_w = over_x(own_w), over_y(own_w)

    lanes = -(-n_exp // 8) * 8
    block = shape((cap, width), bf16)
    w3 = w_qkv.transpose(1, 0, 2)
    slot_r, slot_c, g_pad, g_sent = call(
        "route",
        functools.partial(route_kernel, n_exp, cap),
        [shape((lanes, tp), f32), shape((tp, 128), f32), shape((tp, width), bf16), shape((n_exp, cap, width), bf16)],
        (sc, routes.T, cotangent),
        scratch=[pltpu.VMEM((tp, width), f32)],
        smem=1,
    )
    g_rows = lax.all_to_all(g_sent, "ea", 0, 0, tiled=True)
    x_pad, qkv, attn_in = call(
        "project",
        project_kernel,
        [shape((tp, width), f32), shape((3, tp, width), bf16), shape((tp, width), bf16)],
        (tokens, norm1_gain, norm1_shift, w3, qv_bias),
        flops=8000000000,
    )
    res, ctx, moe_in, probs, *m_sent = call(
        "attn_fwd",
        functools.partial(fwd_kernel, n_exp, cap),
        [
            shape((tp, width), f32), shape((tp, width), bf16), shape((tp, width), bf16),
            shape((images * width // PAIR, 2, SEQ_PAD, SEQ_PAD), bf16),
        ]
        + [block] * n_exp,
        (qkv, x_pad, w_proj, proj_bias, norm2_gain, norm2_shift, slot_r),
        flops=12_000_000_000,
    )
    other_own = over_gx(own_w)
    x_w, y_w = after((x_w, y_w), (moe_in, other_own))
    mine = [own_w, x_w, y_w, over_x(y_w[0]), over_y(x_w[1])]
    weights = mine + [other_own] + [over_gx(v) for v in mine[1:]]
    own_m, *m_sent = after(tuple(m_sent), g_rows)
    first_m = shift(m_sent[0], 1)
    m_rows = [own_m, first_m] + [shift(v, d) for d, v in enumerate(after(tuple(m_sent[1:]), first_m), 2)]

    router = jnp.pad(router_w.T, ((0, 128 - n_exp), (0, 0)))
    groups = [[d] for d in range(4)] if n_ea == 4 else [list(range(n_ea))]
    y_local, gm_local, gm_back = [None] * n_ea, [None] * n_ea, [None] * n_ea
    kept, in_bias_g, out_bias_g, router_g = [], 0.0, 0.0, 0.0
    for index, group in enumerate(groups):
        if index == 1:
            m_rows[1] = after(m_rows[1], gm_local[0])
        ys, gms, (hid, gp, gr, ib, ob, rg) = moe_rows(
            sc, group, [m_rows[d] for d in group], g_rows, weights,
            expert_in_bias, expert_out_bias, router, cap, n_exp, 12_000_000_000 if index > 1 else 1,
        )
        kept.append((gr, hid, gp))
        in_bias_g, out_bias_g, router_g = in_bias_g + ib, out_bias_g + ob, router_g + rg
        for d, y, gm in zip(group, ys, gms, strict=True):
            y_local[d], gm_local[d] = y, gm
            gm_back[d] = shift(gm, n_ea - d) if d else gm
    rows_all = [m_rows[d] for group in groups for d in group]
    keep, send = weight_grads(sc, rows_all, kept, cap)

    def add(*parts):
        return functools.reduce(lambda a, b: a + b, [p.astype(f32) for p in parts]).astype(bf16)

    def sum_b(keep, got):
        return over_b(add(keep[2:], got[2:]))

    def sum_a(keep, got, got_b):
        return over_a(add(keep[1], got[1], got_b[1]))

    def shifts(parts):
        return [shift(v, d) for d, v in enumerate(parts, 1)]

    gathered = call(
        "gather_rows",
        functools.partial(gather_kernel, cap),
        shape((tp, width), f32),
        (slot_c, *gm_back[:-1]),
        flops=4_000_000_000,
    )
    send, slot_l, gathered, gm_last = after((send, slot_c, gathered, gm_back[-1]), keep)
    got = over_gx(send)
    grad_res, small_two = call(
        "norm_two",
        functools.partial(norm_two_kernel, n_exp, cap),
        [shape((tp, width), f32), shape((8, width), f32)],
        (slot_l, res, norm2_gain, g_pad, gathered, gm_last),
    )
    back = list(range(1, n_ea))
    got, grad_res, *y_local = after((got, grad_res, *y_local), small_two)
    got_x = over_x(add(keep[3, 0], got[3, 0]))
    got_y = over_y(add(keep[3, 1], got[3, 1]))
    y_one = shift(y_local[1], n_ea - 1)
    n = width // (8 * zs)
    slabs = lambda l: [shape((4, zs, n, l), bf16)] * 2
    keep_one, send_one, dctx, dqkv, small_one = call(
        "back_one",
        functools.partial(back_one_kernel, zs),
        slabs(3 * first + width) + [
            shape((tp, width), bf16), shape((3, tp, first), bf16), shape((2, first), f32),
        ],
        (sc, grad_res, ctx, w_proj, probs, qkv, attn_in),
        flops=12_000_000_000,
        scratch=[pltpu.VMEM((width, 3 * first + width), f32)],
        smem=1,
    )
    got_x, got_y, send_one, dctx, y_one, *y_later = after(
        (got_x, got_y, send_one, dctx, y_one, *y_local[2:]), small_one
    )
    y_rows = {d: shift(y, n_ea - d) for d, y in enumerate(y_later, 2) if n_ea != 4 or d != 2}
    early = list(y_rows)
    from_x = over_x(jnp.stack([add(keep[1, 0], got[1, 0]), add(keep[1, 1], got[1, 1], got_y)]))
    from_y = over_y(jnp.stack([add(keep[2, 0], got[2, 0], got_x), add(keep[2, 1], got[2, 1])]))
    got_one = over_gx(send_one)
    rest = width - first
    columns = -(-(7 + 6 * n_exp) // 128) * 128
    keep_two, send_two, grad_tokens = call(
        "back_two",
        functools.partial(back_two_kernel, zs, n_exp),
        slabs(3 * rest + columns) + [shape((t, width), f32)],
        (
            sc, probs, qkv, attn_in, dctx, dqkv, grad_res, w3, tokens, norm1_gain,
            small_two, small_one, router_g, in_bias_g.reshape(4, part), out_bias_g,
        ),
        flops=30_000_000_000,
        scratch=[
            pltpu.VMEM((width, 3 * rest + columns), f32),
            pltpu.VMEM((3, tp, rest), bf16),
            pltpu.VMEM((tp, width), f32),
            pltpu.VMEM((columns, width), f32),
        ],
        smem=1,
    )
    got_one, send_two, y_two, *y_early = after(
        (got_one, send_two, y_later[0], *(y_rows[d] for d in early)), grad_tokens
    )
    y_rows = {1: y_one, **dict(zip(early, y_early, strict=True))}
    if n_ea == 4:
        y_rows[2] = shift(y_two, 2)
    got_two = over_gx(send_two)
    b_one = sum_b(keep_one, got_one)
    b_one, got_two, from_x, from_y = after((b_one, got_two, from_x, from_y), keep_two)
    a_one = sum_a(keep_one, got_one, b_one)
    b_two = sum_b(keep_two, got_two)
    in_w_grad, out_w_grad = call(
        "expert_grads",
        split_kernel,
        [shape((1, half, part), f32), shape((1, part, half), f32)],
        (keep[0], got[0], from_x, from_y),
    )
    a_one, b_two, in_w_grad, out_w_grad, y_late = after(
        (a_one, b_two, in_w_grad, out_w_grad, tuple(y_rows[d] for d in back)), got_two
    )
    rolled = jnp.pad(
        lax.dynamic_slice_in_dim(jnp.concatenate([router_w.T, router_w.T]), ea, n_exp, 0),
        ((0, 128 - n_exp), (0, 0)),
    )
    output = call(
        "combine",
        functools.partial(out_kernel, n_exp, cap),
        shape((t, width), bf16),
        (slot_c, moe_in, rolled, res, y_local[0], *y_late),
        scratch=[pltpu.VMEM((tp, width), f32), pltpu.VMEM((t, width), f32)],
    )
    slabs_one = [add(keep_one[0, d], got_one[0, d], b_one[0, d], a_one[d]) for d in range(zs)]
    a_two = sum_a(keep_two, got_two, b_two)
    if zs > 1:
        z_one = shifts(slabs_one[1:])
        z_one, a_two = after((z_one, a_two), b_two)
        own_one = add(slabs_one[0], *z_one)
        slabs_two = [add(keep_two[0, d], got_two[0, d], b_two[0, d], a_two[d]) for d in range(zs)]
        g_one = shifts([own_one] * (zs - 1))
        z_two = shifts(slabs_two[1:])
        g_one, z_two, output = after((g_one, z_two, output), a_two)
        all_one = jnp.stack([own_one, *g_one])
        own_two = add(slabs_two[0], *z_two)
        g_two = shifts([own_two] * (zs - 1))
    else:
        slabs_two = [add(keep_two[0, 0], got_two[0, 0], b_two[0, 0], a_two[0])]
        all_one, all_two = (lax.psum(v[0], "ea")[None] for v in (slabs_one, slabs_two))
        g_two = [all_two]
    one_a = over_a(all_one)
    one_a, g_two = after((one_a, g_two), all_one)
    one_01 = jnp.stack([all_one, one_a])
    one_23 = over_b(one_01)
    if zs > 1:
        all_two = jnp.stack([own_two, *g_two])
    two_a = over_a(all_two)
    one_23, two_a = after((one_23, two_a), all_two)
    two_01 = jnp.stack([all_two, two_a])
    one = [one_01, one_23, over_gx(one_01), over_gx(one_23)]
    two_23 = over_b(two_01)
    w_qkv_g, w_proj_g = unpack(sc, one, zs, n_exp, width, first)
    two_23 = after(two_23, w_proj_g)
    two = [two_01, two_23, over_gx(two_01), over_gx(two_23)]
    w_qkv_g, *vectors, qv_g, router_g, in_bias_g, out_bias_g = unpack(
        sc, two, zs, n_exp, width, rest, w_qkv_g
    )
    return (
        output,
        grad_tokens,
        vectors[0],
        vectors[1],
        w_qkv_g.transpose(1, 0, 2),
        qv_g,
        w_proj_g,
        vectors[4],
        vectors[2],
        vectors[3],
        router_g.T,
        in_w_grad,
        in_bias_g,
        out_w_grad,
        out_bias_g,
    )


def solution(mesh):
    tok = P(("ea", "gx", "gy"), None)
    in_specs = (
        tok, tok, tok, P(), P(), P(), P(), P(), P(), P(), P(), P(),
        P("ea", "gx", "gy"), P("ea", None), P("ea", "gy", "gx"), P("ea", None),
    )
    out_specs = (
        tok, tok, P(), P(), P(), P(), P(), P(), P(), P(), P(),
        P("ea", "gx", "gy"), P("ea", None), P("ea", "gy", "gx"), P("ea", None),
    )
    return jax.shard_map(per_device, mesh=mesh, in_specs=in_specs, out_specs=out_specs, check_vma=False)
```
